32 devices in a mesh: scene: 2 (over core), tile: 16 (over z, y, x).
Axes of the slice: x: 2, y: 2, z: 4, core: 2. Of those that a mesh axis runs over, the one named last changes fastest.
Arguments:
- gaussians: float32 [2, 32, 59, 128], P('scene', 'tile'), as said below
- consensus: float32 [2, 32, 59, 128], P('scene', 'tile'), as said below
- duals: float32 [2, 32, 59, 128], P('scene', 'tile'), may hold values from -0.6 to 0.6
- step_sizes: float32 [59], replicated, may hold values from 0.02 to 0.2
- cameras: float32 [16, 16], replicated, as said below
- camera_ids: int32 [2, 16], P('scene', 'tile'), may hold values from 0 to 15
- block_lists: int32 [2, 16, 16], P('scene', 'tile'), may hold values from 0 to 31, as said below
- depth_order: int32 [2, 16, 16], P('scene', 'tile'), may hold values from 0 to 15, as said below
- block_counts: int32 [2, 16], P('scene', 'tile'), may hold values from 1 to 16, as said below
- targets: float32 [2, 16, 3, 1024], P('scene', 'tile'), may hold values from 0 to 1
- intersection: int32 [2, 16, 2, 64], P('scene', 'tile'), may hold values from 0 to 255, as said below
Outputs:
- updated: float32 [2, 32, 59, 128], P('scene', 'tile')
- new_duals: float32 [2, 32, 59, 128], P('scene', 'tile')
The draws below stay inside these ranges and needn't reach their ends.
Inputs may be any that keep to these rules, and one draw needn't show every extreme that they name: `gaussians`: rows 0 and 1 of each Gaussian lie in -1.5 to 1.5, row 2 in 3 to 6, rows 3 to 5 in log 0.1 to log 0.5, row 6 in 0.8 to 1.2, row 10 in -2 to 6. `consensus`: drawn like gaussians. `cameras`: rotations within 0.15 of the identity about each axis, translations within 0.3, focal lengths 80 to 120, principal point x 40 to 88, y 16 to 48. `block_lists`: each strip lists 16 block numbers whose quotients by 2 all differ. `depth_order`: each strip's entries are a permutation of its slots. `block_counts`: some strip of every group has all 16 slots live. `intersection`: the 128 entries of a device are different local Gaussian numbers and include 0 and 255.
All inputs are finite; a program needn't handle non-finite values.
Results may differ from the reference program's by a relative error of at most 0.0003.
Values sent between devices are 32-bit elements; how exact they have to be, the bound alone decides.
No kernel may reach another device: no remote copies, remote signals or barrier semaphores. Data moves between devices by JAX's collectives and lax.ppermute only.
A program may use at most 64 MiB of HBM per device.

```python
import math
import jax
import jax.numpy as jnp
from jax import lax

PARAMS = 59
BLOCK = 128
BLK_DEV = 2
LISTED = 16
HALF = 64
NCAM = 16
GROUPS = 2
STRIPS = 16
NB = 32
PIX = 1024


def gauss_field(seed_key):
    keys = jax.random.split(seed_key, 7)
    leading = (GROUPS, NB)

    def uniform_rows(subkey, height, lower, upper):
        return jax.random.uniform(subkey, leading + (height, BLOCK), jnp.float32, lower, upper)
    planar = uniform_rows(keys[0], 2, -1.5, 1.5)
    depth_row = uniform_rows(keys[1], 1, 3.0, 6.0)
    log_scale = uniform_rows(keys[2], 3, math.log(0.1), math.log(0.5))
    quat_real = uniform_rows(keys[3], 1, 0.8, 1.2)
    quat_imag = 0.3 * jax.random.normal(keys[4], leading + (3, BLOCK), jnp.float32)
    logit_row = uniform_rows(keys[5], 1, -2.0, 6.0)
    harmonics = 0.3 * jax.random.normal(keys[6], leading + (48, BLOCK), jnp.float32)
    return jnp.concatenate([planar, depth_row, log_scale, quat_real, quat_imag, logit_row, harmonics], 2)


def draw_gaussians(key, part):
    return gauss_field(jax.random.fold_in(key, 11))


def draw_consensus(key, part):
    return gauss_field(jax.random.fold_in(key, 23))


def draw_cameras(key, part):
    keys = jax.random.split(jax.random.fold_in(key, 31), 5)
    angles = jax.random.uniform(keys[0], (NCAM, 3), jnp.float32, -0.15, 0.15)
    cos_v = jnp.cos(angles)
    sin_v = jnp.sin(angles)
    zeros_v = jnp.zeros((NCAM,), jnp.float32)
    ones_v = jnp.ones((NCAM,), jnp.float32)
    turn_x = jnp.stack([jnp.stack([ones_v, zeros_v, zeros_v], -1), jnp.stack([zeros_v, cos_v[:, 0], -sin_v[:, 0]], -1), jnp.stack([zeros_v, sin_v[:, 0], cos_v[:, 0]], -1)], 1)
    turn_y = jnp.stack([jnp.stack([cos_v[:, 1], zeros_v, sin_v[:, 1]], -1), jnp.stack([zeros_v, ones_v, zeros_v], -1), jnp.stack([-sin_v[:, 1], zeros_v, cos_v[:, 1]], -1)], 1)
    turn_z = jnp.stack([jnp.stack([cos_v[:, 2], -sin_v[:, 2], zeros_v], -1), jnp.stack([sin_v[:, 2], cos_v[:, 2], zeros_v], -1), jnp.stack([zeros_v, zeros_v, ones_v], -1)], 1)
    rotation = jnp.einsum('nij,njk,nkl->nil', turn_z, turn_y, turn_x)
    offsets = jax.random.uniform(keys[1], (NCAM, 3), jnp.float32, -0.3, 0.3)
    focal = jax.random.uniform(keys[2], (NCAM, 2), jnp.float32, 80.0, 120.0)
    centre_x = jax.random.uniform(keys[3], (NCAM, 1), jnp.float32, 40.0, 88.0)
    centre_y = jax.random.uniform(keys[4], (NCAM, 1), jnp.float32, 16.0, 48.0)
    return jnp.concatenate([rotation.reshape(NCAM, 9), offsets, focal, centre_x, centre_y], 1)


def distinct_order(seed_key, leading, length):
    scores = jax.random.randint(seed_key, leading + (length,), 0, 1 << 20) * length + jnp.arange(length, dtype=jnp.int32)
    return jnp.argsort(scores, axis=-1).astype(jnp.int32)


def draw_block_lists(key, part):
    keys = jax.random.split(jax.random.fold_in(key, 41), 2)
    owners = distinct_order(keys[0], (GROUPS, STRIPS), STRIPS)[..., :LISTED]
    within = jax.random.randint(keys[1], (GROUPS, STRIPS, LISTED), 0, BLK_DEV)
    return (owners * BLK_DEV + within).astype(jnp.int32)


def draw_depth_order(key, part):
    return distinct_order(jax.random.fold_in(key, 43), (GROUPS, STRIPS), LISTED)


def draw_block_counts(key, part):
    keys = jax.random.split(jax.random.fold_in(key, 47), 3)
    busy = jax.random.randint(keys[0], (GROUPS, STRIPS), 0, 3) == 0
    light = jax.random.randint(keys[1], (GROUPS, STRIPS), 1, max(LISTED // 2, 1) + 1)
    counts_drawn = jnp.where(busy, LISTED, light)
    chosen = jax.random.randint(keys[2], (GROUPS, 1), 0, STRIPS)
    return jnp.where(jnp.arange(STRIPS, dtype=jnp.int32)[None, :] == chosen, LISTED, counts_drawn).astype(jnp.int32)


def draw_intersection(key, part):
    keys = jax.random.split(jax.random.fold_in(key, 53), 2)
    local_size = BLK_DEV * BLOCK
    inner = distinct_order(keys[0], (GROUPS, STRIPS), local_size - 2)[..., :2 * HALF - 2] + 1
    ends = jnp.broadcast_to(jnp.array([0, local_size - 1], jnp.int32), (GROUPS, STRIPS, 2))
    picked = jnp.concatenate([ends, inner], -1)
    mixing = distinct_order(keys[1], (GROUPS, STRIPS), 2 * HALF)
    return jnp.take_along_axis(picked, mixing, axis=-1).reshape(GROUPS, STRIPS, 2, HALF).astype(jnp.int32)


def place_ends(result, rng, smallest, largest):
    place = [jax.random.randint(jax.random.fold_in(rng, axis), (), 0, length) for axis, length in enumerate(result.shape)]
    longest = result.shape.index(max(result.shape))
    next_to = place[:longest] + [(place[longest] + 1) % result.shape[longest]] + place[longest + 1:]
    return result.at[tuple(place)].set(smallest).at[tuple(next_to)].set(largest)


def shard_levels(stream_key, shape, pieces, least, high):
    def one(dim, shards_of):
        draws = jax.random.uniform(jax.random.fold_in(jax.random.fold_in(stream_key, 6), dim), (shards_of,), jnp.float32, least / len(pieces), high / len(pieces))
        return jnp.repeat(jnp.exp(draws), shape[dim] // shards_of).reshape((-1,) + (1,) * (len(shape) - dim - 1))

    gain = one(*pieces[0])
    for cut in pieces[1:]:
        gain = gain * one(*cut)
    return gain


def gaussian(stream_key, extent, deviation, bound, cuts=(), held_as=jnp.bfloat16):
    factor_of = shard_levels(stream_key, extent, cuts, -0.22, 0.18) if cuts else 1.0
    entries = jax.random.normal(stream_key, extent, jnp.float32) * deviation * factor_of
    return jnp.minimum(jnp.maximum(entries, -bound), bound).astype(held_as)


def setup_inputs(seed: int = 0) -> dict:
    seeds = jax.random.split(jax.random.key(seed), 12)
    gaussians = draw_gaussians(jax.random.fold_in(seeds[11], 71), 0)
    consensus = draw_consensus(jax.random.fold_in(seeds[11], 71), 0)
    duals = gaussian(seeds[2], (GROUPS, NB, PARAMS, BLOCK), 0.1, 0.6, ((0, 2), (1, 16)), jnp.float32)
    step_sizes = jnp.clip(jnp.exp(jax.random.uniform(seeds[3], (PARAMS,), jnp.float32, math.log(0.02), math.log(0.2))), 0.02, 0.2)
    cameras = draw_cameras(jax.random.fold_in(seeds[11], 71), 0)
    camera_ids = place_ends(jax.random.randint(seeds[5], (GROUPS, STRIPS), 0, NCAM), jax.random.fold_in(seeds[5], 1), 0, NCAM - 1).astype(jnp.int32)
    block_lists = draw_block_lists(jax.random.fold_in(seeds[11], 71), 0)
    depth_order = draw_depth_order(jax.random.fold_in(seeds[11], 71), 0)
    block_counts = draw_block_counts(jax.random.fold_in(seeds[11], 71), 0)
    targets = jnp.clip(1.0 * jax.random.uniform(seeds[9], (GROUPS, STRIPS, 3, PIX), jnp.float32) ** shard_levels(seeds[9], (GROUPS, STRIPS, 3, PIX), ((0, 2), (1, 16)), -0.2, 0.2), 0.0, 1.0)
    intersection = draw_intersection(jax.random.fold_in(seeds[11], 71), 0)
    return dict(gaussians=gaussians, consensus=consensus, duals=duals, step_sizes=step_sizes, cameras=cameras, camera_ids=camera_ids, block_lists=block_lists, depth_order=depth_order, block_counts=block_counts, targets=targets, intersection=intersection)


highest = lax.Precision.HIGHEST
penalty_weight = 0.5
blur_floor = 0.3
alpha_ceiling = 0.99
sh_zero = 0.28209479177387814
sh_one = 0.4886025119029199
sh_two = (1.0925484305920792, -1.0925484305920792, 0.31539156525252005, -1.0925484305920792, 0.5462742152960396)
sh_three = (-0.5900435899266435, 2.890611442640554, -0.4570457994644658, 0.3731763325901154, -0.4570457994644658, 1.445305721320277, -0.5900435899266435)

def harmonic_basis(toward):
    comp_x, comp_y, comp_z = (toward[0], toward[1], toward[2])
    sq_x, sq_y, sq_z = (comp_x * comp_x, comp_y * comp_y, comp_z * comp_z)
    return jnp.stack([sh_zero + 0.0 * comp_x, -sh_one * comp_y, sh_one * comp_z, -sh_one * comp_x, sh_two[0] * comp_x * comp_y, sh_two[1] * comp_y * comp_z, sh_two[2] * (2.0 * sq_z - sq_x - sq_y), sh_two[3] * comp_x * comp_z, sh_two[4] * (sq_x - sq_y), sh_three[0] * comp_y * (3.0 * sq_x - sq_y), sh_three[1] * comp_x * comp_y * comp_z, sh_three[2] * comp_y * (4.0 * sq_z - sq_x - sq_y), sh_three[3] * comp_z * (2.0 * sq_z - 3.0 * sq_x - 3.0 * sq_y), sh_three[4] * comp_x * (4.0 * sq_z - sq_x - sq_y), sh_three[5] * comp_z * (sq_x - sq_y), sh_three[6] * comp_x * (sq_x - 3.0 * sq_y)])

def gauss_features(gauss_block, camera):
    rotation = camera[0:9].reshape(3, 3)
    shift_vec = camera[9:12]
    focal_x, focal_y, center_x, center_y = (camera[12], camera[13], camera[14], camera[15])
    centre = gauss_block[0:3]
    viewed = jnp.dot(rotation, centre, precision=highest) + shift_vec[:, None]
    inverse = 1.0 / viewed[2]
    screen_x = focal_x * viewed[0] * inverse + center_x
    screen_y = focal_y * viewed[1] * inverse + center_y
    quater = gauss_block[6:10]
    quater = quater / jnp.sqrt(lax.optimization_barrier(jnp.sum(quater * quater, 0)))
    quat_w, quat_x, quat_y, quat_z = (quater[0], quater[1], quater[2], quater[3])
    rot_rows = jnp.stack([jnp.stack([1.0 - 2.0 * (quat_y * quat_y + quat_z * quat_z), 2.0 * (quat_x * quat_y - quat_w * quat_z), 2.0 * (quat_x * quat_z + quat_w * quat_y)]), jnp.stack([2.0 * (quat_x * quat_y + quat_w * quat_z), 1.0 - 2.0 * (quat_x * quat_x + quat_z * quat_z), 2.0 * (quat_y * quat_z - quat_w * quat_x)]), jnp.stack([2.0 * (quat_x * quat_z - quat_w * quat_y), 2.0 * (quat_y * quat_z + quat_w * quat_x), 1.0 - 2.0 * (quat_x * quat_x + quat_y * quat_y)])])
    scales = jnp.exp(gauss_block[3:6])
    spread = rot_rows * scales[None, :, :]
    world_axes = jnp.einsum('ij,jkg->ikg', rotation, spread, precision=highest)
    row_one = focal_x * inverse * world_axes[0] - focal_x * viewed[0] * inverse * inverse * world_axes[2]
    row_two = focal_y * inverse * world_axes[1] - focal_y * viewed[1] * inverse * inverse * world_axes[2]
    cov_xx = lax.optimization_barrier(jnp.sum(row_one * row_one, 0)) + blur_floor
    cov_xy = lax.optimization_barrier(jnp.sum(row_one * row_two, 0))
    cov_yy = lax.optimization_barrier(jnp.sum(row_two * row_two, 0)) + blur_floor
    determ = cov_xx * cov_yy - cov_xy * cov_xy
    conic_a = cov_yy / determ
    conic_b = -cov_xy / determ
    conic_c = cov_xx / determ
    opacity = jax.nn.sigmoid(gauss_block[10])
    eye_pos = -jnp.dot(rotation.T, shift_vec, precision=highest)
    toward = centre - eye_pos[:, None]
    toward = toward / jnp.sqrt(lax.optimization_barrier(jnp.sum(toward * toward, 0)))
    coeffs = gauss_block[11:59].reshape(16, 3, -1)
    colour = lax.optimization_barrier(jnp.sum(harmonic_basis(toward)[:, None, :] * coeffs, 0)) + 0.5
    return (screen_x, screen_y, conic_a, conic_b, conic_c, opacity, colour)

def blend_block(state_pair, gauss_block, camera, pixel_x, pixel_y, strict):
    transmit, colour_sum = state_pair
    screen_x, screen_y, conic_a, conic_b, conic_c, opacity, colour = gauss_features(gauss_block, camera)
    delta_x = pixel_x[:, None] - screen_x[None, :]
    delta_y = pixel_y[:, None] - screen_y[None, :]
    exponent = -0.5 * (conic_a * delta_x * delta_x + conic_c * delta_y * delta_y) - conic_b * delta_x * delta_y
    alpha_px = jnp.minimum(alpha_ceiling, opacity * jnp.exp(exponent))
    logs_kept = jnp.log1p(-alpha_px)
    before = jnp.dot(logs_kept, strict, precision=highest)
    weight = alpha_px * transmit[:, None] * jnp.exp(before)
    colour_sum = colour_sum + jnp.einsum('cg,pg->cp', colour, weight, precision=highest)
    transmit = transmit * jnp.exp(lax.optimization_barrier(jnp.sum(logs_kept, 1)))
    return (transmit, colour_sum)

def strip_loss(listed, camera, strip_index, depth_steps, active_count, target):
    pixels = target.shape[1]
    strip_rows = pixels // 128
    pixel_index = jnp.arange(pixels, dtype=jnp.int32)
    pixel_x = (pixel_index % 128).astype(jnp.float32)
    pixel_y = (pixel_index // 128 + strip_rows * (strip_index % 4)).astype(jnp.float32)
    lane_index = jnp.arange(listed.shape[2], dtype=jnp.int32)
    strict = (lane_index[:, None] < lane_index[None, :]).astype(jnp.float32)
    blender = jax.checkpoint(lambda current, gauss_block: blend_block(current, gauss_block, camera, pixel_x, pixel_y, strict))

    def advance(current, slot_index):
        gauss_block = listed[slot_index]
        current = lax.cond(slot_index < active_count, lambda status: blender(status, gauss_block), lambda status: status, current)
        return (current, None)
    initial = (jnp.ones((pixels,), jnp.float32), jnp.zeros((3, pixels), jnp.float32))
    final_pair, unused = lax.scan(advance, initial, depth_steps)
    residual = final_pair[1] - target
    return 0.5 * jnp.sum(residual * residual)

def strip_gradient(listed, camera, strip_index, depth_steps, active_count, target):
    loss_value, pullback = jax.vjp(lambda blocks: strip_loss(blocks, camera, strip_index, depth_steps, active_count, target), listed)
    return pullback(jnp.ones_like(loss_value))[0]

def place_agreed(field, index_up, index_down, values_up, values_down):
    return field.at[:, index_up].set(values_up).at[:, index_down].set(values_down)

def reference(gaussians, consensus, duals, step_sizes, cameras, camera_ids, block_lists, depth_order, block_counts, targets, intersection):
    num_blocks = gaussians.shape[1]
    block_range = jnp.arange(num_blocks, dtype=jnp.int32)

    def group_sum(group_index):

        def strip_step(running, strip_index):
            listed_ids = block_lists[group_index, strip_index]
            listed = gaussians[group_index][listed_ids]
            camera = cameras[camera_ids[group_index, strip_index]]
            gradients = strip_gradient(listed, camera, strip_index, depth_order[group_index, strip_index], block_counts[group_index, strip_index], targets[group_index, strip_index])
            onehot = (listed_ids[:, None] == block_range[None, :]).astype(jnp.float32)
            return (running + jnp.einsum('kb,kgc->bgc', onehot, gradients, precision=highest), None)
        running, unused = lax.scan(strip_step, jnp.zeros(gaussians.shape[1:], jnp.float32), jnp.arange(STRIPS, dtype=jnp.int32))
        return running
    gradient = lax.map(group_sum, jnp.arange(GROUPS, dtype=jnp.int32))
    updated = gaussians - step_sizes[None, None, :, None] * (gradient + penalty_weight * (gaussians - consensus + duals))
    shifted = updated + duals
    local_view = shifted.reshape(GROUPS, STRIPS, BLK_DEV, PARAMS, BLOCK).transpose(0, 1, 3, 2, 4).reshape(GROUPS, STRIPS, PARAMS, BLK_DEV * BLOCK)
    index_up = intersection[:, :, 0]
    index_down = intersection[:, :, 1]
    up_vals = jnp.take_along_axis(local_view, index_up[:, :, None, :], axis=3)
    down_vals = jnp.take_along_axis(local_view, index_down[:, :, None, :], axis=3)
    from_above = jnp.concatenate([down_vals[1:], jnp.zeros_like(down_vals[:1])], 0)
    from_below = jnp.concatenate([jnp.zeros_like(up_vals[:1]), up_vals[:-1]], 0)
    group_ids = jnp.arange(GROUPS, dtype=jnp.int32)[:, None, None, None]
    agreed_up = jnp.where(group_ids < GROUPS - 1, 0.5 * (up_vals + from_above), up_vals)
    agreed_down = jnp.where(group_ids > 0, 0.5 * (down_vals + from_below), down_vals)
    agreed = jax.vmap(jax.vmap(place_agreed))(local_view, index_up, index_down, agreed_up, agreed_down)
    dual_local = local_view - agreed
    new_duals = dual_local.reshape(GROUPS, STRIPS, PARAMS, BLK_DEV, BLOCK).transpose(0, 1, 3, 2, 4).reshape(GROUPS, STRIPS * BLK_DEV, PARAMS, BLOCK)
    return (updated, new_duals)
```

```python
import functools

import jax
import jax.numpy as jnp
import numpy as np
from jax import lax
from jax.experimental import pallas as pl
from jax.experimental.pallas import tpu as pltpu
from jax.sharding import PartitionSpec as P

penalty_weight = 0.5
blur_floor = 0.3
alpha_ceiling = 0.99
log2e = 1.4426950408889634
sh_zero = 0.28209479177387814
sh_one = 0.4886025119029199
sh_two = (
    1.0925484305920792,
    -1.0925484305920792,
    0.31539156525252005,
    -1.0925484305920792,
    0.5462742152960396,
)
sh_three = (
    -0.5900435899266435,
    2.890611442640554,
    -0.4570457994644658,
    0.3731763325901154,
    -0.4570457994644658,
    1.445305721320277,
    -0.5900435899266435,
)

LANES = 128
SUB = 8
ROWS = 64
KDIM = 32
SEGS = 8
MOMENTS = 6
MSG = 16
highest = lax.Precision.HIGHEST


def harmonic_basis(x, y, z):
    xx, yy, zz = x * x, y * y, z * z
    return [
        sh_zero + 0.0 * x,
        -sh_one * y,
        sh_one * z,
        -sh_one * x,
        sh_two[0] * x * y,
        sh_two[1] * y * z,
        sh_two[2] * (2.0 * zz - xx - yy),
        sh_two[3] * x * z,
        sh_two[4] * (xx - yy),
        sh_three[0] * y * (3.0 * xx - yy),
        sh_three[1] * x * y * z,
        sh_three[2] * y * (4.0 * zz - xx - yy),
        sh_three[3] * z * (2.0 * zz - 3.0 * xx - 3.0 * yy),
        sh_three[4] * x * (4.0 * zz - xx - yy),
        sh_three[5] * z * (xx - yy),
        sh_three[6] * x * (xx - 3.0 * yy),
    ]


def geometry(row, cam):
    mean = [row(0), row(1), row(2)]
    rot = [[cam[3 * i + j] for j in range(3)] for i in range(3)]
    shift = [cam[9 + i] for i in range(3)]
    focal_x, focal_y = cam[12], cam[13]
    view = [
        rot[i][0] * mean[0] + rot[i][1] * mean[1] + rot[i][2] * mean[2] + shift[i] for i in range(3)
    ]
    inverse = 1.0 / view[2]
    u = view[0] * inverse
    v = view[1] * inverse
    quat = [row(6 + i) for i in range(4)]
    norm = lax.rsqrt(sum(q * q for q in quat))
    w, x, y, z = [q * norm for q in quat]
    turn = [
        [1.0 - 2.0 * (y * y + z * z), 2.0 * (x * y - w * z), 2.0 * (x * z + w * y)],
        [2.0 * (x * y + w * z), 1.0 - 2.0 * (x * x + z * z), 2.0 * (y * z - w * x)],
        [2.0 * (x * z - w * y), 2.0 * (y * z + w * x), 1.0 - 2.0 * (x * x + y * y)],
    ]
    scales = [jnp.exp(row(3 + k)) for k in range(3)]
    spread = [[turn[j][k] * scales[k] for k in range(3)] for j in range(3)]
    axes = [
        [sum(rot[i][j] * spread[j][k] for j in range(3)) for k in range(3)] for i in range(3)
    ]
    scale_x = focal_x * inverse
    scale_y = focal_y * inverse
    lean_x = [axes[0][k] - u * axes[2][k] for k in range(3)]
    lean_y = [axes[1][k] - v * axes[2][k] for k in range(3)]
    row_one = [scale_x * lean_x[k] for k in range(3)]
    row_two = [scale_y * lean_y[k] for k in range(3)]
    cov_xx = sum(a * a for a in row_one) + blur_floor
    cov_xy = sum(a * b for a, b in zip(row_one, row_two))
    cov_yy = sum(b * b for b in row_two) + blur_floor
    scale = 1.0 / (cov_xx * cov_yy - cov_xy * cov_xy)
    conic = (cov_yy * scale, -cov_xy * scale, cov_xx * scale)
    eye = [-(rot[0][i] * shift[0] + rot[1][i] * shift[1] + rot[2][i] * shift[2]) for i in range(3)]
    away = [mean[i] - eye[i] for i in range(3)]
    shrink = lax.rsqrt(sum(a * a for a in away))
    toward = [a * shrink for a in away]
    return dict(
        rot=rot,
        view=view,
        inverse=inverse,
        u=u,
        v=v,
        norm=norm,
        unit=(w, x, y, z),
        scales=scales,
        spread=spread,
        axes=axes,
        scale_x=scale_x,
        scale_y=scale_y,
        lean_x=lean_x,
        lean_y=lean_y,
        row_one=row_one,
        row_two=row_two,
        conic=conic,
        shrink=shrink,
        toward=toward,
    )


def three_parts(value):
    high = value.astype(jnp.bfloat16).astype(jnp.float32)
    rest = value - high
    mid = rest.astype(jnp.bfloat16).astype(jnp.float32)
    return high, mid, rest - mid


def sub_roll(value, shift):
    return pltpu.roll(value, shift % SUB, 0)


def render_kernel(
    pixels, hop_bits, me_ref, cam_id_ref, count_ref, list_ref, depth_ref, cameras_ref,
    blocks_ref, target_ref, basis_ref, xmom_ref, order_ref, back_ref, out_ref,
    raw, feat, coef, expo, shade, alphas, weights, carry, before, passed, colours,
    resid, behind, sums, found, rows, slots,
):
    listed = list_ref.shape[0]
    peers = out_ref.shape[0]
    per_owner = blocks_ref.shape[0] // peers
    yrows = pixels // LANES
    groups = LANES // SUB
    me = me_ref[0]
    count = count_ref[0]
    cam_id = cam_id_ref[0]
    cam = [cameras_ref[cam_id, k] for k in range(16)]
    top = ((me % 4) * yrows).astype(jnp.float32)

    def place_slot(j, ends):
        live_end, dead_end = ends
        slot = depth_ref[j]
        live = slot < count
        slots[jnp.where(live, live_end, dead_end)] = slot
        return jnp.where(live, live_end + 1, live_end), jnp.where(live, dead_end, dead_end + 1)

    lax.fori_loop(0, listed, place_slot, (jnp.int32(0), count))

    def fetch(k, _):
        block = list_ref[slots[k]]
        owner = block // per_owner
        if hop_bits is None:
            near = owner
        else:
            apart = me ^ owner
            near = sum((((apart >> bit) & 1) << t) for t, bit in enumerate(hop_bits))
        source = near * per_owner + block % per_owner
        raw[pl.ds(pl.multiple_of(k * ROWS, ROWS), blocks_ref.shape[1]), :] = blocks_ref[source]
        return 0

    lax.fori_loop(0, listed, fetch, 0)

    def row(p):
        return raw[pl.ds(p, listed, stride=ROWS), :]

    geo = geometry(row, cam)
    screen_x = cam[12] * geo["u"] + cam[14]
    screen_y = cam[13] * geo["v"] + cam[15]
    basis = harmonic_basis(*geo["toward"])
    tint = [sum(basis[k] * row(11 + 3 * k + c) for k in range(16)) + 0.5 for c in range(3)]
    log_opacity = -jnp.log(1.0 + jnp.exp(-row(10))) * log2e
    natural = [screen_x - 64.0, screen_y - (top + 4.0), *geo["conic"], log_opacity, *tint]
    for m, value in enumerate(natural):
        feat[m * listed : (m + 1) * listed, :] = value
    feat[...] = jnp.dot(feat[...], order_ref[...], precision=highest)
    sx, sy, ca, cb, cc, lo, *tint = [feat[m * listed : (m + 1) * listed, :] for m in range(9)]
    kxx = (-0.5 * log2e) * ca
    kxy = -log2e * cb
    kyy = (-0.5 * log2e) * cc
    kx = -2.0 * kxx * sx - kxy * sy
    ky = -2.0 * kyy * sy - kxy * sx
    k1 = kxx * sx * sx + kxy * sx * sy + kyy * sy * sy + lo
    for c, value in enumerate([kxx, kxx, kxy, kyy, kx, ky, k1, *tint]):
        for part, piece in enumerate(three_parts(value)):
            coef[pl.ds(part * 10 + c, listed, stride=KDIM), :] = piece
    zero = jnp.zeros((listed, LANES), jnp.float32)
    for c in range(30, KDIM):
        coef[pl.ds(c, listed, stride=KDIM), :] = zero

    sub = lax.broadcasted_iota(jnp.int32, (SUB, LANES), 0)
    one = jnp.ones((SUB, LANES), jnp.float32)
    none = jnp.zeros((SUB, LANES), jnp.float32)
    for y in range(yrows):
        carry[y] = one
    for c in range(3):
        for y in range(yrows):
            resid[c, y] = none

    def spread_row(value, index):
        return jnp.broadcast_to(value[index : index + 1, :], (SUB, LANES))

    def forward(k, _):
        mine = coef[pl.ds(pl.multiple_of(k * KDIM, KDIM), KDIM), :].astype(jnp.bfloat16)
        expo[...] = lax.dot_general(
            mine, basis_ref[...], (((0,), (0,)), ((), ())), preferred_element_type=jnp.float32
        )
        base = pl.multiple_of(k * LANES, LANES)
        shade[pl.ds(base, LANES), :] = expo[:, pixels:]
        kept = [one] * yrows
        total = [[none] * yrows for _ in range(3)]
        for i in range(groups):
            here = pl.ds(pl.multiple_of(base + i * SUB, SUB), SUB)
            tints = [
                expo[i * SUB : (i + 1) * SUB, pixels + c * LANES : pixels + (c + 1) * LANES]
                for c in range(3)
            ]
            for y in range(yrows):
                lanes = slice(y * LANES, (y + 1) * LANES)
                alpha = jnp.minimum(
                    alpha_ceiling, jnp.exp2(expo[i * SUB : (i + 1) * SUB, lanes])
                )
                weight = alpha * kept[y]
                alphas[here, lanes] = alpha
                weights[here, lanes] = weight
                kept[y] = kept[y] - weight
                for c in range(3):
                    total[c][y] = total[c][y] + weight * tints[c]
        for y in range(yrows):
            passed[k, y] = kept[y]
            through = kept[y]
            for step in (1, 2, 4):
                through = through * jnp.where(sub >= step, sub_roll(through, step), 1.0)
            entering = carry[y]
            ahead = entering * jnp.where(sub >= 1, sub_roll(through, 1), 1.0)
            before[k, y] = ahead
            carry[y] = entering * spread_row(through, SUB - 1)
            for c in range(3):
                colours[k, c, y] = total[c][y]
                resid[c, y] = resid[c, y] + ahead * total[c][y]
        return 0

    lax.fori_loop(0, count, forward, 0)

    for y in range(yrows):
        for c in range(3):
            value = jnp.sum(resid[c, y], axis=0, keepdims=True)
            value = value - target_ref[c : c + 1, y * LANES : (y + 1) * LANES]
            resid[c, y] = jnp.broadcast_to(value, (SUB, LANES))
        behind[y] = none

    def backward(back, _):
        k = count - 1 - back
        base = pl.multiple_of(k * LANES, LANES)
        pull = [[None] * yrows for _ in range(3)]
        rear = [None] * yrows
        for y in range(yrows):
            res = [resid[c, y] for c in range(3)]
            gain = passed[k, y]
            value = sum(colours[k, c, y] * res[c] for c in range(3))
            for step in (1, 2, 4):
                inside = sub < SUB - step
                value = value + gain * jnp.where(inside, sub_roll(value, -step), 0.0)
                gain = gain * jnp.where(inside, sub_roll(gain, -step), 1.0)
            last = behind[y]
            ahead = before[k, y]
            at_end = jnp.where(
                sub < SUB - 1, sub_roll(value, -1) + sub_roll(gain, -1) * last, last
            )
            behind[y] = spread_row(value + gain * last, 0)
            rear[y] = ahead * at_end
            for c in range(3):
                pull[c][y] = ahead * res[c]
        for i in reversed(range(groups)):
            here = pl.ds(pl.multiple_of(base + i * SUB, SUB), SUB)
            tints = [shade[here, c * LANES : (c + 1) * LANES] for c in range(3)]
            run = [none, none, none]
            drawn = [none, none, none]
            for y in range(yrows):
                lanes = slice(y * LANES, (y + 1) * LANES)
                alpha = alphas[here, lanes]
                weight = weights[here, lanes]
                gap = (
                    tints[0] * pull[0][y] + tints[1] * pull[1][y] + tints[2] * pull[2][y] - rear[y]
                )
                slope = jnp.where(alpha < alpha_ceiling, weight * gap, 0.0)
                rear[y] = rear[y] + alpha * gap
                run[0] = run[0] + slope
                run[1] = run[1] + run[0]
                run[2] = run[2] + run[1]
                for c in range(3):
                    drawn[c] = drawn[c] + weight * pull[c][y]
            for m, value in enumerate(run + drawn):
                sums[m * LANES + i * SUB : m * LANES + (i + 1) * SUB, :] = value
        value = sums[...]
        high = value.astype(jnp.bfloat16)
        low = (value - high.astype(jnp.float32)).astype(jnp.bfloat16)
        contract = (((1,), (1,)), ((), ()))
        xmom = xmom_ref[...]
        found[k] = lax.dot_general(
            xmom, high, contract, preferred_element_type=jnp.float32
        ) + lax.dot_general(xmom, low, contract, preferred_element_type=jnp.float32)
        return 0

    lax.fori_loop(0, count, backward, 0)

    lane = lax.broadcasted_iota(jnp.int32, (1, LANES), 1)
    middle = (
        lax.broadcasted_iota(jnp.int32, (SUB, LANES), 0) * (LANES // SEGS) + (LANES // SEGS // 2 - 64)
    ).astype(jnp.float32)
    meta = jnp.zeros((1, LANES), jnp.float32)
    for c in range(16):
        meta = jnp.where(lane == c, cam[c], meta)

    rows[...] = jnp.zeros(rows.shape, jnp.float32)

    def gather_moments(k, _):
        part = lambda order, m: found[k, order * SEGS : (order + 1) * SEGS, m * LANES : (m + 1) * LANES]
        add = lambda value: jnp.sum(value, axis=0, keepdims=True)
        off = middle - feat[pl.ds(k, 1), :]
        rise = (yrows - 4.0) - feat[pl.ds(listed + k, 1), :]
        h0, h1, h2 = part(0, 0), part(1, 0), part(2, 0)
        n0, n1 = part(0, 1), part(1, 1)
        s0 = add(h0)
        sx1 = add(h1 + off * h0)
        sxx = add(h2 + off * (2.0 * h1 + off * h0))
        t1 = add(n0)
        tx = add(n1 + off * n0)
        t2 = 2.0 * add(part(0, 2)) - t1
        sy1 = rise * s0 - t1
        sxy = rise * sx1 - tx
        syy = rise * (rise * s0 - 2.0 * t1) + t2
        answer = [s0, sx1, sy1, sxx, sxy, syy] + [add(part(0, 3 + c)) for c in range(3)]
        for m, value in enumerate(answer):
            rows[pl.ds(k * MSG + m, 1), :] = value
        return 0

    lax.fori_loop(0, count, gather_moments, 0)
    rows[...] = jnp.dot(rows[...], back_ref[...], precision=highest)

    if peers > listed:
        absent = jnp.where(lane == 16, -1.0, 0.0)
        for peer in range(peers):
            out_ref[peer] = jnp.broadcast_to(absent, (MSG, LANES))

    def send(k, _):
        block = list_ref[slots[k]]
        owner = block // per_owner
        place = (block % per_owner).astype(jnp.float32)
        rows[pl.ds(k * MSG + 9, 1), :] = jnp.where(lane == 16, place, meta)
        out_ref[owner] = rows[pl.ds(pl.multiple_of(k * MSG, MSG), MSG), :]
        return 0

    lax.fori_loop(0, listed, send, 0)


def owner_kernel(inbox_ref, own_ref, cons_ref, dual_ref, step_ref, share_ref, new_ref, vals_ref, grad):
    blocks = own_ref.shape[0]
    params = own_ref.shape[1]
    strips = inbox_ref.shape[0] // MSG

    def message(m):
        return inbox_ref[pl.ds(m, strips, stride=MSG), :]

    meta = message(9)
    cam = [jnp.broadcast_to(meta[:, k : k + 1], (strips, LANES)) for k in range(17)]
    place = cam[16]

    def row(p):
        value = jnp.broadcast_to(own_ref[0, p : p + 1, :], (strips, LANES))
        for b in range(1, blocks):
            value = jnp.where(place == b, own_ref[b, p : p + 1, :], value)
        return value

    geo = geometry(row, cam)
    s0, sx, sy, sxx, sxy, syy, *drawn = [message(m) for m in range(9)]
    ca, cb, cc = geo["conic"]
    u, v, inverse = geo["u"], geo["v"], geo["inverse"]
    axes, rot = geo["axes"], geo["rot"]
    focal_x, focal_y = cam[12], cam[13]
    grads = {}
    opacity = 1.0 / (1.0 + jnp.exp(-row(10)))
    grads[10] = s0 * (1.0 - opacity)
    t00, t01 = sxx * ca + sxy * cb, sxx * cb + sxy * cc
    t10, t11 = sxy * ca + syy * cb, sxy * cb + syy * cc
    g_xx = 0.5 * (ca * t00 + cb * t10)
    g_xy = ca * t01 + cb * t11
    g_yy = 0.5 * (cb * t01 + cc * t11)
    one, two = geo["row_one"], geo["row_two"]
    g_one = [2.0 * g_xx * one[k] + g_xy * two[k] for k in range(3)]
    g_two = [2.0 * g_yy * two[k] + g_xy * one[k] for k in range(3)]
    px, py = geo["scale_x"], geo["scale_y"]
    g_axes = [
        [px * g_one[k] for k in range(3)],
        [py * g_two[k] for k in range(3)],
        [-(px * u * g_one[k] + py * v * g_two[k]) for k in range(3)],
    ]
    g_px = sum(g_one[k] * geo["lean_x"][k] for k in range(3))
    g_py = sum(g_two[k] * geo["lean_y"][k] for k in range(3))
    g_u = focal_x * (ca * sx + cb * sy) - px * sum(g_one[k] * axes[2][k] for k in range(3))
    g_v = focal_y * (cc * sy + cb * sx) - py * sum(g_two[k] * axes[2][k] for k in range(3))
    view = geo["view"]
    g_inverse = focal_x * g_px + focal_y * g_py + view[0] * g_u + view[1] * g_v
    g_view = [inverse * g_u, inverse * g_v, -inverse * inverse * g_inverse]
    g_spread = [
        [sum(rot[i][j] * g_axes[i][k] for i in range(3)) for k in range(3)] for j in range(3)
    ]
    for k in range(3):
        grads[3 + k] = sum(g_spread[j][k] * geo["spread"][j][k] for j in range(3))
    g = [[g_spread[j][k] * geo["scales"][k] for k in range(3)] for j in range(3)]
    w, x, y, z = geo["unit"]
    g_w = 2.0 * (z * (g[1][0] - g[0][1]) + y * (g[0][2] - g[2][0]) + x * (g[2][1] - g[1][2]))
    g_x = 2.0 * (
        y * (g[0][1] + g[1][0])
        + z * (g[0][2] + g[2][0])
        + w * (g[2][1] - g[1][2])
        - 2.0 * x * (g[1][1] + g[2][2])
    )
    g_y = 2.0 * (
        x * (g[0][1] + g[1][0])
        + z * (g[1][2] + g[2][1])
        + w * (g[0][2] - g[2][0])
        - 2.0 * y * (g[0][0] + g[2][2])
    )
    g_z = 2.0 * (
        x * (g[0][2] + g[2][0])
        + y * (g[1][2] + g[2][1])
        + w * (g[1][0] - g[0][1])
        - 2.0 * z * (g[0][0] + g[1][1])
    )
    along = w * g_w + x * g_x + y * g_y + z * g_z
    for p, (g_q, q) in enumerate(((g_w, w), (g_x, x), (g_y, y), (g_z, z))):
        grads[6 + p] = (g_q - q * along) * geo["norm"]
    x, y, z = geo["toward"]
    basis = harmonic_basis(x, y, z)
    h = [None]
    for k in range(16):
        if k:
            h.append(sum(drawn[c] * row(11 + 3 * k + c) for c in range(3)))
        for c in range(3):
            grads[11 + 3 * k + c] = basis[k] * drawn[c]
    a, d = sh_two, sh_three
    xx, yy, zz, xy, yz, xz = x * x, y * y, z * z, x * y, y * z, x * z
    g_dx = (
        -sh_one * h[3] + a[0] * y * h[4] - 2.0 * a[2] * x * h[6] + a[3] * z * h[7]
        + 2.0 * a[4] * x * h[8] + 6.0 * d[0] * xy * h[9] + d[1] * yz * h[10]
        - 2.0 * d[2] * xy * h[11] - 6.0 * d[3] * xz * h[12]
        + d[4] * (4.0 * zz - 3.0 * xx - yy) * h[13] + 2.0 * d[5] * xz * h[14]
        + 3.0 * d[6] * (xx - yy) * h[15]
    )
    g_dy = (
        -sh_one * h[1] + a[0] * x * h[4] + a[1] * z * h[5] - 2.0 * a[2] * y * h[6]
        - 2.0 * a[4] * y * h[8] + 3.0 * d[0] * (xx - yy) * h[9] + d[1] * xz * h[10]
        + d[2] * (4.0 * zz - xx - 3.0 * yy) * h[11] - 6.0 * d[3] * yz * h[12]
        - 2.0 * d[4] * xy * h[13] - 2.0 * d[5] * yz * h[14] - 6.0 * d[6] * xy * h[15]
    )
    g_dz = (
        sh_one * h[2] + a[1] * y * h[5] + 4.0 * a[2] * z * h[6] + a[3] * x * h[7]
        + d[1] * xy * h[10] + 8.0 * d[2] * yz * h[11]
        + 3.0 * d[3] * (2.0 * zz - xx - yy) * h[12] + 8.0 * d[4] * xz * h[13]
        + d[5] * (xx - yy) * h[14]
    )
    along = x * g_dx + y * g_dy + z * g_dz
    turned = [(gd - t * along) * geo["shrink"] for gd, t in ((g_dx, x), (g_dy, y), (g_dz, z))]
    for j in range(3):
        grads[j] = sum(rot[i][j] * g_view[i] for i in range(3)) + turned[j]
    for b in range(blocks):
        mine = place == b
        for p in range(params):
            grad[b, p : p + 1, :] = jnp.sum(
                jnp.where(mine, grads[p], 0.0), axis=0, keepdims=True
            )

    shape = (params, params)
    diagonal = lax.broadcasted_iota(jnp.int32, shape, 0) == lax.broadcasted_iota(jnp.int32, shape, 1)
    steps = jnp.sum(
        jnp.where(diagonal, jnp.broadcast_to(step_ref[...], shape), 0.0), axis=1, keepdims=True
    )
    half = share_ref.shape[1]
    local = lax.broadcasted_iota(jnp.int32, (LANES, half), 0)
    vals = [jnp.zeros((params, half), jnp.float32) for _ in range(2)]
    for b in range(blocks):
        here = own_ref[b]
        dual = dual_ref[b]
        new = here - steps * (
            grad[b, :params, :] + penalty_weight * (here - cons_ref[b] + dual)
        )
        new_ref[b] = new
        shifted = new + dual
        for side in range(2):
            pick = (share_ref[side : side + 1, :] == local + b * LANES).astype(jnp.float32)
            vals[side] = vals[side] + jnp.dot(shifted, pick, precision=highest)
    for side in range(2):
        vals_ref[side] = vals[side]


def agree_kernel(last_group, group_ref, vals_ref, above_ref, below_ref, share_ref, out_ref):
    group = group_ref[0]
    half = share_ref.shape[1]
    blocks, params = out_ref.shape[0], out_ref.shape[1]
    changes = []
    for side, other, shared in ((0, above_ref, group < last_group), (1, below_ref, group > 0)):
        mine = vals_ref[side]
        change = mine - 0.5 * (mine + other[1 - side])
        changes.append(jnp.where(shared, change, 0.0))
    local = lax.broadcasted_iota(jnp.int32, (LANES, half), 0)
    for b in range(blocks):
        total = jnp.zeros((params, LANES), jnp.float32)
        for side in range(2):
            pick = (share_ref[side : side + 1, :] == local + b * LANES).astype(jnp.float32)
            total = total + lax.dot_general(
                changes[side], pick, (((1,), (1,)), ((), ())), precision=highest,
                preferred_element_type=jnp.float32,
            )
        out_ref[b] = total


def constants(pixels):
    place = np.arange(pixels)
    x = (place % LANES - 64).astype(np.float32)
    y = (place // LANES - 4).astype(np.float32)
    square = (x * x).astype(jnp.bfloat16).astype(np.float32)
    some = np.ones_like(x)
    part = np.zeros((10, pixels + 3 * LANES), np.float32)
    for c, value in enumerate([square, x * x - square, x * y, y * y, x, y, some]):
        part[c, :pixels] = value
    for c in range(3):
        part[7 + c, pixels + c * LANES : pixels + (c + 1) * LANES] = 1.0
    basis = np.zeros((KDIM, pixels + 3 * LANES), np.float32)
    basis[:30] = np.concatenate([part] * 3)
    lane = np.arange(LANES)
    wide = LANES // SEGS
    xmom = np.zeros((3 * SEGS + SEGS, LANES), np.float32)
    for s in range(SEGS):
        near = (lane // wide == s).astype(np.float32)
        offset = lane - s * wide - wide // 2
        for power in range(3):
            xmom[power * SEGS + s] = near * offset**power
    order = np.zeros((LANES, LANES), np.float32)
    groups = LANES // SUB
    for r in range(LANES):
        order[(r % SUB) * groups + r // SUB, r] = 1.0
    return (
        jnp.asarray(basis, jnp.bfloat16),
        jnp.asarray(xmom, jnp.bfloat16),
        jnp.asarray(order),
        jnp.asarray(order.T.copy()),
    )


def vmem():
    return pl.BlockSpec(memory_space=pltpu.VMEM)


def smem():
    return pl.BlockSpec(memory_space=pltpu.SMEM)


def on_device(
    gaussians, consensus, duals, step_sizes, cameras, camera_ids, block_lists, depth_order,
    block_counts, targets, intersection,
):
    own = gaussians[0]
    blocks, params = own.shape[0], own.shape[1]
    peers = lax.axis_size("tile")
    me = lax.axis_index("tile")
    listed = block_lists.shape[2]
    pixels = targets.shape[3]
    yrows = pixels // LANES
    f32 = jnp.float32

    everything = own
    hop_bits = None
    if peers & (peers - 1) == 0:
        hop_bits = list(reversed(range(peers.bit_length() - 1)))
        for bit in hop_bits:
            arrived = lax.ppermute(
                everything, "tile", [(i, i ^ (1 << bit)) for i in range(peers)]
            )
            everything = jnp.concatenate([everything, arrived], 0)
    else:
        everything = lax.all_gather(own, "tile", axis=0, tiled=True)

    basis, xmom, order, back = constants(pixels)
    outbox = pl.pallas_call(
        functools.partial(render_kernel, pixels, hop_bits),
        out_shape=jax.ShapeDtypeStruct((peers, MSG, LANES), f32),
        in_specs=[smem()] * 6 + [vmem()] * 6,
        out_specs=vmem(),
        scratch_shapes=[
            pltpu.VMEM((listed * ROWS, LANES), f32),
            pltpu.VMEM((9 * listed, LANES), f32),
            pltpu.VMEM((listed * KDIM, LANES), f32),
            pltpu.VMEM((LANES, pixels + 3 * LANES), f32),
            pltpu.VMEM((listed * LANES, 3 * LANES), f32),
            pltpu.VMEM((listed * LANES, pixels), f32),
            pltpu.VMEM((listed * LANES, pixels), f32),
            pltpu.VMEM((yrows, SUB, LANES), f32),
            pltpu.VMEM((listed, yrows, SUB, LANES), f32),
            pltpu.VMEM((listed, yrows, SUB, LANES), f32),
            pltpu.VMEM((listed, 3, yrows, SUB, LANES), f32),
            pltpu.VMEM((3, yrows, SUB, LANES), f32),
            pltpu.VMEM((yrows, SUB, LANES), f32),
            pltpu.VMEM((MOMENTS * LANES, LANES), f32),
            pltpu.VMEM((listed, 4 * SEGS, MOMENTS * LANES), f32),
            pltpu.VMEM((listed * MSG, LANES), f32),
            pltpu.SMEM((listed,), jnp.int32),
        ],
        compiler_params=pltpu.CompilerParams(vmem_limit_bytes=48 * 2**20),
        name="render",
    )(
        me[None], camera_ids[0], block_counts[0], block_lists[0, 0], depth_order[0, 0], cameras,
        everything, targets[0, 0], basis, xmom, order, back,
    )
    inbox = lax.all_to_all(outbox, "tile", split_axis=0, concat_axis=0, tiled=True)
    share = intersection[0, 0]
    half = share.shape[1]
    updated, vals = pl.pallas_call(
        owner_kernel,
        out_shape=(
            jax.ShapeDtypeStruct(own.shape, f32),
            jax.ShapeDtypeStruct((2, params, half), f32),
        ),
        in_specs=[vmem()] * 6,
        out_specs=(vmem(), vmem()),
        scratch_shapes=[pltpu.VMEM((blocks, ROWS, LANES), f32)],
        compiler_params=pltpu.CompilerParams(vmem_limit_bytes=32 * 2**20),
        name="owner",
    )(inbox.reshape(peers * MSG, LANES), own, consensus[0], duals[0], step_sizes[None, :], share)
    group_total = lax.axis_size("scene")
    group = lax.axis_index("scene")
    if group_total == 2:
        above = below = lax.ppermute(vals, "scene", [(0, 1), (1, 0)])
    else:
        above = lax.ppermute(vals, "scene", [(g + 1, g) for g in range(group_total - 1)])
        below = lax.ppermute(vals, "scene", [(g, g + 1) for g in range(group_total - 1)])
    new_duals = pl.pallas_call(
        functools.partial(agree_kernel, group_total - 1),
        out_shape=jax.ShapeDtypeStruct(own.shape, f32),
        in_specs=[smem()] + [vmem()] * 4,
        out_specs=vmem(),
        name="agree",
    )(group[None], vals, above, below, share)
    return updated[None], new_duals[None]


def solution(mesh):
    placed = (
        P("scene", "tile", None, None),
        P("scene", "tile", None, None),
        P("scene", "tile", None, None),
        P(),
        P(),
        P("scene", "tile"),
        P("scene", "tile", None),
        P("scene", "tile", None),
        P("scene", "tile"),
        P("scene", "tile", None, None),
        P("scene", "tile", None, None),
    )
    return jax.shard_map(
        on_device,
        mesh=mesh,
        in_specs=placed,
        out_specs=(P("scene", "tile", None, None), P("scene", "tile", None, None)),
        check_vma=False,
    )
```

```python
import functools

import jax
import jax.numpy as jnp
import numpy as np
from jax import lax
from jax.experimental import pallas as pl
from jax.experimental.pallas import tpu as pltpu
from jax.sharding import PartitionSpec as P

penalty_weight = 0.5
blur_floor = 0.3
alpha_ceiling = 0.99
log2e = 1.4426950408889634
sh_zero = 0.28209479177387814
sh_one = 0.4886025119029199
sh_two = (
    1.0925484305920792,
    -1.0925484305920792,
    0.31539156525252005,
    -1.0925484305920792,
    0.5462742152960396,
)
sh_three = (
    -0.5900435899266435,
    2.890611442640554,
    -0.4570457994644658,
    0.3731763325901154,
    -0.4570457994644658,
    1.445305721320277,
    -0.5900435899266435,
)

LANES = 128
SUB = 8
PART = 16
KDIM = 3 * PART
COEFS = 9
INNER = 4
SEGS = 8
MOMENTS = 6
MSG = 16
highest = lax.Precision.HIGHEST


def harmonic_basis(x, y, z):
    xx, yy, zz = x * x, y * y, z * z
    return [
        sh_zero + 0.0 * x,
        -sh_one * y,
        sh_one * z,
        -sh_one * x,
        sh_two[0] * x * y,
        sh_two[1] * y * z,
        sh_two[2] * (2.0 * zz - xx - yy),
        sh_two[3] * x * z,
        sh_two[4] * (xx - yy),
        sh_three[0] * y * (3.0 * xx - yy),
        sh_three[1] * x * y * z,
        sh_three[2] * y * (4.0 * zz - xx - yy),
        sh_three[3] * z * (2.0 * zz - 3.0 * xx - 3.0 * yy),
        sh_three[4] * x * (4.0 * zz - xx - yy),
        sh_three[5] * z * (xx - yy),
        sh_three[6] * x * (xx - 3.0 * yy),
    ]


def geometry(row, cam):
    mean = [row(0), row(1), row(2)]
    rot = [[cam[3 * i + j] for j in range(3)] for i in range(3)]
    shift = [cam[9 + i] for i in range(3)]
    focal_x, focal_y = cam[12], cam[13]
    view = [
        rot[i][0] * mean[0] + rot[i][1] * mean[1] + rot[i][2] * mean[2] + shift[i] for i in range(3)
    ]
    inverse = 1.0 / view[2]
    u = view[0] * inverse
    v = view[1] * inverse
    quat = [row(6 + i) for i in range(4)]
    norm = lax.rsqrt(sum(q * q for q in quat))
    w, x, y, z = [q * norm for q in quat]
    turn = [
        [1.0 - 2.0 * (y * y + z * z), 2.0 * (x * y - w * z), 2.0 * (x * z + w * y)],
        [2.0 * (x * y + w * z), 1.0 - 2.0 * (x * x + z * z), 2.0 * (y * z - w * x)],
        [2.0 * (x * z - w * y), 2.0 * (y * z + w * x), 1.0 - 2.0 * (x * x + y * y)],
    ]
    scales = [jnp.exp(row(3 + k)) for k in range(3)]
    spread = [[turn[j][k] * scales[k] for k in range(3)] for j in range(3)]
    axes = [
        [sum(rot[i][j] * spread[j][k] for j in range(3)) for k in range(3)] for i in range(3)
    ]
    scale_x = focal_x * inverse
    scale_y = focal_y * inverse
    lean_x = [axes[0][k] - u * axes[2][k] for k in range(3)]
    lean_y = [axes[1][k] - v * axes[2][k] for k in range(3)]
    row_one = [scale_x * lean_x[k] for k in range(3)]
    row_two = [scale_y * lean_y[k] for k in range(3)]
    cov_xx = sum(a * a for a in row_one) + blur_floor
    cov_xy = sum(a * b for a, b in zip(row_one, row_two))
    cov_yy = sum(b * b for b in row_two) + blur_floor
    scale = 1.0 / (cov_xx * cov_yy - cov_xy * cov_xy)
    conic = (cov_yy * scale, -cov_xy * scale, cov_xx * scale)
    eye = [-(rot[0][i] * shift[0] + rot[1][i] * shift[1] + rot[2][i] * shift[2]) for i in range(3)]
    away = [mean[i] - eye[i] for i in range(3)]
    shrink = lax.rsqrt(sum(a * a for a in away))
    toward = [a * shrink for a in away]
    return dict(
        rot=rot,
        view=view,
        inverse=inverse,
        u=u,
        v=v,
        norm=norm,
        unit=(w, x, y, z),
        scales=scales,
        spread=spread,
        axes=axes,
        scale_x=scale_x,
        scale_y=scale_y,
        lean_x=lean_x,
        lean_y=lean_y,
        row_one=row_one,
        row_two=row_two,
        conic=conic,
        shrink=shrink,
        toward=toward,
    )


def three_parts(value):
    high = value.astype(jnp.bfloat16).astype(jnp.float32)
    rest = value - high
    mid = rest.astype(jnp.bfloat16).astype(jnp.float32)
    return high, mid, rest - mid


def exact_pick(value, pick):
    high, mid, low = [part.astype(jnp.bfloat16) for part in three_parts(value)]
    dot = functools.partial(jnp.dot, preferred_element_type=jnp.float32)
    return (dot(high, pick) + dot(mid, pick)) + dot(low, pick)


def sub_roll(value, shift):
    return pltpu.roll(value, shift % SUB, 0)


def prepare_kernel(
    links, group_ref, own_ref, cons_ref, dual_ref, step_ref, share_ref, *refs
):
    others, (base_ref, steps_ref, pick_ref, mask_ref) = refs[: len(links)], refs[len(links) :]
    blocks, params = own_ref.shape[0], own_ref.shape[1]
    group = group_ref[0]
    shape = (params, params)
    diagonal = lax.broadcasted_iota(jnp.int32, shape, 0) == lax.broadcasted_iota(jnp.int32, shape, 1)
    steps = jnp.sum(
        jnp.where(diagonal, jnp.broadcast_to(step_ref[...], shape), 0.0), axis=1, keepdims=True
    )
    steps = jnp.broadcast_to(steps, (params, LANES))
    steps_ref[...] = steps
    for b in range(blocks):
        here = own_ref[b]
        base_ref[b] = here - steps * (penalty_weight * (here - cons_ref[b] + dual_ref[b]))
    half = share_ref.shape[1]
    local = lax.broadcasted_iota(jnp.int32, (blocks * LANES, half), 0)
    contract = (((1,), (1,)), ((), ()))
    for n, (side_of, exists_of) in enumerate(links):
        other = others[n]
        up = side_of(group)
        mine = jnp.where(up, share_ref[0:1, :], share_ref[1:2, :])
        theirs = jnp.where(up, other[1:2, :], other[0:1, :])
        source = (local == mine).astype(jnp.bfloat16)
        target = (local == theirs).astype(jnp.bfloat16)
        pick_ref[n] = lax.dot_general(
            source, target, contract, preferred_element_type=jnp.float32
        ).astype(jnp.bfloat16)
        there = jnp.full((SUB, half), jnp.where(exists_of(group), 1.0, 0.0)).astype(jnp.bfloat16)
        mask = lax.dot_general(there, source, contract, preferred_element_type=jnp.float32)
        for b in range(blocks):
            mask_ref[n, b] = mask[:, b * LANES : (b + 1) * LANES]


def project_kernel(masks, yrows, me_ref, raw_ref, ids_ref, cameras_ref, order_ref, *refs):
    outs, feat = refs[:INNER], refs[INNER]
    outer = len(masks)
    blocks = raw_ref.shape[0] // outer
    me = me_ref[0]
    ids = jnp.concatenate([ids_ref[...]] * (SUB // INNER), axis=0)
    lane = lax.broadcasted_iota(jnp.int32, (SUB, LANES), 1)
    sub = lax.broadcasted_iota(jnp.int32, (SUB, LANES), 0)
    ncam = cameras_ref.shape[0]
    chosen = lax.broadcasted_iota(jnp.int32, (SUB, ncam), 1) == ids[:, 0:1]
    shots = jnp.dot(chosen.astype(jnp.float32), cameras_ref[...], precision=highest)
    cam = [jnp.broadcast_to(shots[:, k : k + 1], (SUB, LANES)) for k in range(16)]
    top = (((me & 3) ^ (sub & 3)) * yrows).astype(jnp.float32)
    lists = ids[:, LANES:]
    rows = outer * INNER
    for v in range(rows // SUB):
        owners = [2 * v, 2 * v + 1]
        first = jnp.where(sub < INNER, (me ^ masks[owners[0]]) * blocks, (me ^ masks[owners[1]]) * blocks)
        found = []
        for b in range(1, blocks):
            same = (lists == first[:, : lists.shape[1]] + b).astype(jnp.float32)
            found.append(jnp.broadcast_to(jnp.max(same, axis=1, keepdims=True), (SUB, LANES)) > 0.5)

        def row(p):
            def of(b):
                return jnp.where(
                    sub < INNER,
                    jnp.broadcast_to(raw_ref[owners[0] * blocks + b, p : p + 1, :], (SUB, LANES)),
                    jnp.broadcast_to(raw_ref[owners[1] * blocks + b, p : p + 1, :], (SUB, LANES)),
                )

            value = of(0)
            for b in range(1, blocks):
                value = jnp.where(found[b - 1], of(b), value)
            return value

        geo = geometry(row, cam)
        sx = cam[12] * geo["u"] + (cam[14] - 64.0)
        sy = cam[13] * geo["v"] + (cam[15] - top - 4.0)
        basis = harmonic_basis(*geo["toward"])
        tint = [sum(basis[k] * row(11 + 3 * k + c) for k in range(16)) + 0.5 for c in range(3)]
        lo = -jnp.log(1.0 + jnp.exp(-row(10))) * log2e
        ca, cb, cc = geo["conic"]
        kxx = (-0.5 * log2e) * ca
        kxy = -log2e * cb
        kyy = (-0.5 * log2e) * cc
        kx = -2.0 * kxx * sx - kxy * sy
        ky = -2.0 * kyy * sy - kxy * sx
        k1 = kxx * sx * sx + kxy * sx * sy + kyy * sy * sy + lo
        for m, value in enumerate([kxx, kxy, kyy, kx, ky, k1, *tint]):
            feat[m * rows + v * SUB : m * rows + (v + 1) * SUB, :] = value
    feat[...] = exact_pick(feat[...], order_ref[...])
    for j in range(INNER):
        outs[j][...] = feat[pl.ds(j, COEFS * outer, stride=INNER), :]


def render_kernel(
    pixels, blocks, hop_bits, me_ref, cam_id_ref, count_ref, list_ref, depth_ref, cameras_ref,
    src0, src1, src2, src3, target_ref, basis_ref, xmom_ref, back_ref, out_ref,
    raw, coef, expo, shade, alphas, weights, carry, before, passed, colours,
    resid, behind, sums, found, rows, slots,
):
    listed = list_ref.shape[0]
    peers = out_ref.shape[0]
    outer = peers // INNER
    per_owner = blocks
    yrows = pixels // LANES
    groups = LANES // SUB
    me = me_ref[0]
    count = count_ref[0]
    cam_id = cam_id_ref[0]
    top = ((me % 4) * yrows).astype(jnp.float32)

    def place_slot(j, ends):
        live_end, dead_end = ends
        slot = depth_ref[j]
        live = slot < count
        slots[jnp.where(live, live_end, dead_end)] = slot
        return jnp.where(live, live_end + 1, live_end), jnp.where(live, dead_end, dead_end + 1)

    lax.fori_loop(0, listed, place_slot, (jnp.int32(0), count))

    for j, src in enumerate((src0, src1, src2, src3)):
        raw[j * COEFS * outer : (j + 1) * COEFS * outer, :] = src[...]
    coef[...] = jnp.zeros(coef.shape, jnp.float32)

    def fetch(k, _):
        apart = me ^ (list_ref[slots[k]] // per_owner)
        near = sum((((apart >> bit) & 1) << t) for t, bit in enumerate(hop_bits))
        start = (apart & (INNER - 1)) * (COEFS * outer) + near
        value = raw[pl.ds(start, COEFS, stride=outer), :]
        for part, piece in enumerate(three_parts(value)):
            base = pl.multiple_of(k * KDIM + part * PART, PART)
            coef[pl.ds(base, COEFS), :] = piece
            coef[pl.ds(base + COEFS, 1), :] = piece[0:1, :]
        return 0

    lax.fori_loop(0, count, fetch, 0)

    sub = lax.broadcasted_iota(jnp.int32, (SUB, LANES), 0)
    one = jnp.ones((SUB, LANES), jnp.float32)
    none = jnp.zeros((SUB, LANES), jnp.float32)
    for y in range(yrows):
        carry[y] = one
    for c in range(3):
        for y in range(yrows):
            resid[c, y] = none

    def spread_row(value, index):
        return jnp.broadcast_to(value[index : index + 1, :], (SUB, LANES))

    def forward(k, _):
        mine = coef[pl.ds(pl.multiple_of(k * KDIM, PART), KDIM), :].astype(jnp.bfloat16)
        expo[...] = lax.dot_general(
            mine, basis_ref[...], (((0,), (0,)), ((), ())), preferred_element_type=jnp.float32
        )
        base = pl.multiple_of(k * LANES, LANES)
        shade[pl.ds(base, LANES), :] = expo[:, pixels:]
        kept = [one] * yrows
        total = [[none] * yrows for _ in range(3)]
        for i in range(groups):
            here = pl.ds(pl.multiple_of(base + i * SUB, SUB), SUB)
            tints = [
                expo[i * SUB : (i + 1) * SUB, pixels + c * LANES : pixels + (c + 1) * LANES]
                for c in range(3)
            ]
            for y in range(yrows):
                lanes = slice(y * LANES, (y + 1) * LANES)
                alpha = jnp.minimum(
                    alpha_ceiling, jnp.exp2(expo[i * SUB : (i + 1) * SUB, lanes])
                )
                weight = alpha * kept[y]
                alphas[here, lanes] = alpha
                weights[here, lanes] = weight
                kept[y] = kept[y] - weight
                for c in range(3):
                    total[c][y] = total[c][y] + weight * tints[c]
        for y in range(yrows):
            passed[k, y] = kept[y]
            through = kept[y]
            for step in (1, 2, 4):
                through = through * jnp.where(sub >= step, sub_roll(through, step), 1.0)
            entering = carry[y]
            ahead = entering * jnp.where(sub >= 1, sub_roll(through, 1), 1.0)
            before[k, y] = ahead
            carry[y] = entering * spread_row(through, SUB - 1)
            for c in range(3):
                colours[k, c, y] = total[c][y]
                resid[c, y] = resid[c, y] + ahead * total[c][y]
        return 0

    lax.fori_loop(0, count, forward, 0)

    for y in range(yrows):
        for c in range(3):
            value = jnp.sum(resid[c, y], axis=0, keepdims=True)
            value = value - target_ref[c : c + 1, y * LANES : (y + 1) * LANES]
            resid[c, y] = jnp.broadcast_to(value, (SUB, LANES))
        behind[y] = none

    def backward(back, _):
        k = count - 1 - back
        base = pl.multiple_of(k * LANES, LANES)
        pull = [[None] * yrows for _ in range(3)]
        rear = [None] * yrows
        for y in range(yrows):
            res = [resid[c, y] for c in range(3)]
            gain = passed[k, y]
            value = sum(colours[k, c, y] * res[c] for c in range(3))
            for step in (1, 2, 4):
                inside = sub < SUB - step
                value = value + gain * jnp.where(inside, sub_roll(value, -step), 0.0)
                gain = gain * jnp.where(inside, sub_roll(gain, -step), 1.0)
            last = behind[y]
            ahead = before[k, y]
            at_end = jnp.where(
                sub < SUB - 1, sub_roll(value, -1) + sub_roll(gain, -1) * last, last
            )
            behind[y] = spread_row(value + gain * last, 0)
            rear[y] = ahead * at_end
            for c in range(3):
                pull[c][y] = ahead * res[c]
        for i in reversed(range(groups)):
            here = pl.ds(pl.multiple_of(base + i * SUB, SUB), SUB)
            tints = [shade[here, c * LANES : (c + 1) * LANES] for c in range(3)]
            run = [none, none, none]
            drawn = [none, none, none]
            for y in range(yrows):
                lanes = slice(y * LANES, (y + 1) * LANES)
                alpha = alphas[here, lanes]
                weight = weights[here, lanes]
                gap = (
                    tints[0] * pull[0][y] + tints[1] * pull[1][y] + tints[2] * pull[2][y] - rear[y]
                )
                slope = jnp.where(alpha < alpha_ceiling, weight * gap, 0.0)
                rear[y] = rear[y] + alpha * gap
                run[0] = run[0] + slope
                run[1] = run[1] + run[0]
                run[2] = run[2] + run[1]
                for c in range(3):
                    drawn[c] = drawn[c] + weight * pull[c][y]
            for m, value in enumerate(run + drawn):
                sums[m * LANES + i * SUB : m * LANES + (i + 1) * SUB, :] = value
        value = sums[...]
        high = value.astype(jnp.bfloat16)
        low = (value - high.astype(jnp.float32)).astype(jnp.bfloat16)
        contract = (((1,), (1,)), ((), ()))
        xmom = xmom_ref[...]
        found[k] = lax.dot_general(
            xmom, high, contract, preferred_element_type=jnp.float32
        ) + lax.dot_general(xmom, low, contract, preferred_element_type=jnp.float32)
        return 0

    lax.fori_loop(0, count, backward, 0)

    lane = lax.broadcasted_iota(jnp.int32, (1, LANES), 1)
    middle = (
        lax.broadcasted_iota(jnp.int32, (SUB, LANES), 0) * (LANES // SEGS)
        + (LANES // SEGS // 2 - 64)
    ).astype(jnp.float32)
    meta = jnp.where(lane == 17, top, 0.0)
    for c in range(16):
        meta = jnp.where(lane == c, cameras_ref[cam_id, c], meta)

    rows[...] = jnp.zeros(rows.shape, jnp.float32)

    def gather_moments(k, _):
        part = lambda order, m: found[k, order * SEGS : (order + 1) * SEGS, m * LANES : (m + 1) * LANES]
        add = lambda value: jnp.sum(value, axis=0, keepdims=True)
        rise = yrows - 4.0
        h0, h1, h2 = part(0, 0), part(1, 0), part(2, 0)
        n0, n1 = part(0, 1), part(1, 1)
        s0 = add(h0)
        x1 = add(h1 + middle * h0)
        x2 = add(h2 + middle * (2.0 * h1 + middle * h0))
        t1 = add(n0)
        tx = add(n1 + middle * n0)
        t2 = 2.0 * add(part(0, 2)) - t1
        answer = [s0, x1, rise * s0 - t1, x2, rise * x1 - tx, rise * (rise * s0 - 2.0 * t1) + t2]
        answer += [add(part(0, 3 + c)) for c in range(3)]
        for m, value in enumerate(answer):
            rows[pl.ds(k * MSG + m, 1), :] = value
        return 0

    lax.fori_loop(0, count, gather_moments, 0)
    rows[...] = exact_pick(rows[...], back_ref[...])

    if peers > listed:
        absent = jnp.where(lane == 16, -1.0, 0.0)
        for peer in range(peers):
            out_ref[peer] = jnp.broadcast_to(absent, (MSG, LANES))

    def send(k, _):
        block = list_ref[slots[k]]
        owner = block // per_owner
        place = (block % per_owner).astype(jnp.float32)
        rows[pl.ds(k * MSG + 9, 1), :] = jnp.where(lane == 16, place, meta)
        out_ref[owner] = rows[pl.ds(pl.multiple_of(k * MSG, MSG), MSG), :]
        return 0

    lax.fori_loop(0, listed, send, 0)


def owner_kernel(
    inbox_ref, own_ref, base_ref, dual_ref, steps_ref, pick_ref, new_ref, shifted_ref, sent_ref, grad
):
    blocks = own_ref.shape[0]
    params = own_ref.shape[1]
    strips = inbox_ref.shape[0] // MSG

    def message(m):
        return inbox_ref[pl.ds(m, strips, stride=MSG), :]

    meta = message(9)
    cam = [jnp.broadcast_to(meta[:, k : k + 1], (strips, LANES)) for k in range(18)]
    place, top = cam[16], cam[17]

    def row(p):
        value = jnp.broadcast_to(own_ref[0, p : p + 1, :], (strips, LANES))
        for b in range(1, blocks):
            value = jnp.where(place == b, own_ref[b, p : p + 1, :], value)
        return value

    geo = geometry(row, cam)
    u, v, inverse = geo["u"], geo["v"], geo["inverse"]
    focal_x, focal_y = cam[12], cam[13]
    at_x = focal_x * u + (cam[14] - 64.0)
    at_y = focal_y * v + (cam[15] - top - 4.0)
    s0, x1, y1, x2, xy, y2, *drawn = [message(m) for m in range(9)]
    sx = x1 - at_x * s0
    sy = y1 - at_y * s0
    sxx = x2 - at_x * (x1 + sx)
    sxy = xy - at_x * y1 - at_y * sx
    syy = y2 - at_y * (y1 + sy)
    ca, cb, cc = geo["conic"]
    axes, rot = geo["axes"], geo["rot"]
    grads = {}
    opacity = 1.0 / (1.0 + jnp.exp(-row(10)))
    grads[10] = s0 * (1.0 - opacity)
    t00, t01 = sxx * ca + sxy * cb, sxx * cb + sxy * cc
    t10, t11 = sxy * ca + syy * cb, sxy * cb + syy * cc
    g_xx = 0.5 * (ca * t00 + cb * t10)
    g_xy = ca * t01 + cb * t11
    g_yy = 0.5 * (cb * t01 + cc * t11)
    one, two = geo["row_one"], geo["row_two"]
    g_one = [2.0 * g_xx * one[k] + g_xy * two[k] for k in range(3)]
    g_two = [2.0 * g_yy * two[k] + g_xy * one[k] for k in range(3)]
    px, py = geo["scale_x"], geo["scale_y"]
    g_axes = [
        [px * g_one[k] for k in range(3)],
        [py * g_two[k] for k in range(3)],
        [-(px * u * g_one[k] + py * v * g_two[k]) for k in range(3)],
    ]
    g_px = sum(g_one[k] * geo["lean_x"][k] for k in range(3))
    g_py = sum(g_two[k] * geo["lean_y"][k] for k in range(3))
    g_u = focal_x * (ca * sx + cb * sy) - px * sum(g_one[k] * axes[2][k] for k in range(3))
    g_v = focal_y * (cc * sy + cb * sx) - py * sum(g_two[k] * axes[2][k] for k in range(3))
    view = geo["view"]
    g_inverse = focal_x * g_px + focal_y * g_py + view[0] * g_u + view[1] * g_v
    g_view = [inverse * g_u, inverse * g_v, -inverse * inverse * g_inverse]
    g_spread = [
        [sum(rot[i][j] * g_axes[i][k] for i in range(3)) for k in range(3)] for j in range(3)
    ]
    for k in range(3):
        grads[3 + k] = sum(g_spread[j][k] * geo["spread"][j][k] for j in range(3))
    g = [[g_spread[j][k] * geo["scales"][k] for k in range(3)] for j in range(3)]
    w, x, y, z = geo["unit"]
    g_w = 2.0 * (z * (g[1][0] - g[0][1]) + y * (g[0][2] - g[2][0]) + x * (g[2][1] - g[1][2]))
    g_x = 2.0 * (
        y * (g[0][1] + g[1][0])
        + z * (g[0][2] + g[2][0])
        + w * (g[2][1] - g[1][2])
        - 2.0 * x * (g[1][1] + g[2][2])
    )
    g_y = 2.0 * (
        x * (g[0][1] + g[1][0])
        + z * (g[1][2] + g[2][1])
        + w * (g[0][2] - g[2][0])
        - 2.0 * y * (g[0][0] + g[2][2])
    )
    g_z = 2.0 * (
        x * (g[0][2] + g[2][0])
        + y * (g[1][2] + g[2][1])
        + w * (g[1][0] - g[0][1])
        - 2.0 * z * (g[0][0] + g[1][1])
    )
    along = w * g_w + x * g_x + y * g_y + z * g_z
    for p, (g_q, q) in enumerate(((g_w, w), (g_x, x), (g_y, y), (g_z, z))):
        grads[6 + p] = (g_q - q * along) * geo["norm"]
    x, y, z = geo["toward"]
    basis = harmonic_basis(x, y, z)
    h = [None]
    for k in range(16):
        if k:
            h.append(sum(drawn[c] * row(11 + 3 * k + c) for c in range(3)))
        for c in range(3):
            grads[11 + 3 * k + c] = basis[k] * drawn[c]
    a, d = sh_two, sh_three
    xx, yy, zz, xy, yz, xz = x * x, y * y, z * z, x * y, y * z, x * z
    g_dx = (
        -sh_one * h[3] + a[0] * y * h[4] - 2.0 * a[2] * x * h[6] + a[3] * z * h[7]
        + 2.0 * a[4] * x * h[8] + 6.0 * d[0] * xy * h[9] + d[1] * yz * h[10]
        - 2.0 * d[2] * xy * h[11] - 6.0 * d[3] * xz * h[12]
        + d[4] * (4.0 * zz - 3.0 * xx - yy) * h[13] + 2.0 * d[5] * xz * h[14]
        + 3.0 * d[6] * (xx - yy) * h[15]
    )
    g_dy = (
        -sh_one * h[1] + a[0] * x * h[4] + a[1] * z * h[5] - 2.0 * a[2] * y * h[6]
        - 2.0 * a[4] * y * h[8] + 3.0 * d[0] * (xx - yy) * h[9] + d[1] * xz * h[10]
        + d[2] * (4.0 * zz - xx - 3.0 * yy) * h[11] - 6.0 * d[3] * yz * h[12]
        - 2.0 * d[4] * xy * h[13] - 2.0 * d[5] * yz * h[14] - 6.0 * d[6] * xy * h[15]
    )
    g_dz = (
        sh_one * h[2] + a[1] * y * h[5] + 4.0 * a[2] * z * h[6] + a[3] * x * h[7]
        + d[1] * xy * h[10] + 8.0 * d[2] * yz * h[11]
        + 3.0 * d[3] * (2.0 * zz - xx - yy) * h[12] + 8.0 * d[4] * xz * h[13]
        + d[5] * (xx - yy) * h[14]
    )
    along = x * g_dx + y * g_dy + z * g_dz
    turned = [(gd - t * along) * geo["shrink"] for gd, t in ((g_dx, x), (g_dy, y), (g_dz, z))]
    for j in range(3):
        grads[j] = sum(rot[i][j] * g_view[i] for i in range(3)) + turned[j]
    for b in range(blocks):
        mine = place == b
        for p in range(params):
            grad[b, p : p + 1, :] = jnp.sum(
                jnp.where(mine, grads[p], 0.0), axis=0, keepdims=True
            )

    parts = []
    for b in range(blocks):
        new = base_ref[b] - steps_ref[...] * grad[b, :params, :]
        shifted = new + dual_ref[b]
        new_ref[b] = new
        shifted_ref[b] = shifted
        parts.append(shifted)
    shifted = jnp.concatenate(parts, axis=1)
    for n in range(pick_ref.shape[0]):
        value = exact_pick(shifted, pick_ref[n])
        for b in range(blocks):
            sent_ref[n, b] = value[:, b * LANES : (b + 1) * LANES]


def constants(pixels):
    place = np.arange(pixels)
    x = (place % LANES - 64).astype(np.float32)
    y = (place // LANES - 4).astype(np.float32)
    square = (x * x).astype(jnp.bfloat16).astype(np.float32)
    part = np.zeros((PART, pixels + 3 * LANES), np.float32)
    for c, value in enumerate([square, x * y, y * y, x, y, np.ones_like(x)]):
        part[c, :pixels] = value
    for c in range(3):
        part[6 + c, pixels + c * LANES : pixels + (c + 1) * LANES] = 1.0
    part[COEFS, :pixels] = x * x - square
    basis = np.concatenate([part] * 3)
    lane = np.arange(LANES)
    wide = LANES // SEGS
    xmom = np.zeros((3 * SEGS + SEGS, LANES), np.float32)
    for s in range(SEGS):
        near = (lane // wide == s).astype(np.float32)
        offset = lane - s * wide - wide // 2
        for power in range(3):
            xmom[power * SEGS + s] = near * offset**power
    order = np.zeros((LANES, LANES), np.float32)
    groups = LANES // SUB
    for r in range(LANES):
        order[(r % SUB) * groups + r // SUB, r] = 1.0
    return [jnp.asarray(value, jnp.bfloat16) for value in (basis, xmom, order, order.T)]


def vmem(number=1):
    return [pl.BlockSpec(memory_space=pltpu.VMEM)] * number


def smem(number=1):
    return [pl.BlockSpec(memory_space=pltpu.SMEM)] * number


def params_with(mib):
    return pltpu.CompilerParams(vmem_limit_bytes=mib * 2**20)


def on_device(
    gaussians, consensus, duals, step_sizes, cameras, camera_ids, block_lists, depth_order,
    block_counts, targets, intersection,
):
    own = gaussians[0]
    blocks, params = own.shape[0], own.shape[1]
    peers = lax.axis_size("tile")
    me = lax.axis_index("tile")[None]
    listed = block_lists.shape[2]
    pixels = targets.shape[3]
    yrows = pixels // LANES
    outer = peers // INNER
    f32 = jnp.float32
    shape_of = jax.ShapeDtypeStruct
    basis, xmom, order, back = constants(pixels)

    def swap(value, mask):
        return lax.ppermute(value, "tile", [(i, i ^ mask) for i in range(peers)])

    hop_bits = list(reversed(range(2, peers.bit_length() - 1)))
    ids = jnp.concatenate(
        [jnp.broadcast_to(camera_ids, (1, LANES)), block_lists[0]], axis=1
    )
    everything = own
    masks = [0]
    for step, bit in enumerate(hop_bits):
        arrived = swap(everything, 1 << bit)
        if step < 2:
            ids = jnp.concatenate([ids, swap(ids, 1 << step)], 0)
        everything = jnp.concatenate([everything, arrived], 0)
        masks += [mask | (1 << bit) for mask in masks]

    group_total = lax.axis_size("scene")
    group = lax.axis_index("scene")[None]
    share = intersection[0, 0]
    if group_total == 2:
        routes = [[(0, 1), (1, 0)]]
        links = [(lambda g: g == 0, lambda g: g >= 0)]
    else:
        routes = [
            [(g + 1, g) for g in range(group_total - 1)],
            [(g, g + 1) for g in range(group_total - 1)],
        ]
        links = [
            (lambda g: g >= 0, lambda g: g < group_total - 1),
            (lambda g: g < 0, lambda g: g > 0),
        ]
    lists = [lax.ppermute(share, "scene", route) for route in routes]

    base, steps, pick, mask = pl.pallas_call(
        functools.partial(prepare_kernel, links),
        out_shape=(
            shape_of(own.shape, f32),
            shape_of((params, LANES), f32),
            shape_of((len(links), blocks * LANES, blocks * LANES), jnp.bfloat16),
            shape_of((len(links), blocks, SUB, LANES), f32),
        ),
        in_specs=smem() + vmem(5 + len(links)),
        out_specs=tuple(vmem(4)),
        name="prepare",
    )(group, own, consensus[0], duals[0], step_sizes[None, :], share, *lists)

    messages = pl.pallas_call(
        functools.partial(project_kernel, masks, yrows),
        out_shape=tuple([shape_of((COEFS * outer, LANES), f32)] * INNER),
        in_specs=smem() + vmem(4),
        out_specs=tuple(vmem(INNER)),
        scratch_shapes=[pltpu.VMEM((COEFS * outer * INNER, LANES), f32)],
        name="project",
    )(me, everything, ids, cameras, order)
    sources = [messages[0]] + [swap(messages[j], j) for j in range(1, INNER)]

    outbox = pl.pallas_call(
        functools.partial(render_kernel, pixels, blocks, hop_bits),
        out_shape=shape_of((peers, MSG, LANES), f32),
        in_specs=smem(6) + vmem(INNER + 4),
        out_specs=vmem()[0],
        scratch_shapes=[
            pltpu.VMEM((COEFS * peers, LANES), f32),
            pltpu.VMEM((listed * KDIM, LANES), f32),
            pltpu.VMEM((LANES, pixels + 3 * LANES), f32),
            pltpu.VMEM((listed * LANES, 3 * LANES), f32),
            pltpu.VMEM((listed * LANES, pixels), f32),
            pltpu.VMEM((listed * LANES, pixels), f32),
            pltpu.VMEM((yrows, SUB, LANES), f32),
            pltpu.VMEM((listed, yrows, SUB, LANES), f32),
            pltpu.VMEM((listed, yrows, SUB, LANES), f32),
            pltpu.VMEM((listed, 3, yrows, SUB, LANES), f32),
            pltpu.VMEM((3, yrows, SUB, LANES), f32),
            pltpu.VMEM((yrows, SUB, LANES), f32),
            pltpu.VMEM((MOMENTS * LANES, LANES), f32),
            pltpu.VMEM((listed, 4 * SEGS, MOMENTS * LANES), f32),
            pltpu.VMEM((listed * MSG, LANES), f32),
            pltpu.SMEM((listed,), jnp.int32),
        ],
        compiler_params=params_with(48),
        name="render",
    )(
        me, camera_ids[0], block_counts[0], block_lists[0, 0], depth_order[0, 0], cameras,
        *sources, targets[0, 0], basis, xmom, back,
    )
    inbox = lax.all_to_all(outbox, "tile", split_axis=0, concat_axis=0, tiled=True)
    updated, shifted, sent = pl.pallas_call(
        owner_kernel,
        out_shape=(
            shape_of(own.shape, f32),
            shape_of(own.shape, f32),
            shape_of((len(links),) + own.shape, f32),
        ),
        in_specs=vmem(6),
        out_specs=tuple(vmem(3)),
        scratch_shapes=[pltpu.VMEM((blocks, params + 5, LANES), f32)],
        name="owner",
    )(inbox.reshape(peers * MSG, LANES), own, base, duals[0], steps, pick)
    new_duals = jnp.zeros_like(shifted)
    for n, route in enumerate(routes):
        theirs = lax.ppermute(sent[n], "scene", route)
        change = shifted - 0.5 * (shifted + theirs)
        new_duals = jnp.where(mask[n, :, :1, :] > 0.5, change, new_duals)
    return updated[None], new_duals[None]


def solution(mesh):
    placed = (
        P("scene", "tile", None, None),
        P("scene", "tile", None, None),
        P("scene", "tile", None, None),
        P(),
        P(),
        P("scene", "tile"),
        P("scene", "tile", None),
        P("scene", "tile", None),
        P("scene", "tile"),
        P("scene", "tile", None, None),
        P("scene", "tile", None, None),
    )
    return jax.shard_map(
        on_device,
        mesh=mesh,
        in_specs=placed,
        out_specs=(P("scene", "tile", None, None), P("scene", "tile", None, None)),
        check_vma=False,
    )
```

```python
import functools

import jax
import jax.numpy as jnp
import numpy as np
from jax import lax
from jax.experimental import pallas as pl
from jax.experimental.pallas import tpu as pltpu
from jax.sharding import PartitionSpec as P

penalty_weight = 0.5
blur_floor = 0.3
alpha_ceiling = 0.99
log2e = 1.4426950408889634
sh_zero = 0.28209479177387814
sh_one = 0.4886025119029199
sh_two = (
    1.0925484305920792,
    -1.0925484305920792,
    0.31539156525252005,
    -1.0925484305920792,
    0.5462742152960396,
)
sh_three = (
    -0.5900435899266435,
    2.890611442640554,
    -0.4570457994644658,
    0.3731763325901154,
    -0.4570457994644658,
    1.445305721320277,
    -0.5900435899266435,
)

LANES = 128
SUB = 8
PART = 16
KDIM = 3 * PART
COEFS = 9
INNER = 4
SEGS = 8
MOMENTS = 6
MSG = 16
highest = lax.Precision.HIGHEST


def harmonic_basis(x, y, z):
    xx, yy, zz = x * x, y * y, z * z
    return [
        sh_zero + 0.0 * x,
        -sh_one * y,
        sh_one * z,
        -sh_one * x,
        sh_two[0] * x * y,
        sh_two[1] * y * z,
        sh_two[2] * (2.0 * zz - xx - yy),
        sh_two[3] * x * z,
        sh_two[4] * (xx - yy),
        sh_three[0] * y * (3.0 * xx - yy),
        sh_three[1] * x * y * z,
        sh_three[2] * y * (4.0 * zz - xx - yy),
        sh_three[3] * z * (2.0 * zz - 3.0 * xx - 3.0 * yy),
        sh_three[4] * x * (4.0 * zz - xx - yy),
        sh_three[5] * z * (xx - yy),
        sh_three[6] * x * (xx - 3.0 * yy),
    ]


def geometry(row, cam):
    mean = [row(0), row(1), row(2)]
    rot = [[cam[3 * i + j] for j in range(3)] for i in range(3)]
    shift = [cam[9 + i] for i in range(3)]
    focal_x, focal_y = cam[12], cam[13]
    view = [
        rot[i][0] * mean[0] + rot[i][1] * mean[1] + rot[i][2] * mean[2] + shift[i] for i in range(3)
    ]
    inverse = 1.0 / view[2]
    u = view[0] * inverse
    v = view[1] * inverse
    quat = [row(6 + i) for i in range(4)]
    norm = lax.rsqrt(sum(q * q for q in quat))
    w, x, y, z = [q * norm for q in quat]
    turn = [
        [1.0 - 2.0 * (y * y + z * z), 2.0 * (x * y - w * z), 2.0 * (x * z + w * y)],
        [2.0 * (x * y + w * z), 1.0 - 2.0 * (x * x + z * z), 2.0 * (y * z - w * x)],
        [2.0 * (x * z - w * y), 2.0 * (y * z + w * x), 1.0 - 2.0 * (x * x + y * y)],
    ]
    scales = [jnp.exp(row(3 + k)) for k in range(3)]
    spread = [[turn[j][k] * scales[k] for k in range(3)] for j in range(3)]
    axes = [
        [sum(rot[i][j] * spread[j][k] for j in range(3)) for k in range(3)] for i in range(3)
    ]
    scale_x = focal_x * inverse
    scale_y = focal_y * inverse
    lean_x = [axes[0][k] - u * axes[2][k] for k in range(3)]
    lean_y = [axes[1][k] - v * axes[2][k] for k in range(3)]
    row_one = [scale_x * lean_x[k] for k in range(3)]
    row_two = [scale_y * lean_y[k] for k in range(3)]
    cov_xx = sum(a * a for a in row_one) + blur_floor
    cov_xy = sum(a * b for a, b in zip(row_one, row_two))
    cov_yy = sum(b * b for b in row_two) + blur_floor
    scale = 1.0 / (cov_xx * cov_yy - cov_xy * cov_xy)
    conic = (cov_yy * scale, -cov_xy * scale, cov_xx * scale)
    eye = [-(rot[0][i] * shift[0] + rot[1][i] * shift[1] + rot[2][i] * shift[2]) for i in range(3)]
    away = [mean[i] - eye[i] for i in range(3)]
    shrink = lax.rsqrt(sum(a * a for a in away))
    toward = [a * shrink for a in away]
    return dict(
        rot=rot,
        view=view,
        inverse=inverse,
        u=u,
        v=v,
        norm=norm,
        unit=(w, x, y, z),
        scales=scales,
        spread=spread,
        axes=axes,
        scale_x=scale_x,
        scale_y=scale_y,
        lean_x=lean_x,
        lean_y=lean_y,
        row_one=row_one,
        row_two=row_two,
        conic=conic,
        shrink=shrink,
        toward=toward,
    )


def three_parts(value):
    high = value.astype(jnp.bfloat16).astype(jnp.float32)
    rest = value - high
    mid = rest.astype(jnp.bfloat16).astype(jnp.float32)
    return high, mid, rest - mid


def exact_pick(value, pick):
    high, mid, low = [part.astype(jnp.bfloat16) for part in three_parts(value)]
    dot = functools.partial(jnp.dot, preferred_element_type=jnp.float32)
    return (dot(high, pick) + dot(mid, pick)) + dot(low, pick)


def sub_roll(value, shift):
    return pltpu.roll(value, shift % SUB, 0)


def prepare_kernel(
    links, group_ref, own_ref, cons_ref, dual_ref, step_ref, share_ref, *refs
):
    others, (base_ref, steps_ref, pick_ref, mask_ref) = refs[: len(links)], refs[len(links) :]
    params, blocks = own_ref.shape[0], own_ref.shape[1]
    group = group_ref[0]
    for p in range(params):
        step = step_ref[p]
        here = own_ref[p]
        steps_ref[p] = jnp.full((blocks, LANES), step)
        base_ref[p] = here - step * (penalty_weight * (here - cons_ref[p] + dual_ref[p]))
    half = share_ref.shape[1]
    local = lax.broadcasted_iota(jnp.int32, (blocks * LANES, half), 0)
    contract = (((1,), (1,)), ((), ()))
    for n, (side_of, exists_of) in enumerate(links):
        other = others[n]
        up = side_of(group)
        mine = jnp.where(up, share_ref[0:1, :], share_ref[1:2, :])
        theirs = jnp.where(up, other[1:2, :], other[0:1, :])
        source = (local == mine).astype(jnp.bfloat16)
        target = (local == theirs).astype(jnp.bfloat16)
        pick_ref[n] = lax.dot_general(
            source, target, contract, preferred_element_type=jnp.float32
        ).astype(jnp.bfloat16)
        there = jnp.full((SUB, half), jnp.where(exists_of(group), 1.0, 0.0)).astype(jnp.bfloat16)
        mask = lax.dot_general(there, source, contract, preferred_element_type=jnp.float32)
        for b in range(blocks):
            mask_ref[n, b : b + 1, :] = mask[0:1, b * LANES : (b + 1) * LANES]


def project_kernel(masks, yrows, me_ref, raw_ref, ids_ref, cameras_ref, order_ref, *refs):
    outs, feat = refs[:INNER], refs[INNER]
    outer = len(masks)
    blocks = raw_ref.shape[2]
    me = me_ref[0]
    ids = jnp.concatenate([ids_ref[...]] * (SUB // INNER), axis=0)
    lane = lax.broadcasted_iota(jnp.int32, (SUB, LANES), 1)
    sub = lax.broadcasted_iota(jnp.int32, (SUB, LANES), 0)
    ncam = cameras_ref.shape[0]
    chosen = lax.broadcasted_iota(jnp.int32, (SUB, ncam), 1) == ids[:, 0:1]
    shots = jnp.dot(chosen.astype(jnp.float32), cameras_ref[...], precision=highest)
    cam = [jnp.broadcast_to(shots[:, k : k + 1], (SUB, LANES)) for k in range(16)]
    top = (((me & 3) ^ (sub & 3)) * yrows).astype(jnp.float32)
    lists = ids[:, LANES:]
    rows = outer * INNER
    for v in range(rows // SUB):
        owners = [2 * v, 2 * v + 1]
        first = jnp.where(sub < INNER, (me ^ masks[owners[0]]) * blocks, (me ^ masks[owners[1]]) * blocks)
        found = []
        for b in range(1, blocks):
            same = (lists == first[:, : lists.shape[1]] + b).astype(jnp.float32)
            found.append(jnp.broadcast_to(jnp.max(same, axis=1, keepdims=True), (SUB, LANES)) > 0.5)

        def row(p):
            def of(b):
                return jnp.where(
                    sub < INNER,
                    jnp.broadcast_to(raw_ref[owners[0], p, b : b + 1, :], (SUB, LANES)),
                    jnp.broadcast_to(raw_ref[owners[1], p, b : b + 1, :], (SUB, LANES)),
                )

            value = of(0)
            for b in range(1, blocks):
                value = jnp.where(found[b - 1], of(b), value)
            return value

        geo = geometry(row, cam)
        sx = cam[12] * geo["u"] + (cam[14] - 64.0)
        sy = cam[13] * geo["v"] + (cam[15] - top - 4.0)
        basis = harmonic_basis(*geo["toward"])
        tint = [sum(basis[k] * row(11 + 3 * k + c) for k in range(16)) + 0.5 for c in range(3)]
        lo = -jnp.log(1.0 + jnp.exp(-row(10))) * log2e
        ca, cb, cc = geo["conic"]
        kxx = (-0.5 * log2e) * ca
        kxy = -log2e * cb
        kyy = (-0.5 * log2e) * cc
        kx = -2.0 * kxx * sx - kxy * sy
        ky = -2.0 * kyy * sy - kxy * sx
        k1 = kxx * sx * sx + kxy * sx * sy + kyy * sy * sy + lo
        for m, value in enumerate([kxx, kxy, kyy, kx, ky, k1, *tint]):
            feat[m * rows + v * SUB : m * rows + (v + 1) * SUB, :] = value
    feat[...] = exact_pick(feat[...], order_ref[...])
    for j in range(INNER):
        outs[j][...] = feat[pl.ds(j, COEFS * outer, stride=INNER), :]


def render_kernel(
    pixels, blocks, hop_bits, me_ref, cam_id_ref, count_ref, list_ref, depth_ref, cameras_ref,
    src0, src1, src2, src3, target_ref, basis_ref, xmom_ref, back_ref, out_ref,
    raw, coef, expo, shade, alphas, weights, carry, before, passed, colours,
    resid, behind, sums, found, rows, slots,
):
    listed = list_ref.shape[0]
    peers = out_ref.shape[0]
    outer = peers // INNER
    per_owner = blocks
    yrows = pixels // LANES
    groups = LANES // SUB
    me = me_ref[0]
    count = count_ref[0]
    cam_id = cam_id_ref[0]
    top = ((me % 4) * yrows).astype(jnp.float32)

    def place_slot(j, ends):
        live_end, dead_end = ends
        slot = depth_ref[j]
        live = slot < count
        slots[jnp.where(live, live_end, dead_end)] = slot
        return jnp.where(live, live_end + 1, live_end), jnp.where(live, dead_end, dead_end + 1)

    lax.fori_loop(0, listed, place_slot, (jnp.int32(0), count))

    for j, src in enumerate((src0, src1, src2, src3)):
        raw[j * COEFS * outer : (j + 1) * COEFS * outer, :] = src[...]
    coef[...] = jnp.zeros(coef.shape, jnp.float32)

    def fetch(k, _):
        apart = me ^ (list_ref[slots[k]] // per_owner)
        near = sum((((apart >> bit) & 1) << t) for t, bit in enumerate(hop_bits))
        start = (apart & (INNER - 1)) * (COEFS * outer) + near
        value = raw[pl.ds(start, COEFS, stride=outer), :]
        for part, piece in enumerate(three_parts(value)):
            base = pl.multiple_of(k * KDIM + part * PART, PART)
            coef[pl.ds(base, COEFS), :] = piece
            coef[pl.ds(base + COEFS, 1), :] = piece[0:1, :]
        return 0

    lax.fori_loop(0, count, fetch, 0)

    sub = lax.broadcasted_iota(jnp.int32, (SUB, LANES), 0)
    one = jnp.ones((SUB, LANES), jnp.float32)
    none = jnp.zeros((SUB, LANES), jnp.float32)
    for y in range(yrows):
        carry[y] = one
    for c in range(3):
        for y in range(yrows):
            resid[c, y] = none

    def spread_row(value, index):
        return jnp.broadcast_to(value[index : index + 1, :], (SUB, LANES))

    def forward(k, _):
        mine = coef[pl.ds(pl.multiple_of(k * KDIM, PART), KDIM), :].astype(jnp.bfloat16)
        expo[...] = lax.dot_general(
            mine, basis_ref[...], (((0,), (0,)), ((), ())), preferred_element_type=jnp.float32
        )
        base = pl.multiple_of(k * LANES, LANES)
        shade[pl.ds(base, LANES), :] = expo[:, pixels:]
        kept = [one] * yrows
        total = [[none] * yrows for _ in range(3)]
        for i in range(groups):
            here = pl.ds(pl.multiple_of(base + i * SUB, SUB), SUB)
            tints = [
                expo[i * SUB : (i + 1) * SUB, pixels + c * LANES : pixels + (c + 1) * LANES]
                for c in range(3)
            ]
            for y in range(yrows):
                lanes = slice(y * LANES, (y + 1) * LANES)
                alpha = jnp.minimum(
                    alpha_ceiling, jnp.exp2(expo[i * SUB : (i + 1) * SUB, lanes])
                )
                weight = alpha * kept[y]
                alphas[here, lanes] = alpha
                weights[here, lanes] = weight
                kept[y] = kept[y] - weight
                for c in range(3):
                    total[c][y] = total[c][y] + weight * tints[c]
        for y in range(yrows):
            passed[k, y] = kept[y]
            through = kept[y]
            for step in (1, 2, 4):
                through = through * jnp.where(sub >= step, sub_roll(through, step), 1.0)
            entering = carry[y]
            ahead = entering * jnp.where(sub >= 1, sub_roll(through, 1), 1.0)
            before[k, y] = ahead
            carry[y] = entering * spread_row(through, SUB - 1)
            for c in range(3):
                colours[k, c, y] = total[c][y]
                resid[c, y] = resid[c, y] + ahead * total[c][y]
        return 0

    lax.fori_loop(0, count, forward, 0)

    for y in range(yrows):
        for c in range(3):
            value = jnp.sum(resid[c, y], axis=0, keepdims=True)
            value = value - target_ref[c : c + 1, y * LANES : (y + 1) * LANES]
            resid[c, y] = jnp.broadcast_to(value, (SUB, LANES))
        behind[y] = none

    def backward(back, _):
        k = count - 1 - back
        base = pl.multiple_of(k * LANES, LANES)
        pull = [[None] * yrows for _ in range(3)]
        rear = [None] * yrows
        for y in range(yrows):
            res = [resid[c, y] for c in range(3)]
            gain = passed[k, y]
            value = sum(colours[k, c, y] * res[c] for c in range(3))
            for step in (1, 2, 4):
                inside = sub < SUB - step
                value = value + gain * jnp.where(inside, sub_roll(value, -step), 0.0)
                gain = gain * jnp.where(inside, sub_roll(gain, -step), 1.0)
            last = behind[y]
            ahead = before[k, y]
            at_end = jnp.where(
                sub < SUB - 1, sub_roll(value, -1) + sub_roll(gain, -1) * last, last
            )
            behind[y] = spread_row(value + gain * last, 0)
            rear[y] = ahead * at_end
            for c in range(3):
                pull[c][y] = ahead * res[c]
        for i in reversed(range(groups)):
            here = pl.ds(pl.multiple_of(base + i * SUB, SUB), SUB)
            tints = [shade[here, c * LANES : (c + 1) * LANES] for c in range(3)]
            run = [none, none, none]
            drawn = [none, none, none]
            for y in range(yrows):
                lanes = slice(y * LANES, (y + 1) * LANES)
                alpha = alphas[here, lanes]
                weight = weights[here, lanes]
                gap = (
                    tints[0] * pull[0][y] + tints[1] * pull[1][y] + tints[2] * pull[2][y] - rear[y]
                )
                slope = jnp.where(alpha < alpha_ceiling, weight * gap, 0.0)
                rear[y] = rear[y] + alpha * gap
                run[0] = run[0] + slope
                run[1] = run[1] + run[0]
                run[2] = run[2] + run[1]
                for c in range(3):
                    drawn[c] = drawn[c] + weight * pull[c][y]
            for m, value in enumerate(run + drawn):
                sums[m * LANES + i * SUB : m * LANES + (i + 1) * SUB, :] = value
        value = sums[...]
        high = value.astype(jnp.bfloat16)
        low = (value - high.astype(jnp.float32)).astype(jnp.bfloat16)
        contract = (((1,), (1,)), ((), ()))
        xmom = xmom_ref[...]
        found[k] = lax.dot_general(
            xmom, high, contract, preferred_element_type=jnp.float32
        ) + lax.dot_general(xmom, low, contract, preferred_element_type=jnp.float32)
        return 0

    lax.fori_loop(0, count, backward, 0)

    lane = lax.broadcasted_iota(jnp.int32, (1, LANES), 1)
    middle = (
        lax.broadcasted_iota(jnp.int32, (SUB, LANES), 0) * (LANES // SEGS)
        + (LANES // SEGS // 2 - 64)
    ).astype(jnp.float32)
    meta = jnp.where(lane == 17, top, 0.0)
    for c in range(16):
        meta = jnp.where(lane == c, cameras_ref[cam_id, c], meta)

    rows[...] = jnp.zeros(rows.shape, jnp.float32)

    def gather_moments(k, _):
        part = lambda order, m: found[k, order * SEGS : (order + 1) * SEGS, m * LANES : (m + 1) * LANES]
        add = lambda value: jnp.sum(value, axis=0, keepdims=True)
        rise = yrows - 4.0
        h0, h1, h2 = part(0, 0), part(1, 0), part(2, 0)
        n0, n1 = part(0, 1), part(1, 1)
        s0 = add(h0)
        x1 = add(h1 + middle * h0)
        x2 = add(h2 + middle * (2.0 * h1 + middle * h0))
        t1 = add(n0)
        tx = add(n1 + middle * n0)
        t2 = 2.0 * add(part(0, 2)) - t1
        answer = [s0, x1, rise * s0 - t1, x2, rise * x1 - tx, rise * (rise * s0 - 2.0 * t1) + t2]
        answer += [add(part(0, 3 + c)) for c in range(3)]
        for m, value in enumerate(answer):
            rows[pl.ds(k * MSG + m, 1), :] = value
        return 0

    lax.fori_loop(0, count, gather_moments, 0)
    rows[...] = exact_pick(rows[...], back_ref[...])

    if peers > listed:
        absent = jnp.where(lane == 16, -1.0, 0.0)
        for peer in range(peers):
            out_ref[peer] = jnp.broadcast_to(absent, (MSG, LANES))

    def send(k, _):
        block = list_ref[slots[k]]
        owner = block // per_owner
        place = (block % per_owner).astype(jnp.float32)
        rows[pl.ds(k * MSG + 9, 1), :] = jnp.where(lane == 16, place, meta)
        out_ref[owner] = rows[pl.ds(pl.multiple_of(k * MSG, MSG), MSG), :]
        return 0

    lax.fori_loop(0, listed, send, 0)


def owner_kernel(
    inbox_ref, own_ref, base_ref, dual_ref, steps_ref, pick_ref, new_ref, shifted_ref, sent_ref,
    grad, moved
):
    params, blocks = own_ref.shape[0], own_ref.shape[1]
    strips = inbox_ref.shape[0] // MSG

    def message(m):
        return inbox_ref[pl.ds(m, strips, stride=MSG), :]

    meta = message(9)
    cam = [jnp.broadcast_to(meta[:, k : k + 1], (strips, LANES)) for k in range(18)]
    place, top = cam[16], cam[17]

    def row(p):
        value = jnp.broadcast_to(own_ref[p, 0:1, :], (strips, LANES))
        for b in range(1, blocks):
            value = jnp.where(place == b, own_ref[p, b : b + 1, :], value)
        return value

    geo = geometry(row, cam)
    u, v, inverse = geo["u"], geo["v"], geo["inverse"]
    focal_x, focal_y = cam[12], cam[13]
    at_x = focal_x * u + (cam[14] - 64.0)
    at_y = focal_y * v + (cam[15] - top - 4.0)
    s0, x1, y1, x2, xy, y2, *drawn = [message(m) for m in range(9)]
    sx = x1 - at_x * s0
    sy = y1 - at_y * s0
    sxx = x2 - at_x * (x1 + sx)
    sxy = xy - at_x * y1 - at_y * sx
    syy = y2 - at_y * (y1 + sy)
    ca, cb, cc = geo["conic"]
    axes, rot = geo["axes"], geo["rot"]
    grads = {}
    opacity = 1.0 / (1.0 + jnp.exp(-row(10)))
    grads[10] = s0 * (1.0 - opacity)
    t00, t01 = sxx * ca + sxy * cb, sxx * cb + sxy * cc
    t10, t11 = sxy * ca + syy * cb, sxy * cb + syy * cc
    g_xx = 0.5 * (ca * t00 + cb * t10)
    g_xy = ca * t01 + cb * t11
    g_yy = 0.5 * (cb * t01 + cc * t11)
    one, two = geo["row_one"], geo["row_two"]
    g_one = [2.0 * g_xx * one[k] + g_xy * two[k] for k in range(3)]
    g_two = [2.0 * g_yy * two[k] + g_xy * one[k] for k in range(3)]
    px, py = geo["scale_x"], geo["scale_y"]
    g_axes = [
        [px * g_one[k] for k in range(3)],
        [py * g_two[k] for k in range(3)],
        [-(px * u * g_one[k] + py * v * g_two[k]) for k in range(3)],
    ]
    g_px = sum(g_one[k] * geo["lean_x"][k] for k in range(3))
    g_py = sum(g_two[k] * geo["lean_y"][k] for k in range(3))
    g_u = focal_x * (ca * sx + cb * sy) - px * sum(g_one[k] * axes[2][k] for k in range(3))
    g_v = focal_y * (cc * sy + cb * sx) - py * sum(g_two[k] * axes[2][k] for k in range(3))
    view = geo["view"]
    g_inverse = focal_x * g_px + focal_y * g_py + view[0] * g_u + view[1] * g_v
    g_view = [inverse * g_u, inverse * g_v, -inverse * inverse * g_inverse]
    g_spread = [
        [sum(rot[i][j] * g_axes[i][k] for i in range(3)) for k in range(3)] for j in range(3)
    ]
    for k in range(3):
        grads[3 + k] = sum(g_spread[j][k] * geo["spread"][j][k] for j in range(3))
    g = [[g_spread[j][k] * geo["scales"][k] for k in range(3)] for j in range(3)]
    w, x, y, z = geo["unit"]
    g_w = 2.0 * (z * (g[1][0] - g[0][1]) + y * (g[0][2] - g[2][0]) + x * (g[2][1] - g[1][2]))
    g_x = 2.0 * (
        y * (g[0][1] + g[1][0])
        + z * (g[0][2] + g[2][0])
        + w * (g[2][1] - g[1][2])
        - 2.0 * x * (g[1][1] + g[2][2])
    )
    g_y = 2.0 * (
        x * (g[0][1] + g[1][0])
        + z * (g[1][2] + g[2][1])
        + w * (g[0][2] - g[2][0])
        - 2.0 * y * (g[0][0] + g[2][2])
    )
    g_z = 2.0 * (
        x * (g[0][2] + g[2][0])
        + y * (g[1][2] + g[2][1])
        + w * (g[1][0] - g[0][1])
        - 2.0 * z * (g[0][0] + g[1][1])
    )
    along = w * g_w + x * g_x + y * g_y + z * g_z
    for p, (g_q, q) in enumerate(((g_w, w), (g_x, x), (g_y, y), (g_z, z))):
        grads[6 + p] = (g_q - q * along) * geo["norm"]
    x, y, z = geo["toward"]
    basis = harmonic_basis(x, y, z)
    h = [None]
    for k in range(16):
        if k:
            h.append(sum(drawn[c] * row(11 + 3 * k + c) for c in range(3)))
        for c in range(3):
            grads[11 + 3 * k + c] = basis[k] * drawn[c]
    a, d = sh_two, sh_three
    xx, yy, zz, xy, yz, xz = x * x, y * y, z * z, x * y, y * z, x * z
    g_dx = (
        -sh_one * h[3] + a[0] * y * h[4] - 2.0 * a[2] * x * h[6] + a[3] * z * h[7]
        + 2.0 * a[4] * x * h[8] + 6.0 * d[0] * xy * h[9] + d[1] * yz * h[10]
        - 2.0 * d[2] * xy * h[11] - 6.0 * d[3] * xz * h[12]
        + d[4] * (4.0 * zz - 3.0 * xx - yy) * h[13] + 2.0 * d[5] * xz * h[14]
        + 3.0 * d[6] * (xx - yy) * h[15]
    )
    g_dy = (
        -sh_one * h[1] + a[0] * x * h[4] + a[1] * z * h[5] - 2.0 * a[2] * y * h[6]
        - 2.0 * a[4] * y * h[8] + 3.0 * d[0] * (xx - yy) * h[9] + d[1] * xz * h[10]
        + d[2] * (4.0 * zz - xx - 3.0 * yy) * h[11] - 6.0 * d[3] * yz * h[12]
        - 2.0 * d[4] * xy * h[13] - 2.0 * d[5] * yz * h[14] - 6.0 * d[6] * xy * h[15]
    )
    g_dz = (
        sh_one * h[2] + a[1] * y * h[5] + 4.0 * a[2] * z * h[6] + a[3] * x * h[7]
        + d[1] * xy * h[10] + 8.0 * d[2] * yz * h[11]
        + 3.0 * d[3] * (2.0 * zz - xx - yy) * h[12] + 8.0 * d[4] * xz * h[13]
        + d[5] * (xx - yy) * h[14]
    )
    along = x * g_dx + y * g_dy + z * g_dz
    turned = [(gd - t * along) * geo["shrink"] for gd, t in ((g_dx, x), (g_dy, y), (g_dz, z))]
    for j in range(3):
        grads[j] = sum(rot[i][j] * g_view[i] for i in range(3)) + turned[j]
    for b in range(blocks):
        mine = place == b
        for p in range(params):
            grad[p * blocks + b : p * blocks + b + 1, :] = jnp.sum(
                jnp.where(mine, grads[p], 0.0), axis=0, keepdims=True
            )

    for p in range(params):
        here = slice(p * blocks, (p + 1) * blocks)
        new = base_ref[p] - steps_ref[p] * grad[here, :]
        shifted = new + dual_ref[p]
        new_ref[p] = new
        shifted_ref[p] = shifted
        moved[here, :] = shifted
    shifted = jnp.concatenate(
        [moved[pl.ds(b, params, stride=blocks), :] for b in range(blocks)], axis=1
    )
    for n in range(pick_ref.shape[0]):
        value = exact_pick(shifted, pick_ref[n])
        for b in range(blocks):
            moved[pl.ds(b, params, stride=blocks), :] = value[:, b * LANES : (b + 1) * LANES]
        for p in range(params):
            sent_ref[n, p] = moved[p * blocks : (p + 1) * blocks, :]


def constants(pixels):
    place = np.arange(pixels)
    x = (place % LANES - 64).astype(np.float32)
    y = (place // LANES - 4).astype(np.float32)
    square = (x * x).astype(jnp.bfloat16).astype(np.float32)
    part = np.zeros((PART, pixels + 3 * LANES), np.float32)
    for c, value in enumerate([square, x * y, y * y, x, y, np.ones_like(x)]):
        part[c, :pixels] = value
    for c in range(3):
        part[6 + c, pixels + c * LANES : pixels + (c + 1) * LANES] = 1.0
    part[COEFS, :pixels] = x * x - square
    basis = np.concatenate([part] * 3)
    lane = np.arange(LANES)
    wide = LANES // SEGS
    xmom = np.zeros((3 * SEGS + SEGS, LANES), np.float32)
    for s in range(SEGS):
        near = (lane // wide == s).astype(np.float32)
        offset = lane - s * wide - wide // 2
        for power in range(3):
            xmom[power * SEGS + s] = near * offset**power
    order = np.zeros((LANES, LANES), np.float32)
    groups = LANES // SUB
    for r in range(LANES):
        order[(r % SUB) * groups + r // SUB, r] = 1.0
    return [jnp.asarray(value, jnp.bfloat16) for value in (basis, xmom, order, order.T)]


def vmem(number=1):
    return [pl.BlockSpec(memory_space=pltpu.VMEM)] * number


def smem(number=1):
    return [pl.BlockSpec(memory_space=pltpu.SMEM)] * number


def params_with(mib):
    return pltpu.CompilerParams(vmem_limit_bytes=mib * 2**20)


def on_device(
    gaussians, consensus, duals, step_sizes, cameras, camera_ids, block_lists, depth_order,
    block_counts, targets, intersection,
):
    own, prior, dual = [value[0].swapaxes(0, 1) for value in (gaussians, consensus, duals)]
    params, blocks = own.shape[0], own.shape[1]
    peers = lax.axis_size("tile")
    me = lax.axis_index("tile")[None]
    listed = block_lists.shape[2]
    pixels = targets.shape[3]
    yrows = pixels // LANES
    outer = peers // INNER
    f32 = jnp.float32
    shape_of = jax.ShapeDtypeStruct
    basis, xmom, order, back = constants(pixels)

    def swap(value, mask):
        return lax.ppermute(value, "tile", [(i, i ^ mask) for i in range(peers)])

    hop_bits = list(reversed(range(2, peers.bit_length() - 1)))
    ids = jnp.concatenate(
        [jnp.broadcast_to(camera_ids, (1, LANES)), block_lists[0]], axis=1
    )
    everything = own[None]
    masks = [0]
    for step, bit in enumerate(hop_bits):
        arrived = swap(everything, 1 << bit)
        if step < 2:
            ids = jnp.concatenate([ids, swap(ids, 1 << step)], 0)
        everything = jnp.concatenate([everything, arrived], 0)
        masks += [mask | (1 << bit) for mask in masks]

    group_total = lax.axis_size("scene")
    group = lax.axis_index("scene")[None]
    share = intersection[0, 0]
    if group_total == 2:
        routes = [[(0, 1), (1, 0)]]
        links = [(lambda g: g == 0, lambda g: g >= 0)]
    else:
        routes = [
            [(g + 1, g) for g in range(group_total - 1)],
            [(g, g + 1) for g in range(group_total - 1)],
        ]
        links = [
            (lambda g: g >= 0, lambda g: g < group_total - 1),
            (lambda g: g < 0, lambda g: g > 0),
        ]
    lists = [lax.ppermute(share, "scene", route) for route in routes]

    base, steps, pick, mask = pl.pallas_call(
        functools.partial(prepare_kernel, links),
        out_shape=(
            shape_of(own.shape, f32),
            shape_of(own.shape, f32),
            shape_of((len(links), blocks * LANES, blocks * LANES), jnp.bfloat16),
            shape_of((len(links), blocks, LANES), f32),
        ),
        in_specs=smem() + vmem(3) + smem() + vmem(1 + len(links)),
        out_specs=tuple(vmem(4)),
        compiler_params=params_with(8),
        name="prepare",
    )(group, own, prior, dual, step_sizes, share, *lists)

    messages = pl.pallas_call(
        functools.partial(project_kernel, masks, yrows),
        out_shape=tuple([shape_of((COEFS * outer, LANES), f32)] * INNER),
        in_specs=smem() + vmem(4),
        out_specs=tuple(vmem(INNER)),
        scratch_shapes=[pltpu.VMEM((COEFS * outer * INNER, LANES), f32)],
        compiler_params=params_with(8),
        name="project",
    )(me, everything, ids, cameras, order)
    sources = [messages[0]] + [swap(messages[j], j) for j in range(1, INNER)]

    outbox = pl.pallas_call(
        functools.partial(render_kernel, pixels, blocks, hop_bits),
        out_shape=shape_of((peers, MSG, LANES), f32),
        in_specs=smem(6) + vmem(INNER + 4),
        out_specs=vmem()[0],
        scratch_shapes=[
            pltpu.VMEM((COEFS * peers, LANES), f32),
            pltpu.VMEM((listed * KDIM, LANES), f32),
            pltpu.VMEM((LANES, pixels + 3 * LANES), f32),
            pltpu.VMEM((listed * LANES, 3 * LANES), f32),
            pltpu.VMEM((listed * LANES, pixels), f32),
            pltpu.VMEM((listed * LANES, pixels), f32),
            pltpu.VMEM((yrows, SUB, LANES), f32),
            pltpu.VMEM((listed, yrows, SUB, LANES), f32),
            pltpu.VMEM((listed, yrows, SUB, LANES), f32),
            pltpu.VMEM((listed, 3, yrows, SUB, LANES), f32),
            pltpu.VMEM((3, yrows, SUB, LANES), f32),
            pltpu.VMEM((yrows, SUB, LANES), f32),
            pltpu.VMEM((MOMENTS * LANES, LANES), f32),
            pltpu.VMEM((listed, 4 * SEGS, MOMENTS * LANES), f32),
            pltpu.VMEM((listed * MSG, LANES), f32),
            pltpu.SMEM((listed,), jnp.int32),
        ],
        compiler_params=params_with(48),
        name="render",
    )(
        me, camera_ids[0], block_counts[0], block_lists[0, 0], depth_order[0, 0], cameras,
        *sources, targets[0, 0], basis, xmom, back,
    )
    inbox = lax.all_to_all(outbox, "tile", split_axis=0, concat_axis=0, tiled=True)
    updated, shifted, sent = pl.pallas_call(
        owner_kernel,
        out_shape=(
            shape_of(own.shape, f32),
            shape_of(own.shape, f32),
            shape_of((len(links),) + own.shape, f32),
        ),
        in_specs=vmem(6),
        out_specs=tuple(vmem(3)),
        scratch_shapes=[pltpu.VMEM((params * blocks, LANES), f32)] * 2,
        compiler_params=params_with(16),
        name="owner",
    )(inbox.reshape(peers * MSG, LANES), own, base, dual, steps, pick)
    new_duals = jnp.zeros_like(shifted)
    for n, route in enumerate(routes):
        theirs = lax.ppermute(sent[n], "scene", route)
        change = shifted - 0.5 * (shifted + theirs)
        new_duals = jnp.where(mask[n] > 0.5, change, new_duals)
    return updated.swapaxes(0, 1)[None], new_duals.swapaxes(0, 1)[None]


def solution(mesh):
    placed = (
        P("scene", "tile", None, None),
        P("scene", "tile", None, None),
        P("scene", "tile", None, None),
        P(),
        P(),
        P("scene", "tile"),
        P("scene", "tile", None),
        P("scene", "tile", None),
        P("scene", "tile"),
        P("scene", "tile", None, None),
        P("scene", "tile", None, None),
    )
    return jax.shard_map(
        on_device,
        mesh=mesh,
        in_specs=placed,
        out_specs=(P("scene", "tile", None, None), P("scene", "tile", None, None)),
        check_vma=False,
    )
```

```python
import functools

import jax
import jax.numpy as jnp
import numpy as np
from jax import lax
from jax.experimental import pallas as pl
from jax.experimental.pallas import tpu as pltpu
from jax.sharding import PartitionSpec as P

penalty_weight = 0.5
blur_floor = 0.3
alpha_ceiling = 0.99
log2e = 1.4426950408889634
sh_zero = 0.28209479177387814
sh_one = 0.4886025119029199
sh_two = (
    1.0925484305920792,
    -1.0925484305920792,
    0.31539156525252005,
    -1.0925484305920792,
    0.5462742152960396,
)
sh_three = (
    -0.5900435899266435,
    2.890611442640554,
    -0.4570457994644658,
    0.3731763325901154,
    -0.4570457994644658,
    1.445305721320277,
    -0.5900435899266435,
)

LANES = 128
SUB = 8
PART = 16
KDIM = 3 * PART
COEFS = 9
INNER = 4
MOMENTS = 6
WIDE = 256
MSG = 16
highest = lax.Precision.HIGHEST


def harmonic_basis(x, y, z):
    xx, yy, zz = x * x, y * y, z * z
    return [
        sh_zero + 0.0 * x,
        -sh_one * y,
        sh_one * z,
        -sh_one * x,
        sh_two[0] * x * y,
        sh_two[1] * y * z,
        sh_two[2] * (2.0 * zz - xx - yy),
        sh_two[3] * x * z,
        sh_two[4] * (xx - yy),
        sh_three[0] * y * (3.0 * xx - yy),
        sh_three[1] * x * y * z,
        sh_three[2] * y * (4.0 * zz - xx - yy),
        sh_three[3] * z * (2.0 * zz - 3.0 * xx - 3.0 * yy),
        sh_three[4] * x * (4.0 * zz - xx - yy),
        sh_three[5] * z * (xx - yy),
        sh_three[6] * x * (xx - 3.0 * yy),
    ]


def geometry(row, cam):
    mean = [row(0), row(1), row(2)]
    rot = [[cam[3 * i + j] for j in range(3)] for i in range(3)]
    shift = [cam[9 + i] for i in range(3)]
    focal_x, focal_y = cam[12], cam[13]
    view = [
        rot[i][0] * mean[0] + rot[i][1] * mean[1] + rot[i][2] * mean[2] + shift[i] for i in range(3)
    ]
    inverse = 1.0 / view[2]
    u = view[0] * inverse
    v = view[1] * inverse
    quat = [row(6 + i) for i in range(4)]
    norm = lax.rsqrt(sum(q * q for q in quat))
    w, x, y, z = [q * norm for q in quat]
    turn = [
        [1.0 - 2.0 * (y * y + z * z), 2.0 * (x * y - w * z), 2.0 * (x * z + w * y)],
        [2.0 * (x * y + w * z), 1.0 - 2.0 * (x * x + z * z), 2.0 * (y * z - w * x)],
        [2.0 * (x * z - w * y), 2.0 * (y * z + w * x), 1.0 - 2.0 * (x * x + y * y)],
    ]
    scales = [jnp.exp(row(3 + k)) for k in range(3)]
    spread = [[turn[j][k] * scales[k] for k in range(3)] for j in range(3)]
    axes = [
        [sum(rot[i][j] * spread[j][k] for j in range(3)) for k in range(3)] for i in range(3)
    ]
    scale_x = focal_x * inverse
    scale_y = focal_y * inverse
    lean_x = [axes[0][k] - u * axes[2][k] for k in range(3)]
    lean_y = [axes[1][k] - v * axes[2][k] for k in range(3)]
    row_one = [scale_x * lean_x[k] for k in range(3)]
    row_two = [scale_y * lean_y[k] for k in range(3)]
    cov_xx = sum(a * a for a in row_one) + blur_floor
    cov_xy = sum(a * b for a, b in zip(row_one, row_two))
    cov_yy = sum(b * b for b in row_two) + blur_floor
    scale = 1.0 / (cov_xx * cov_yy - cov_xy * cov_xy)
    conic = (cov_yy * scale, -cov_xy * scale, cov_xx * scale)
    eye = [-(rot[0][i] * shift[0] + rot[1][i] * shift[1] + rot[2][i] * shift[2]) for i in range(3)]
    away = [mean[i] - eye[i] for i in range(3)]
    shrink = lax.rsqrt(sum(a * a for a in away))
    toward = [a * shrink for a in away]
    return dict(
        rot=rot,
        view=view,
        inverse=inverse,
        u=u,
        v=v,
        norm=norm,
        unit=(w, x, y, z),
        scales=scales,
        spread=spread,
        axes=axes,
        scale_x=scale_x,
        scale_y=scale_y,
        lean_x=lean_x,
        lean_y=lean_y,
        row_one=row_one,
        row_two=row_two,
        conic=conic,
        shrink=shrink,
        toward=toward,
    )


def three_parts(value):
    high = value.astype(jnp.bfloat16).astype(jnp.float32)
    rest = value - high
    mid = rest.astype(jnp.bfloat16).astype(jnp.float32)
    return high, mid, rest - mid


def exact_pick(value, pick):
    high, mid, low = [part.astype(jnp.bfloat16) for part in three_parts(value)]
    dot = functools.partial(jnp.dot, preferred_element_type=jnp.float32)
    return (dot(high, pick) + dot(mid, pick)) + dot(low, pick)


def sub_roll(value, shift):
    return pltpu.roll(value, shift % SUB, 0)


def prepare_kernel(
    links, group_ref, own_ref, cons_ref, dual_ref, step_ref, share_ref, *refs
):
    others, (base_ref, steps_ref, pick_ref, mask_ref) = refs[: len(links)], refs[len(links) :]
    params, blocks = own_ref.shape[0], own_ref.shape[1]
    group = group_ref[0]
    for p in range(params):
        step = step_ref[p]
        here = own_ref[p]
        steps_ref[p] = jnp.full((blocks, LANES), step)
        base_ref[p] = here - step * (penalty_weight * (here - cons_ref[p] + dual_ref[p]))
    half = share_ref.shape[1]
    local = lax.broadcasted_iota(jnp.int32, (blocks * LANES, half), 0)
    contract = (((1,), (1,)), ((), ()))
    for n, (side_of, exists_of) in enumerate(links):
        other = others[n]
        up = side_of(group)
        mine = jnp.where(up, share_ref[0:1, :], share_ref[1:2, :])
        theirs = jnp.where(up, other[1:2, :], other[0:1, :])
        source = (local == mine).astype(jnp.bfloat16)
        target = (local == theirs).astype(jnp.bfloat16)
        pick_ref[n] = lax.dot_general(
            source, target, contract, preferred_element_type=jnp.float32
        ).astype(jnp.bfloat16)
        there = jnp.full((SUB, half), jnp.where(exists_of(group), 1.0, 0.0)).astype(jnp.bfloat16)
        mask = lax.dot_general(there, source, contract, preferred_element_type=jnp.float32)
        for b in range(blocks):
            mask_ref[n, b : b + 1, :] = mask[0:1, b * LANES : (b + 1) * LANES]


def project_kernel(masks, yrows, me_ref, raw_ref, ids_ref, cameras_ref, order_ref, *refs):
    outs, feat = refs[:INNER], refs[INNER]
    outer = len(masks)
    blocks = raw_ref.shape[2]
    me = me_ref[0]
    ids = jnp.concatenate([ids_ref[...]] * (SUB // INNER), axis=0)
    lane = lax.broadcasted_iota(jnp.int32, (SUB, LANES), 1)
    sub = lax.broadcasted_iota(jnp.int32, (SUB, LANES), 0)
    ncam = cameras_ref.shape[0]
    chosen = lax.broadcasted_iota(jnp.int32, (SUB, ncam), 1) == ids[:, 0:1]
    shots = jnp.dot(chosen.astype(jnp.float32), cameras_ref[...], precision=highest)
    cam = [jnp.broadcast_to(shots[:, k : k + 1], (SUB, LANES)) for k in range(16)]
    top = (((me & 3) ^ (sub & 3)) * yrows).astype(jnp.float32)
    lists = ids[:, LANES:]
    rows = outer * INNER
    for v in range(rows // SUB):
        owners = [2 * v, 2 * v + 1]
        first = jnp.where(sub < INNER, (me ^ masks[owners[0]]) * blocks, (me ^ masks[owners[1]]) * blocks)
        found = []
        for b in range(1, blocks):
            same = (lists == first[:, : lists.shape[1]] + b).astype(jnp.float32)
            found.append(jnp.broadcast_to(jnp.max(same, axis=1, keepdims=True), (SUB, LANES)) > 0.5)

        def row(p):
            def of(b):
                return jnp.where(
                    sub < INNER,
                    jnp.broadcast_to(raw_ref[owners[0], p, b : b + 1, :], (SUB, LANES)),
                    jnp.broadcast_to(raw_ref[owners[1], p, b : b + 1, :], (SUB, LANES)),
                )

            value = of(0)
            for b in range(1, blocks):
                value = jnp.where(found[b - 1], of(b), value)
            return value

        geo = geometry(row, cam)
        sx = cam[12] * geo["u"] + (cam[14] - 64.0)
        sy = cam[13] * geo["v"] + (cam[15] - top - 4.0)
        basis = harmonic_basis(*geo["toward"])
        tint = [sum(basis[k] * row(11 + 3 * k + c) for k in range(16)) + 0.5 for c in range(3)]
        lo = -jnp.log(1.0 + jnp.exp(-row(10))) * log2e
        ca, cb, cc = geo["conic"]
        kxx = (-0.5 * log2e) * ca
        kxy = -log2e * cb
        kyy = (-0.5 * log2e) * cc
        kx = -2.0 * kxx * sx - kxy * sy
        ky = -2.0 * kyy * sy - kxy * sx
        k1 = kxx * sx * sx + kxy * sx * sy + kyy * sy * sy + lo
        for m, value in enumerate([kxx, kxy, kyy, kx, ky, k1, *tint]):
            feat[m * rows + v * SUB : m * rows + (v + 1) * SUB, :] = value
    feat[...] = exact_pick(feat[...], order_ref[...])
    for j in range(INNER):
        outs[j][...] = feat[pl.ds(j, COEFS * outer, stride=INNER), :]


def render_kernel(
    pixels, blocks, hop_bits, me_ref, cam_id_ref, count_ref, list_ref, depth_ref, cameras_ref,
    src0, src1, src2, src3, target_ref, basis_ref, xmom_ref, back_ref, out_ref,
    raw, coef, shade, stage_a, stage_b, gaps_a, gaps_b, alphas, weights, carry, before, passed,
    colours, resid, mirror, pulls, behind, sums_a, sums_b, found, rows, slots,
):
    listed = list_ref.shape[0]
    peers = out_ref.shape[0]
    outer = peers // INNER
    per_owner = blocks
    yrows = pixels // LANES
    groups = LANES // SUB
    me = me_ref[0]
    count = count_ref[0]
    cam_id = cam_id_ref[0]
    top = ((me % 4) * yrows).astype(jnp.float32)

    def place_slot(j, ends):
        live_end, dead_end = ends
        slot = depth_ref[j]
        live = slot < count
        slots[jnp.where(live, live_end, dead_end)] = slot
        return jnp.where(live, live_end + 1, live_end), jnp.where(live, dead_end, dead_end + 1)

    lax.fori_loop(0, listed, place_slot, (jnp.int32(0), count))

    for j, src in enumerate((src0, src1, src2, src3)):
        raw[j * COEFS * outer : (j + 1) * COEFS * outer, :] = src[...]
    coef[...] = jnp.zeros(coef.shape, jnp.float32)
    for k in range(coef.shape[0] // KDIM):
        coef[k * KDIM + 5 : k * KDIM + 6, :] = jnp.full((1, LANES), -4096.0)

    def fetch(k, _):
        apart = me ^ (list_ref[slots[k]] // per_owner)
        near = sum((((apart >> bit) & 1) << t) for t, bit in enumerate(hop_bits))
        start = (apart & (INNER - 1)) * (COEFS * outer) + near
        value = raw[pl.ds(start, COEFS, stride=outer), :]
        for part, piece in enumerate(three_parts(value)):
            base = pl.multiple_of(k * KDIM + part * PART, PART)
            coef[pl.ds(base, COEFS), :] = piece
            coef[pl.ds(base + COEFS, 1), :] = piece[0:1, :]
            coef[pl.ds(base + COEFS + 1, 3), :] = piece[COEFS - 3 : COEFS, :]
        return 0

    lax.fori_loop(0, count, fetch, 0)

    sub = lax.broadcasted_iota(jnp.int32, (SUB, LANES), 0)
    one = jnp.ones((SUB, LANES), jnp.float32)
    none = jnp.zeros((SUB, LANES), jnp.float32)
    row_sets = [range(yrows // 2), range(yrows // 2, yrows)]
    for y in range(yrows):
        carry[y] = one
        behind[y] = none
        for c in range(3):
            resid[c, y] = none

    def spread_row(value, index):
        return jnp.broadcast_to(value[index : index + 1, :], (SUB, LANES))

    def rows_at(start, size, step):
        return pl.ds(pl.multiple_of(start, step), size)

    def product(k, right, out, finish):
        mine = coef[rows_at(k * KDIM, KDIM, PART), :].T.astype(jnp.bfloat16)
        for start in range(0, pixels, WIDE):
            here = slice(start, start + WIDE)
            out[:, here] = finish(
                jnp.dot(mine, right[:, here], preferred_element_type=jnp.float32)
            )
        if right.shape[1] > pixels:
            shade[rows_at(k * LANES, LANES, LANES), :] = jnp.dot(
                mine, right[:, pixels:], preferred_element_type=jnp.float32
            )

    def to_alpha(value):
        return jnp.minimum(alpha_ceiling, jnp.exp2(value))

    def as_it_is(value):
        return value

    def chain(k, stage):
        base = pl.multiple_of(k * LANES, LANES)
        kept = [one] * yrows
        for i in range(groups):
            here = rows_at(base + i * SUB, SUB, SUB)
            for y in range(yrows):
                lanes = slice(y * LANES, (y + 1) * LANES)
                alpha = stage[i * SUB : (i + 1) * SUB, lanes]
                weight = alpha * kept[y]
                alphas[here, lanes] = alpha
                weights[here, lanes] = weight
                kept[y] = kept[y] - weight
        for y in range(yrows):
            passed[k, y] = kept[y]

    def tally(k, ended):
        base = pl.multiple_of(k * LANES, LANES)
        for some in row_sets:
            total = [[last - last for last in ends] for ends in ended]
            for i in range(groups):
                here = rows_at(base + i * SUB, SUB, SUB)
                tints = [shade[here, c * LANES : (c + 1) * LANES] for c in range(3)]
                for j, y in enumerate(some):
                    weight = weights[here, y * LANES : (y + 1) * LANES]
                    for c in range(3):
                        total[c][j] = total[c][j] + weight * tints[c]
            for j, y in enumerate(some):
                through = passed[k, y]
                for step in (1, 2, 4):
                    through = through * jnp.where(sub >= step, sub_roll(through, step), 1.0)
                entering = carry[y]
                ahead = entering * jnp.where(sub >= 1, sub_roll(through, 1), 1.0)
                before[k, y] = ahead
                carry[y] = entering * spread_row(through, SUB - 1)
                for c in range(3):
                    colours[k, c, y] = total[c][j]
                    resid[c, y] = resid[c, y] + ahead * total[c][j]
            ended = total
        return ended

    pairs = (count + 1) // 2
    fresh = [[none] * (yrows // 2)] * 3
    product(0, basis_ref, stage_a, to_alpha)
    product(1, basis_ref, stage_b, to_alpha)

    def advance(pair):
        chain(2 * pair, stage_a)
        product(2 * pair + 2, basis_ref, stage_a, to_alpha)
        chain(2 * pair + 1, stage_b)
        product(2 * pair + 3, basis_ref, stage_b, to_alpha)

    def forward(pair, _):
        tally(2 * pair - 1, tally(2 * pair - 2, fresh))
        advance(pair)
        return 0

    advance(0)
    lax.fori_loop(1, pairs, forward, 0)
    tally(2 * pairs - 1, tally(2 * pairs - 2, fresh))

    mirror[...] = jnp.zeros(mirror.shape, jnp.float32)
    for y in range(yrows):
        for c in range(3):
            value = jnp.sum(resid[c, y], axis=0, keepdims=True)
            value = value - target_ref[c : c + 1, y * LANES : (y + 1) * LANES]
            resid[c, y] = jnp.broadcast_to(value, (SUB, LANES))
            high, low, _ = three_parts(value)
            for piece in range(3):
                lanes = slice(y * LANES, (y + 1) * LANES)
                at = piece * PART + COEFS - 3 + c
                mirror[at : at + 1, lanes] = high
                if piece < 2:
                    mirror[at + 4 : at + 5, lanes] = low
    pulls[...] = mirror[...].astype(jnp.bfloat16)

    def follow(k, stage, gaps):
        base = pl.multiple_of(k * LANES, LANES)
        rear = [None] * yrows
        for y in range(yrows):
            gain = passed[k, y]
            value = sum(colours[k, c, y] * resid[c, y] for c in range(3))
            for step in (1, 2, 4):
                inside = sub < SUB - step
                value = value + gain * jnp.where(inside, sub_roll(value, -step), 0.0)
                gain = gain * jnp.where(inside, sub_roll(gain, -step), 1.0)
            last = behind[y]
            rear[y] = jnp.where(
                sub < SUB - 1, sub_roll(value, -1) + sub_roll(gain, -1) * last, last
            )
            behind[y] = spread_row(value + gain * last, 0)
        for i in reversed(range(groups)):
            here = slice(i * SUB, (i + 1) * SUB)
            for y in range(yrows):
                lanes = slice(y * LANES, (y + 1) * LANES)
                gap = stage[here, lanes] - rear[y]
                gaps[here, lanes] = gap
                rear[y] = rear[y] + alphas[rows_at(base + i * SUB, SUB, SUB), lanes] * gap

    def weigh(k, gaps, sums):
        base = pl.multiple_of(k * LANES, LANES)
        front = [before[k, y] for y in range(yrows)]
        for i in range(groups):
            at = slice(i * SUB, (i + 1) * SUB)
            here = rows_at(base + i * SUB, SUB, SUB)
            run = [none] * MOMENTS
            for y in range(yrows):
                lanes = slice(y * LANES, (y + 1) * LANES)
                weight = weights[here, lanes] * front[y]
                slope = jnp.where(alphas[here, lanes] < alpha_ceiling, weight * gaps[at, lanes], 0.0)
                run[0] = run[0] + slope
                run[1] = run[1] + run[0]
                run[2] = run[2] + run[1]
                for c in range(3):
                    run[3 + c] = run[3 + c] + weight * resid[c, y]
            for m, value in enumerate(run):
                sums[m * LANES + i * SUB : m * LANES + (i + 1) * SUB, :] = value

    def moments(k, sums):
        value = sums[...]
        high = value.astype(jnp.bfloat16)
        low = (value - high.astype(jnp.float32)).astype(jnp.bfloat16)
        contract = (((1,), (1,)), ((), ()))
        xmom = xmom_ref[...]
        found[k] = lax.dot_general(
            xmom, high, contract, preferred_element_type=jnp.float32
        ) + lax.dot_general(xmom, low, contract, preferred_element_type=jnp.float32)

    rearmost = 2 * pairs - 1
    product(rearmost, pulls, stage_a, as_it_is)
    product(rearmost - 1, pulls, stage_b, as_it_is)

    def retreat(k):
        follow(k, stage_a, gaps_a)
        product(jnp.maximum(k - 2, 0), pulls, stage_a, as_it_is)
        follow(k - 1, stage_b, gaps_b)
        product(jnp.maximum(k - 3, 0), pulls, stage_b, as_it_is)

    def collect(k):
        moments(k + 2, sums_a)
        weigh(k, gaps_a, sums_a)
        moments(k + 1, sums_b)
        weigh(k - 1, gaps_b, sums_b)

    def backward(pair, _):
        k = rearmost - 2 * pair
        collect(k + 2)
        retreat(k)
        return 0

    retreat(rearmost)
    lax.fori_loop(1, pairs, backward, 0)
    collect(jnp.int32(1))
    moments(1, sums_a)
    moments(0, sums_b)

    lane = lax.broadcasted_iota(jnp.int32, (1, LANES), 1)
    meta = jnp.where(lane == 17, top, 0.0)
    for c in range(16):
        meta = jnp.where(lane == c, cameras_ref[cam_id, c], meta)

    rows[...] = jnp.zeros(rows.shape, jnp.float32)

    def gather_moments(k, _):
        part = lambda order, m: found[k, order : order + 1, m * LANES : (m + 1) * LANES]
        rise = yrows - 4.0
        s0, x1, x2 = part(0, 0), part(1, 0), part(2, 0) + part(3, 0)
        t1, tx, t2 = part(0, 1), part(1, 1), 2.0 * part(0, 2) - part(0, 1)
        answer = [s0, x1, rise * s0 - t1, x2, rise * x1 - tx, rise * (rise * s0 - 2.0 * t1) + t2]
        answer += [part(0, 3 + c) for c in range(3)]
        for m, value in enumerate(answer):
            rows[pl.ds(k * MSG + m, 1), :] = value
        return 0

    lax.fori_loop(0, count, gather_moments, 0)
    rows[...] = exact_pick(rows[...], back_ref[...])

    if peers > listed:
        absent = jnp.where(lane == 16, -1.0, 0.0)
        for peer in range(peers):
            out_ref[peer] = jnp.broadcast_to(absent, (MSG, LANES))

    def send(k, _):
        block = list_ref[slots[k]]
        owner = block // per_owner
        place = (block % per_owner).astype(jnp.float32)
        rows[pl.ds(k * MSG + 9, 1), :] = jnp.where(lane == 16, place, meta)
        out_ref[owner] = rows[pl.ds(pl.multiple_of(k * MSG, MSG), MSG), :]
        return 0

    lax.fori_loop(0, listed, send, 0)


def owner_kernel(
    inbox_ref, own_ref, base_ref, dual_ref, steps_ref, pick_ref, new_ref, shifted_ref, sent_ref,
    grad, moved
):
    params, blocks = own_ref.shape[0], own_ref.shape[1]
    strips = inbox_ref.shape[0] // MSG

    def message(m):
        return inbox_ref[pl.ds(m, strips, stride=MSG), :]

    meta = message(9)
    cam = [jnp.broadcast_to(meta[:, k : k + 1], (strips, LANES)) for k in range(18)]
    place, top = cam[16], cam[17]

    def row(p):
        value = jnp.broadcast_to(own_ref[p, 0:1, :], (strips, LANES))
        for b in range(1, blocks):
            value = jnp.where(place == b, own_ref[p, b : b + 1, :], value)
        return value

    geo = geometry(row, cam)
    u, v, inverse = geo["u"], geo["v"], geo["inverse"]
    focal_x, focal_y = cam[12], cam[13]
    at_x = focal_x * u + (cam[14] - 64.0)
    at_y = focal_y * v + (cam[15] - top - 4.0)
    s0, x1, y1, x2, xy, y2, *drawn = [message(m) for m in range(9)]
    sx = x1 - at_x * s0
    sy = y1 - at_y * s0
    sxx = x2 - at_x * (x1 + sx)
    sxy = xy - at_x * y1 - at_y * sx
    syy = y2 - at_y * (y1 + sy)
    ca, cb, cc = geo["conic"]
    axes, rot = geo["axes"], geo["rot"]
    grads = {}
    opacity = 1.0 / (1.0 + jnp.exp(-row(10)))
    grads[10] = s0 * (1.0 - opacity)
    t00, t01 = sxx * ca + sxy * cb, sxx * cb + sxy * cc
    t10, t11 = sxy * ca + syy * cb, sxy * cb + syy * cc
    g_xx = 0.5 * (ca * t00 + cb * t10)
    g_xy = ca * t01 + cb * t11
    g_yy = 0.5 * (cb * t01 + cc * t11)
    one, two = geo["row_one"], geo["row_two"]
    g_one = [2.0 * g_xx * one[k] + g_xy * two[k] for k in range(3)]
    g_two = [2.0 * g_yy * two[k] + g_xy * one[k] for k in range(3)]
    px, py = geo["scale_x"], geo["scale_y"]
    g_axes = [
        [px * g_one[k] for k in range(3)],
        [py * g_two[k] for k in range(3)],
        [-(px * u * g_one[k] + py * v * g_two[k]) for k in range(3)],
    ]
    g_px = sum(g_one[k] * geo["lean_x"][k] for k in range(3))
    g_py = sum(g_two[k] * geo["lean_y"][k] for k in range(3))
    g_u = focal_x * (ca * sx + cb * sy) - px * sum(g_one[k] * axes[2][k] for k in range(3))
    g_v = focal_y * (cc * sy + cb * sx) - py * sum(g_two[k] * axes[2][k] for k in range(3))
    view = geo["view"]
    g_inverse = focal_x * g_px + focal_y * g_py + view[0] * g_u + view[1] * g_v
    g_view = [inverse * g_u, inverse * g_v, -inverse * inverse * g_inverse]
    g_spread = [
        [sum(rot[i][j] * g_axes[i][k] for i in range(3)) for k in range(3)] for j in range(3)
    ]
    for k in range(3):
        grads[3 + k] = sum(g_spread[j][k] * geo["spread"][j][k] for j in range(3))
    g = [[g_spread[j][k] * geo["scales"][k] for k in range(3)] for j in range(3)]
    w, x, y, z = geo["unit"]
    g_w = 2.0 * (z * (g[1][0] - g[0][1]) + y * (g[0][2] - g[2][0]) + x * (g[2][1] - g[1][2]))
    g_x = 2.0 * (
        y * (g[0][1] + g[1][0])
        + z * (g[0][2] + g[2][0])
        + w * (g[2][1] - g[1][2])
        - 2.0 * x * (g[1][1] + g[2][2])
    )
    g_y = 2.0 * (
        x * (g[0][1] + g[1][0])
        + z * (g[1][2] + g[2][1])
        + w * (g[0][2] - g[2][0])
        - 2.0 * y * (g[0][0] + g[2][2])
    )
    g_z = 2.0 * (
        x * (g[0][2] + g[2][0])
        + y * (g[1][2] + g[2][1])
        + w * (g[1][0] - g[0][1])
        - 2.0 * z * (g[0][0] + g[1][1])
    )
    along = w * g_w + x * g_x + y * g_y + z * g_z
    for p, (g_q, q) in enumerate(((g_w, w), (g_x, x), (g_y, y), (g_z, z))):
        grads[6 + p] = (g_q - q * along) * geo["norm"]
    x, y, z = geo["toward"]
    basis = harmonic_basis(x, y, z)
    h = [None]
    for k in range(16):
        if k:
            h.append(sum(drawn[c] * row(11 + 3 * k + c) for c in range(3)))
        for c in range(3):
            grads[11 + 3 * k + c] = basis[k] * drawn[c]
    a, d = sh_two, sh_three
    xx, yy, zz, xy, yz, xz = x * x, y * y, z * z, x * y, y * z, x * z
    g_dx = (
        -sh_one * h[3] + a[0] * y * h[4] - 2.0 * a[2] * x * h[6] + a[3] * z * h[7]
        + 2.0 * a[4] * x * h[8] + 6.0 * d[0] * xy * h[9] + d[1] * yz * h[10]
        - 2.0 * d[2] * xy * h[11] - 6.0 * d[3] * xz * h[12]
        + d[4] * (4.0 * zz - 3.0 * xx - yy) * h[13] + 2.0 * d[5] * xz * h[14]
        + 3.0 * d[6] * (xx - yy) * h[15]
    )
    g_dy = (
        -sh_one * h[1] + a[0] * x * h[4] + a[1] * z * h[5] - 2.0 * a[2] * y * h[6]
        - 2.0 * a[4] * y * h[8] + 3.0 * d[0] * (xx - yy) * h[9] + d[1] * xz * h[10]
        + d[2] * (4.0 * zz - xx - 3.0 * yy) * h[11] - 6.0 * d[3] * yz * h[12]
        - 2.0 * d[4] * xy * h[13] - 2.0 * d[5] * yz * h[14] - 6.0 * d[6] * xy * h[15]
    )
    g_dz = (
        sh_one * h[2] + a[1] * y * h[5] + 4.0 * a[2] * z * h[6] + a[3] * x * h[7]
        + d[1] * xy * h[10] + 8.0 * d[2] * yz * h[11]
        + 3.0 * d[3] * (2.0 * zz - xx - yy) * h[12] + 8.0 * d[4] * xz * h[13]
        + d[5] * (xx - yy) * h[14]
    )
    along = x * g_dx + y * g_dy + z * g_dz
    turned = [(gd - t * along) * geo["shrink"] for gd, t in ((g_dx, x), (g_dy, y), (g_dz, z))]
    for j in range(3):
        grads[j] = sum(rot[i][j] * g_view[i] for i in range(3)) + turned[j]
    for b in range(blocks):
        mine = place == b
        for p in range(params):
            grad[p * blocks + b : p * blocks + b + 1, :] = jnp.sum(
                jnp.where(mine, grads[p], 0.0), axis=0, keepdims=True
            )

    for p in range(params):
        here = slice(p * blocks, (p + 1) * blocks)
        new = base_ref[p] - steps_ref[p] * grad[here, :]
        shifted = new + dual_ref[p]
        new_ref[p] = new
        shifted_ref[p] = shifted
        moved[here, :] = shifted
    shifted = jnp.concatenate(
        [moved[pl.ds(b, params, stride=blocks), :] for b in range(blocks)], axis=1
    )
    for n in range(pick_ref.shape[0]):
        value = exact_pick(shifted, pick_ref[n])
        for b in range(blocks):
            moved[pl.ds(b, params, stride=blocks), :] = value[:, b * LANES : (b + 1) * LANES]
        for p in range(params):
            sent_ref[n, p] = moved[p * blocks : (p + 1) * blocks, :]


def constants(pixels):
    place = np.arange(pixels)
    x = (place % LANES - 64).astype(np.float32)
    y = (place // LANES - 4).astype(np.float32)
    square = (x * x).astype(jnp.bfloat16).astype(np.float32)
    part = np.zeros((PART, pixels + 3 * LANES), np.float32)
    for c, value in enumerate([square, x * y, y * y, x, y, np.ones_like(x)]):
        part[c, :pixels] = value
    part[COEFS, :pixels] = x * x - square
    for c in range(3):
        part[COEFS - 3 + c, pixels + c * LANES : pixels + (c + 1) * LANES] = 1.0
    basis = np.concatenate([part] * 3)
    xmom = np.zeros((SUB, LANES), np.float32)
    xmom[:4] = [np.ones(LANES), x[:LANES], square[:LANES], (x * x - square)[:LANES]]
    order = np.zeros((LANES, LANES), np.float32)
    groups = LANES // SUB
    for r in range(LANES):
        order[(r % SUB) * groups + r // SUB, r] = 1.0
    return [jnp.asarray(value, jnp.bfloat16) for value in (basis, xmom, order, order.T)]


def vmem(number=1):
    return [pl.BlockSpec(memory_space=pltpu.VMEM)] * number


def smem(number=1):
    return [pl.BlockSpec(memory_space=pltpu.SMEM)] * number


def params_with(mib):
    return pltpu.CompilerParams(vmem_limit_bytes=mib * 2**20)


def on_device(
    gaussians, consensus, duals, step_sizes, cameras, camera_ids, block_lists, depth_order,
    block_counts, targets, intersection,
):
    own, prior, dual = [value[0].swapaxes(0, 1) for value in (gaussians, consensus, duals)]
    params, blocks = own.shape[0], own.shape[1]
    peers = lax.axis_size("tile")
    me = lax.axis_index("tile")[None]
    listed = block_lists.shape[2]
    pixels = targets.shape[3]
    yrows = pixels // LANES
    outer = peers // INNER
    f32 = jnp.float32
    shape_of = jax.ShapeDtypeStruct
    basis, xmom, order, back = constants(pixels)

    def swap(value, mask):
        return lax.ppermute(value, "tile", [(i, i ^ mask) for i in range(peers)])

    hop_bits = list(reversed(range(2, peers.bit_length() - 1)))
    ids = jnp.concatenate(
        [jnp.broadcast_to(camera_ids, (1, LANES)), block_lists[0]], axis=1
    )
    everything = own[None]
    masks = [0]
    for step, bit in enumerate(hop_bits):
        arrived = swap(everything, 1 << bit)
        if step < 2:
            ids = jnp.concatenate([ids, swap(ids, 1 << step)], 0)
        everything = jnp.concatenate([everything, arrived], 0)
        masks += [mask | (1 << bit) for mask in masks]

    group_total = lax.axis_size("scene")
    group = lax.axis_index("scene")[None]
    share = intersection[0, 0]
    if group_total == 2:
        routes = [[(0, 1), (1, 0)]]
        links = [(lambda g: g == 0, lambda g: g >= 0)]
    else:
        routes = [
            [(g + 1, g) for g in range(group_total - 1)],
            [(g, g + 1) for g in range(group_total - 1)],
        ]
        links = [
            (lambda g: g >= 0, lambda g: g < group_total - 1),
            (lambda g: g < 0, lambda g: g > 0),
        ]
    lists = [lax.ppermute(share, "scene", route) for route in routes]

    base, steps, pick, mask = pl.pallas_call(
        functools.partial(prepare_kernel, links),
        out_shape=(
            shape_of(own.shape, f32),
            shape_of(own.shape, f32),
            shape_of((len(links), blocks * LANES, blocks * LANES), jnp.bfloat16),
            shape_of((len(links), blocks, LANES), f32),
        ),
        in_specs=smem() + vmem(3) + smem() + vmem(1 + len(links)),
        out_specs=tuple(vmem(4)),
        compiler_params=params_with(8),
        name="prepare",
    )(group, own, prior, dual, step_sizes, share, *lists)

    messages = pl.pallas_call(
        functools.partial(project_kernel, masks, yrows),
        out_shape=tuple([shape_of((COEFS * outer, LANES), f32)] * INNER),
        in_specs=smem() + vmem(4),
        out_specs=tuple(vmem(INNER)),
        scratch_shapes=[pltpu.VMEM((COEFS * outer * INNER, LANES), f32)],
        compiler_params=params_with(8),
        name="project",
    )(me, everything, ids, cameras, order)
    sources = [messages[0]] + [swap(messages[j], j) for j in range(1, INNER)]

    outbox = pl.pallas_call(
        functools.partial(render_kernel, pixels, blocks, hop_bits),
        out_shape=shape_of((peers, MSG, LANES), f32),
        in_specs=smem(6) + vmem(INNER + 4),
        out_specs=vmem()[0],
        scratch_shapes=[
            pltpu.VMEM((COEFS * peers, LANES), f32),
            pltpu.VMEM(((listed + 2) * KDIM, LANES), f32),
            pltpu.VMEM(((listed + 2) * LANES, 3 * LANES), f32),
            pltpu.VMEM((LANES, pixels), f32),
            pltpu.VMEM((LANES, pixels), f32),
            pltpu.VMEM((LANES, pixels), f32),
            pltpu.VMEM((LANES, pixels), f32),
            pltpu.VMEM(((listed + 1) * LANES, pixels), f32),
            pltpu.VMEM(((listed + 1) * LANES, pixels), f32),
            pltpu.VMEM((yrows, SUB, LANES), f32),
            pltpu.VMEM((listed + 1, yrows, SUB, LANES), f32),
            pltpu.VMEM((listed + 1, yrows, SUB, LANES), f32),
            pltpu.VMEM((listed + 1, 3, yrows, SUB, LANES), f32),
            pltpu.VMEM((3, yrows, SUB, LANES), f32),
            pltpu.VMEM((KDIM, pixels), f32),
            pltpu.VMEM((KDIM, pixels), jnp.bfloat16),
            pltpu.VMEM((yrows, SUB, LANES), f32),
            pltpu.VMEM((MOMENTS * LANES, LANES), f32),
            pltpu.VMEM((MOMENTS * LANES, LANES), f32),
            pltpu.VMEM((listed + 4, SUB, MOMENTS * LANES), f32),
            pltpu.VMEM((listed * MSG, LANES), f32),
            pltpu.SMEM((listed,), jnp.int32),
        ],
        compiler_params=params_with(48),
        name="render",
    )(
        me, camera_ids[0], block_counts[0], block_lists[0, 0], depth_order[0, 0], cameras,
        *sources, targets[0, 0], basis, xmom, back,
    )
    inbox = lax.all_to_all(outbox, "tile", split_axis=0, concat_axis=0, tiled=True)
    updated, shifted, sent = pl.pallas_call(
        owner_kernel,
        out_shape=(
            shape_of(own.shape, f32),
            shape_of(own.shape, f32),
            shape_of((len(links),) + own.shape, f32),
        ),
        in_specs=vmem(6),
        out_specs=tuple(vmem(3)),
        scratch_shapes=[pltpu.VMEM((params * blocks, LANES), f32)] * 2,
        compiler_params=params_with(16),
        name="owner",
    )(inbox.reshape(peers * MSG, LANES), own, base, dual, steps, pick)
    new_duals = jnp.zeros_like(shifted)
    for n, route in enumerate(routes):
        theirs = lax.ppermute(sent[n], "scene", route)
        change = shifted - 0.5 * (shifted + theirs)
        new_duals = jnp.where(mask[n] > 0.5, change, new_duals)
    return updated.swapaxes(0, 1)[None], new_duals.swapaxes(0, 1)[None]


def solution(mesh):
    placed = (
        P("scene", "tile", None, None),
        P("scene", "tile", None, None),
        P("scene", "tile", None, None),
        P(),
        P(),
        P("scene", "tile"),
        P("scene", "tile", None),
        P("scene", "tile", None),
        P("scene", "tile"),
        P("scene", "tile", None, None),
        P("scene", "tile", None, None),
    )
    return jax.shard_map(
        on_device,
        mesh=mesh,
        in_specs=placed,
        out_specs=(P("scene", "tile", None, None), P("scene", "tile", None, None)),
        check_vma=False,
    )
```

```python
import functools

import jax
import jax.numpy as jnp
import numpy as np
from jax import lax
from jax.experimental import pallas as pl
from jax.experimental.pallas import tpu as pltpu
from jax.sharding import PartitionSpec as P

penalty_weight = 0.5
blur_floor = 0.3
alpha_ceiling = 0.99
log2e = 1.4426950408889634
sh_zero = 0.28209479177387814
sh_one = 0.4886025119029199
sh_two = (
    1.0925484305920792,
    -1.0925484305920792,
    0.31539156525252005,
    -1.0925484305920792,
    0.5462742152960396,
)
sh_three = (
    -0.5900435899266435,
    2.890611442640554,
    -0.4570457994644658,
    0.3731763325901154,
    -0.4570457994644658,
    1.445305721320277,
    -0.5900435899266435,
)

LANES = 128
SUB = 8
PART = 16
KDIM = 3 * PART
COEFS = 9
INNER = 4
MOMENTS = 6
WIDE = 256
MSG = 16
highest = lax.Precision.HIGHEST


def harmonic_basis(x, y, z):
    xx, yy, zz = x * x, y * y, z * z
    return [
        sh_zero + 0.0 * x,
        -sh_one * y,
        sh_one * z,
        -sh_one * x,
        sh_two[0] * x * y,
        sh_two[1] * y * z,
        sh_two[2] * (2.0 * zz - xx - yy),
        sh_two[3] * x * z,
        sh_two[4] * (xx - yy),
        sh_three[0] * y * (3.0 * xx - yy),
        sh_three[1] * x * y * z,
        sh_three[2] * y * (4.0 * zz - xx - yy),
        sh_three[3] * z * (2.0 * zz - 3.0 * xx - 3.0 * yy),
        sh_three[4] * x * (4.0 * zz - xx - yy),
        sh_three[5] * z * (xx - yy),
        sh_three[6] * x * (xx - 3.0 * yy),
    ]


def geometry(row, cam):
    mean = [row(0), row(1), row(2)]
    rot = [[cam[3 * i + j] for j in range(3)] for i in range(3)]
    shift = [cam[9 + i] for i in range(3)]
    focal_x, focal_y = cam[12], cam[13]
    view = [
        rot[i][0] * mean[0] + rot[i][1] * mean[1] + rot[i][2] * mean[2] + shift[i] for i in range(3)
    ]
    inverse = 1.0 / view[2]
    u = view[0] * inverse
    v = view[1] * inverse
    quat = [row(6 + i) for i in range(4)]
    norm = lax.rsqrt(sum(q * q for q in quat))
    w, x, y, z = [q * norm for q in quat]
    turn = [
        [1.0 - 2.0 * (y * y + z * z), 2.0 * (x * y - w * z), 2.0 * (x * z + w * y)],
        [2.0 * (x * y + w * z), 1.0 - 2.0 * (x * x + z * z), 2.0 * (y * z - w * x)],
        [2.0 * (x * z - w * y), 2.0 * (y * z + w * x), 1.0 - 2.0 * (x * x + y * y)],
    ]
    scales = [jnp.exp(row(3 + k)) for k in range(3)]
    spread = [[turn[j][k] * scales[k] for k in range(3)] for j in range(3)]
    axes = [
        [sum(rot[i][j] * spread[j][k] for j in range(3)) for k in range(3)] for i in range(3)
    ]
    scale_x = focal_x * inverse
    scale_y = focal_y * inverse
    lean_x = [axes[0][k] - u * axes[2][k] for k in range(3)]
    lean_y = [axes[1][k] - v * axes[2][k] for k in range(3)]
    row_one = [scale_x * lean_x[k] for k in range(3)]
    row_two = [scale_y * lean_y[k] for k in range(3)]
    cov_xx = sum(a * a for a in row_one) + blur_floor
    cov_xy = sum(a * b for a, b in zip(row_one, row_two))
    cov_yy = sum(b * b for b in row_two) + blur_floor
    scale = 1.0 / (cov_xx * cov_yy - cov_xy * cov_xy)
    conic = (cov_yy * scale, -cov_xy * scale, cov_xx * scale)
    eye = [-(rot[0][i] * shift[0] + rot[1][i] * shift[1] + rot[2][i] * shift[2]) for i in range(3)]
    away = [mean[i] - eye[i] for i in range(3)]
    shrink = lax.rsqrt(sum(a * a for a in away))
    toward = [a * shrink for a in away]
    return dict(
        rot=rot,
        view=view,
        inverse=inverse,
        u=u,
        v=v,
        norm=norm,
        unit=(w, x, y, z),
        scales=scales,
        spread=spread,
        axes=axes,
        scale_x=scale_x,
        scale_y=scale_y,
        lean_x=lean_x,
        lean_y=lean_y,
        row_one=row_one,
        row_two=row_two,
        conic=conic,
        shrink=shrink,
        toward=toward,
    )


def three_parts(value):
    high = value.astype(jnp.bfloat16).astype(jnp.float32)
    rest = value - high
    mid = rest.astype(jnp.bfloat16).astype(jnp.float32)
    return high, mid, rest - mid


def exact_pick(value, pick):
    high, mid, low = [part.astype(jnp.bfloat16) for part in three_parts(value)]
    dot = functools.partial(jnp.dot, preferred_element_type=jnp.float32)
    return (dot(high, pick) + dot(mid, pick)) + dot(low, pick)


def segment_order(back):
    shape = (LANES, LANES)
    gauss = lax.broadcasted_iota(jnp.int32, shape, int(back))
    place = lax.broadcasted_iota(jnp.int32, shape, 1 - int(back))
    return (gauss == (place % SUB) * (LANES // SUB) + place // SUB).astype(jnp.bfloat16)


def sub_roll(value, shift):
    return pltpu.roll(value, shift % SUB, 0)


def prepare_kernel(
    links, group_ref, own_ref, cons_ref, dual_ref, step_ref, share_ref, *refs
):
    others, (base_ref, steps_ref, pick_ref, mask_ref) = refs[: len(links)], refs[len(links) :]
    params, blocks = own_ref.shape[0], own_ref.shape[1]
    group = group_ref[0]
    for p in range(params):
        step = step_ref[p]
        here = own_ref[p]
        steps_ref[p] = jnp.full((blocks, LANES), step)
        base_ref[p] = here - step * (penalty_weight * (here - cons_ref[p] + dual_ref[p]))
    half = share_ref.shape[1]
    local = lax.broadcasted_iota(jnp.int32, (blocks * LANES, half), 0)
    contract = (((1,), (1,)), ((), ()))
    for n, (side_of, exists_of) in enumerate(links):
        other = others[n]
        up = side_of(group)
        mine = jnp.where(up, share_ref[0:1, :], share_ref[1:2, :])
        theirs = jnp.where(up, other[1:2, :], other[0:1, :])
        source = (local == mine).astype(jnp.bfloat16)
        target = (local == theirs).astype(jnp.bfloat16)
        pick_ref[n] = lax.dot_general(
            source, target, contract, preferred_element_type=jnp.float32
        ).astype(jnp.bfloat16)
        there = jnp.full((SUB, half), jnp.where(exists_of(group), 1.0, 0.0)).astype(jnp.bfloat16)
        mask = lax.dot_general(there, source, contract, preferred_element_type=jnp.float32)
        for b in range(blocks):
            mask_ref[n, b : b + 1, :] = mask[0:1, b * LANES : (b + 1) * LANES]


def pack_kernel(
    camera_ref, count_ref, list_ref, depth_ref, cameras_ref, own_ref, mine_ref, pack_ref, held_ref
):
    held_ref[...] = own_ref[...]
    listed = list_ref.shape[1]
    blocks = list_ref[...]
    mine_ref[:, :16] = cameras_ref[pl.ds(camera_ref[0, 0], 1), :]
    mine_ref[:, 16:] = blocks.astype(jnp.float32)
    pack_ref[:, :listed] = blocks
    pack_ref[:, listed : 2 * listed] = depth_ref[...]
    pack_ref[:, 2 * listed :] = jnp.full((1, listed), count_ref[0, 0], jnp.int32)


def project_kernel(masks, yrows, listed, me_ref, raw_ref, ids_ref, *refs):
    outs, feat = refs[:INNER], refs[INNER]
    outer = len(masks)
    blocks = raw_ref.shape[2]
    me = me_ref[0]
    ids = jnp.concatenate([ids_ref[...]] * (SUB // INNER), axis=0)
    lane = lax.broadcasted_iota(jnp.int32, (SUB, LANES), 1)
    sub = lax.broadcasted_iota(jnp.int32, (SUB, LANES), 0)
    cam = [jnp.broadcast_to(ids[:, k : k + 1], (SUB, LANES)) for k in range(16)]
    top = (((me & 3) ^ (sub & 3)) * yrows).astype(jnp.float32)
    lists = ids[:, 16 : 16 + listed]
    rows = outer * INNER
    for v in range(rows // SUB):
        owners = [2 * v, 2 * v + 1]
        first = jnp.where(sub < INNER, (me ^ masks[owners[0]]) * blocks, (me ^ masks[owners[1]]) * blocks)
        found = []
        for b in range(1, blocks):
            same = (lists == (first[:, :listed] + b).astype(jnp.float32)).astype(jnp.float32)
            found.append(jnp.broadcast_to(jnp.max(same, axis=1, keepdims=True), (SUB, LANES)) > 0.5)

        def row(p):
            def of(b):
                return jnp.where(
                    sub < INNER,
                    jnp.broadcast_to(raw_ref[owners[0], p, b : b + 1, :], (SUB, LANES)),
                    jnp.broadcast_to(raw_ref[owners[1], p, b : b + 1, :], (SUB, LANES)),
                )

            value = of(0)
            for b in range(1, blocks):
                value = jnp.where(found[b - 1], of(b), value)
            return value

        geo = geometry(row, cam)
        sx = cam[12] * geo["u"] + (cam[14] - 64.0)
        sy = cam[13] * geo["v"] + (cam[15] - top - 4.0)
        basis = harmonic_basis(*geo["toward"])
        tint = [sum(basis[k] * row(11 + 3 * k + c) for k in range(16)) + 0.5 for c in range(3)]
        lo = -jnp.log(1.0 + jnp.exp(-row(10))) * log2e
        ca, cb, cc = geo["conic"]
        kxx = (-0.5 * log2e) * ca
        kxy = -log2e * cb
        kyy = (-0.5 * log2e) * cc
        kx = -2.0 * kxx * sx - kxy * sy
        ky = -2.0 * kyy * sy - kxy * sx
        k1 = kxx * sx * sx + kxy * sx * sy + kyy * sy * sy + lo
        for m, value in enumerate([kxx, kxy, kyy, kx, ky, k1, *tint]):
            feat[m * rows + v * SUB : m * rows + (v + 1) * SUB, :] = value
    feat[...] = exact_pick(feat[...], segment_order(False))
    for j in range(INNER):
        outs[j][...] = feat[pl.ds(j, COEFS * outer, stride=INNER), :]


def render_kernel(
    pixels, blocks, listed, hop_bits, me_ref, pack_ref, ids_ref, src0, src1, src2, src3, target_ref,
    basis_ref, out_ref,
    raw, coef, shade, stage_a, stage_b, gaps_a, gaps_b, alphas, weights, carry, before, passed,
    colours, resid, mirror, pulls, behind, sums_a, sums_b, found, rows, slots,
):
    peers = out_ref.shape[0]
    outer = peers // INNER
    per_owner = blocks
    yrows = pixels // LANES
    groups = LANES // SUB
    me = me_ref[0]
    count = pack_ref[0, 2 * listed]
    top = ((me % 4) * yrows).astype(jnp.float32)

    def place_slot(j, ends):
        live_end, dead_end = ends
        slot = pack_ref[0, listed + j]
        live = slot < count
        slots[jnp.where(live, live_end, dead_end)] = slot
        return jnp.where(live, live_end + 1, live_end), jnp.where(live, dead_end, dead_end + 1)

    lax.fori_loop(0, listed, place_slot, (jnp.int32(0), count))

    for j, src in enumerate((src0, src1, src2, src3)):
        raw[j * COEFS * outer : (j + 1) * COEFS * outer, :] = src[...]
    coef[...] = jnp.zeros(coef.shape, jnp.float32)
    for k in range(coef.shape[0] // KDIM):
        coef[k * KDIM + 5 : k * KDIM + 6, :] = jnp.full((1, LANES), -4096.0)

    def fetch(k, _):
        apart = me ^ (pack_ref[0, slots[k]] // per_owner)
        near = sum((((apart >> bit) & 1) << t) for t, bit in enumerate(hop_bits))
        start = (apart & (INNER - 1)) * (COEFS * outer) + near
        value = raw[pl.ds(start, COEFS, stride=outer), :]
        for part, piece in enumerate(three_parts(value)):
            base = pl.multiple_of(k * KDIM + part * PART, PART)
            coef[pl.ds(base, COEFS), :] = piece
            coef[pl.ds(base + COEFS, 1), :] = piece[0:1, :]
            coef[pl.ds(base + COEFS + 1, 3), :] = piece[COEFS - 3 : COEFS, :]
        return 0

    lax.fori_loop(0, count, fetch, 0)

    sub = lax.broadcasted_iota(jnp.int32, (SUB, LANES), 0)
    one = jnp.ones((SUB, LANES), jnp.float32)
    none = jnp.zeros((SUB, LANES), jnp.float32)
    row_sets = [range(yrows // 2), range(yrows // 2, yrows)]
    for y in range(yrows):
        carry[y] = one
        behind[y] = none
        for c in range(3):
            resid[c, y] = none

    def spread_row(value, index):
        return jnp.broadcast_to(value[index : index + 1, :], (SUB, LANES))

    def rows_at(start, size, step):
        return pl.ds(pl.multiple_of(start, step), size)

    def product(k, right, out, finish):
        mine = coef[rows_at(k * KDIM, KDIM, PART), :].T.astype(jnp.bfloat16)
        for start in range(0, pixels, WIDE):
            here = slice(start, start + WIDE)
            out[:, here] = finish(
                jnp.dot(mine, right[:, here], preferred_element_type=jnp.float32)
            )
        if right.shape[1] > pixels:
            shade[rows_at(k * LANES, LANES, LANES), :] = jnp.dot(
                mine, right[:, pixels:], preferred_element_type=jnp.float32
            )

    def to_alpha(value):
        return jnp.minimum(alpha_ceiling, jnp.exp2(value))

    def as_it_is(value):
        return value

    def chain(k, stage):
        base = pl.multiple_of(k * LANES, LANES)
        kept = [one] * yrows
        for i in range(groups):
            here = rows_at(base + i * SUB, SUB, SUB)
            for y in range(yrows):
                lanes = slice(y * LANES, (y + 1) * LANES)
                alpha = stage[i * SUB : (i + 1) * SUB, lanes]
                weight = alpha * kept[y]
                alphas[here, lanes] = alpha
                weights[here, lanes] = weight
                kept[y] = kept[y] - weight
        for y in range(yrows):
            passed[k, y] = kept[y]

    def tally(k, ended):
        base = pl.multiple_of(k * LANES, LANES)
        for some in row_sets:
            total = [[last - last for last in ends] for ends in ended]
            for i in range(groups):
                here = rows_at(base + i * SUB, SUB, SUB)
                tints = [shade[here, c * LANES : (c + 1) * LANES] for c in range(3)]
                for j, y in enumerate(some):
                    weight = weights[here, y * LANES : (y + 1) * LANES]
                    for c in range(3):
                        total[c][j] = total[c][j] + weight * tints[c]
            for j, y in enumerate(some):
                through = passed[k, y]
                for step in (1, 2, 4):
                    through = through * jnp.where(sub >= step, sub_roll(through, step), 1.0)
                entering = carry[y]
                ahead = entering * jnp.where(sub >= 1, sub_roll(through, 1), 1.0)
                before[k, y] = ahead
                carry[y] = entering * spread_row(through, SUB - 1)
                for c in range(3):
                    colours[k, c, y] = total[c][j]
                    resid[c, y] = resid[c, y] + ahead * total[c][j]
            ended = total
        return ended

    pairs = (count + 1) // 2
    fresh = [[none] * (yrows // 2)] * 3
    product(0, basis_ref, stage_a, to_alpha)
    product(1, basis_ref, stage_b, to_alpha)

    def advance(pair):
        chain(2 * pair, stage_a)
        product(2 * pair + 2, basis_ref, stage_a, to_alpha)
        chain(2 * pair + 1, stage_b)
        product(2 * pair + 3, basis_ref, stage_b, to_alpha)

    def forward(pair, _):
        tally(2 * pair - 1, tally(2 * pair - 2, fresh))
        advance(pair)
        return 0

    advance(0)
    lax.fori_loop(1, pairs, forward, 0)
    tally(2 * pairs - 1, tally(2 * pairs - 2, fresh))

    mirror[...] = jnp.zeros(mirror.shape, jnp.float32)
    for y in range(yrows):
        for c in range(3):
            value = jnp.sum(resid[c, y], axis=0, keepdims=True)
            value = value - target_ref[c : c + 1, y * LANES : (y + 1) * LANES]
            resid[c, y] = jnp.broadcast_to(value, (SUB, LANES))
            high, low, _ = three_parts(value)
            for piece in range(3):
                lanes = slice(y * LANES, (y + 1) * LANES)
                at = piece * PART + COEFS - 3 + c
                mirror[at : at + 1, lanes] = high
                if piece < 2:
                    mirror[at + 4 : at + 5, lanes] = low
    pulls[...] = mirror[...].astype(jnp.bfloat16)

    def follow(k, stage, gaps):
        base = pl.multiple_of(k * LANES, LANES)
        rear = [None] * yrows
        for y in range(yrows):
            gain = passed[k, y]
            value = sum(colours[k, c, y] * resid[c, y] for c in range(3))
            for step in (1, 2, 4):
                inside = sub < SUB - step
                value = value + gain * jnp.where(inside, sub_roll(value, -step), 0.0)
                gain = gain * jnp.where(inside, sub_roll(gain, -step), 1.0)
            last = behind[y]
            rear[y] = jnp.where(
                sub < SUB - 1, sub_roll(value, -1) + sub_roll(gain, -1) * last, last
            )
            behind[y] = spread_row(value + gain * last, 0)
        for i in reversed(range(groups)):
            here = slice(i * SUB, (i + 1) * SUB)
            for y in range(yrows):
                lanes = slice(y * LANES, (y + 1) * LANES)
                gap = stage[here, lanes] - rear[y]
                gaps[here, lanes] = gap
                rear[y] = rear[y] + alphas[rows_at(base + i * SUB, SUB, SUB), lanes] * gap

    def weigh(k, gaps, sums):
        base = pl.multiple_of(k * LANES, LANES)
        front = [before[k, y] for y in range(yrows)]
        for i in range(groups):
            at = slice(i * SUB, (i + 1) * SUB)
            here = rows_at(base + i * SUB, SUB, SUB)
            run = [none] * MOMENTS
            for y in range(yrows):
                lanes = slice(y * LANES, (y + 1) * LANES)
                weight = weights[here, lanes] * front[y]
                slope = jnp.where(alphas[here, lanes] < alpha_ceiling, weight * gaps[at, lanes], 0.0)
                run[0] = run[0] + slope
                run[1] = run[1] + run[0]
                run[2] = run[2] + run[1]
                for c in range(3):
                    run[3 + c] = run[3 + c] + weight * resid[c, y]
            for m, value in enumerate(run):
                sums[m * LANES + i * SUB : m * LANES + (i + 1) * SUB, :] = value

    across = (lax.broadcasted_iota(jnp.int32, (SUB, LANES), 1) - 64).astype(jnp.float32)
    square = across * across
    coarse = square.astype(jnp.bfloat16).astype(jnp.float32)
    xmom = jnp.where(sub == 0, one, jnp.where(sub == 1, across, none))
    xmom = jnp.where(sub == 2, coarse, jnp.where(sub == 3, square - coarse, xmom))
    xmom = xmom.astype(jnp.bfloat16)

    def moments(k, sums):
        value = sums[...]
        high = value.astype(jnp.bfloat16)
        low = (value - high.astype(jnp.float32)).astype(jnp.bfloat16)
        contract = (((1,), (1,)), ((), ()))
        found[k] = lax.dot_general(
            xmom, high, contract, preferred_element_type=jnp.float32
        ) + lax.dot_general(xmom, low, contract, preferred_element_type=jnp.float32)

    rearmost = 2 * pairs - 1
    product(rearmost, pulls, stage_a, as_it_is)
    product(rearmost - 1, pulls, stage_b, as_it_is)

    def retreat(k):
        follow(k, stage_a, gaps_a)
        product(jnp.maximum(k - 2, 0), pulls, stage_a, as_it_is)
        follow(k - 1, stage_b, gaps_b)
        product(jnp.maximum(k - 3, 0), pulls, stage_b, as_it_is)

    def collect(k):
        moments(k + 2, sums_a)
        weigh(k, gaps_a, sums_a)
        moments(k + 1, sums_b)
        weigh(k - 1, gaps_b, sums_b)

    def backward(pair, _):
        k = rearmost - 2 * pair
        collect(k + 2)
        retreat(k)
        return 0

    retreat(rearmost)
    lax.fori_loop(1, pairs, backward, 0)
    collect(jnp.int32(1))
    moments(1, sums_a)
    moments(0, sums_b)

    lane = lax.broadcasted_iota(jnp.int32, (1, LANES), 1)
    camera = jnp.concatenate([ids_ref[...], jnp.zeros((1, LANES - ids_ref.shape[1]), jnp.float32)], 1)
    meta = jnp.where(lane < 16, camera, jnp.where(lane == 17, top, 0.0))

    rows[...] = jnp.zeros(rows.shape, jnp.float32)

    def gather_moments(k, _):
        part = lambda order, m: found[k, order : order + 1, m * LANES : (m + 1) * LANES]
        rise = yrows - 4.0
        s0, x1, x2 = part(0, 0), part(1, 0), part(2, 0) + part(3, 0)
        t1, tx, t2 = part(0, 1), part(1, 1), 2.0 * part(0, 2) - part(0, 1)
        answer = [s0, x1, rise * s0 - t1, x2, rise * x1 - tx, rise * (rise * s0 - 2.0 * t1) + t2]
        answer += [part(0, 3 + c) for c in range(3)]
        for m, value in enumerate(answer):
            rows[pl.ds(k * MSG + m, 1), :] = value
        return 0

    lax.fori_loop(0, count, gather_moments, 0)
    rows[...] = exact_pick(rows[...], segment_order(True))

    if peers > listed:
        absent = jnp.where(lane == 16, -1.0, 0.0)
        for peer in range(peers):
            out_ref[peer] = jnp.broadcast_to(absent, (MSG, LANES))

    def send(k, _):
        block = pack_ref[0, slots[k]]
        owner = block // per_owner
        place = (block % per_owner).astype(jnp.float32)
        rows[pl.ds(k * MSG + 9, 1), :] = jnp.where(lane == 16, place, meta)
        out_ref[owner] = rows[pl.ds(pl.multiple_of(k * MSG, MSG), MSG), :]
        return 0

    lax.fori_loop(0, listed, send, 0)


def owner_kernel(
    inbox_ref, own_ref, base_ref, dual_ref, steps_ref, pick_ref, new_ref, shifted_ref, sent_ref,
    grad, moved
):
    params, blocks = own_ref.shape[0], own_ref.shape[1]
    strips = inbox_ref.shape[0] // MSG

    def message(m):
        return inbox_ref[pl.ds(m, strips, stride=MSG), :]

    meta = message(9)
    cam = [jnp.broadcast_to(meta[:, k : k + 1], (strips, LANES)) for k in range(18)]
    place, top = cam[16], cam[17]

    def row(p):
        value = jnp.broadcast_to(own_ref[p, 0:1, :], (strips, LANES))
        for b in range(1, blocks):
            value = jnp.where(place == b, own_ref[p, b : b + 1, :], value)
        return value

    geo = geometry(row, cam)
    u, v, inverse = geo["u"], geo["v"], geo["inverse"]
    focal_x, focal_y = cam[12], cam[13]
    at_x = focal_x * u + (cam[14] - 64.0)
    at_y = focal_y * v + (cam[15] - top - 4.0)
    s0, x1, y1, x2, xy, y2, *drawn = [message(m) for m in range(9)]
    sx = x1 - at_x * s0
    sy = y1 - at_y * s0
    sxx = x2 - at_x * (x1 + sx)
    sxy = xy - at_x * y1 - at_y * sx
    syy = y2 - at_y * (y1 + sy)
    ca, cb, cc = geo["conic"]
    axes, rot = geo["axes"], geo["rot"]
    grads = {}
    opacity = 1.0 / (1.0 + jnp.exp(-row(10)))
    grads[10] = s0 * (1.0 - opacity)
    t00, t01 = sxx * ca + sxy * cb, sxx * cb + sxy * cc
    t10, t11 = sxy * ca + syy * cb, sxy * cb + syy * cc
    g_xx = 0.5 * (ca * t00 + cb * t10)
    g_xy = ca * t01 + cb * t11
    g_yy = 0.5 * (cb * t01 + cc * t11)
    one, two = geo["row_one"], geo["row_two"]
    g_one = [2.0 * g_xx * one[k] + g_xy * two[k] for k in range(3)]
    g_two = [2.0 * g_yy * two[k] + g_xy * one[k] for k in range(3)]
    px, py = geo["scale_x"], geo["scale_y"]
    g_axes = [
        [px * g_one[k] for k in range(3)],
        [py * g_two[k] for k in range(3)],
        [-(px * u * g_one[k] + py * v * g_two[k]) for k in range(3)],
    ]
    g_px = sum(g_one[k] * geo["lean_x"][k] for k in range(3))
    g_py = sum(g_two[k] * geo["lean_y"][k] for k in range(3))
    g_u = focal_x * (ca * sx + cb * sy) - px * sum(g_one[k] * axes[2][k] for k in range(3))
    g_v = focal_y * (cc * sy + cb * sx) - py * sum(g_two[k] * axes[2][k] for k in range(3))
    view = geo["view"]
    g_inverse = focal_x * g_px + focal_y * g_py + view[0] * g_u + view[1] * g_v
    g_view = [inverse * g_u, inverse * g_v, -inverse * inverse * g_inverse]
    g_spread = [
        [sum(rot[i][j] * g_axes[i][k] for i in range(3)) for k in range(3)] for j in range(3)
    ]
    for k in range(3):
        grads[3 + k] = sum(g_spread[j][k] * geo["spread"][j][k] for j in range(3))
    g = [[g_spread[j][k] * geo["scales"][k] for k in range(3)] for j in range(3)]
    w, x, y, z = geo["unit"]
    g_w = 2.0 * (z * (g[1][0] - g[0][1]) + y * (g[0][2] - g[2][0]) + x * (g[2][1] - g[1][2]))
    g_x = 2.0 * (
        y * (g[0][1] + g[1][0])
        + z * (g[0][2] + g[2][0])
        + w * (g[2][1] - g[1][2])
        - 2.0 * x * (g[1][1] + g[2][2])
    )
    g_y = 2.0 * (
        x * (g[0][1] + g[1][0])
        + z * (g[1][2] + g[2][1])
        + w * (g[0][2] - g[2][0])
        - 2.0 * y * (g[0][0] + g[2][2])
    )
    g_z = 2.0 * (
        x * (g[0][2] + g[2][0])
        + y * (g[1][2] + g[2][1])
        + w * (g[1][0] - g[0][1])
        - 2.0 * z * (g[0][0] + g[1][1])
    )
    along = w * g_w + x * g_x + y * g_y + z * g_z
    for p, (g_q, q) in enumerate(((g_w, w), (g_x, x), (g_y, y), (g_z, z))):
        grads[6 + p] = (g_q - q * along) * geo["norm"]
    x, y, z = geo["toward"]
    basis = harmonic_basis(x, y, z)
    h = [None]
    for k in range(16):
        if k:
            h.append(sum(drawn[c] * row(11 + 3 * k + c) for c in range(3)))
        for c in range(3):
            grads[11 + 3 * k + c] = basis[k] * drawn[c]
    a, d = sh_two, sh_three
    xx, yy, zz, xy, yz, xz = x * x, y * y, z * z, x * y, y * z, x * z
    g_dx = (
        -sh_one * h[3] + a[0] * y * h[4] - 2.0 * a[2] * x * h[6] + a[3] * z * h[7]
        + 2.0 * a[4] * x * h[8] + 6.0 * d[0] * xy * h[9] + d[1] * yz * h[10]
        - 2.0 * d[2] * xy * h[11] - 6.0 * d[3] * xz * h[12]
        + d[4] * (4.0 * zz - 3.0 * xx - yy) * h[13] + 2.0 * d[5] * xz * h[14]
        + 3.0 * d[6] * (xx - yy) * h[15]
    )
    g_dy = (
        -sh_one * h[1] + a[0] * x * h[4] + a[1] * z * h[5] - 2.0 * a[2] * y * h[6]
        - 2.0 * a[4] * y * h[8] + 3.0 * d[0] * (xx - yy) * h[9] + d[1] * xz * h[10]
        + d[2] * (4.0 * zz - xx - 3.0 * yy) * h[11] - 6.0 * d[3] * yz * h[12]
        - 2.0 * d[4] * xy * h[13] - 2.0 * d[5] * yz * h[14] - 6.0 * d[6] * xy * h[15]
    )
    g_dz = (
        sh_one * h[2] + a[1] * y * h[5] + 4.0 * a[2] * z * h[6] + a[3] * x * h[7]
        + d[1] * xy * h[10] + 8.0 * d[2] * yz * h[11]
        + 3.0 * d[3] * (2.0 * zz - xx - yy) * h[12] + 8.0 * d[4] * xz * h[13]
        + d[5] * (xx - yy) * h[14]
    )
    along = x * g_dx + y * g_dy + z * g_dz
    turned = [(gd - t * along) * geo["shrink"] for gd, t in ((g_dx, x), (g_dy, y), (g_dz, z))]
    for j in range(3):
        grads[j] = sum(rot[i][j] * g_view[i] for i in range(3)) + turned[j]
    for b in range(blocks):
        mine = place == b
        for p in range(params):
            grad[p * blocks + b : p * blocks + b + 1, :] = jnp.sum(
                jnp.where(mine, grads[p], 0.0), axis=0, keepdims=True
            )

    for p in range(params):
        here = slice(p * blocks, (p + 1) * blocks)
        new = base_ref[p] - steps_ref[p] * grad[here, :]
        shifted = new + dual_ref[p]
        new_ref[p] = new
        shifted_ref[p] = shifted
        moved[here, :] = shifted
    shifted = jnp.concatenate(
        [moved[pl.ds(b, params, stride=blocks), :] for b in range(blocks)], axis=1
    )
    for n in range(pick_ref.shape[0]):
        value = exact_pick(shifted, pick_ref[n])
        for b in range(blocks):
            moved[pl.ds(b, params, stride=blocks), :] = value[:, b * LANES : (b + 1) * LANES]
        for p in range(params):
            sent_ref[n, p] = moved[p * blocks : (p + 1) * blocks, :]


def constants(pixels):
    place = np.arange(pixels)
    x = (place % LANES - 64).astype(np.float32)
    y = (place // LANES - 4).astype(np.float32)
    square = (x * x).astype(jnp.bfloat16).astype(np.float32)
    part = np.zeros((PART, pixels + 3 * LANES), np.float32)
    for c, value in enumerate([square, x * y, y * y, x, y, np.ones_like(x)]):
        part[c, :pixels] = value
    part[COEFS, :pixels] = x * x - square
    for c in range(3):
        part[COEFS - 3 + c, pixels + c * LANES : pixels + (c + 1) * LANES] = 1.0
    basis = np.concatenate([part] * 3)
    return jnp.asarray(basis, jnp.bfloat16)


def vmem(number=1):
    return [pl.BlockSpec(memory_space=pltpu.VMEM)] * number


def smem(number=1):
    return [pl.BlockSpec(memory_space=pltpu.SMEM)] * number


def params_with(mib):
    return pltpu.CompilerParams(vmem_limit_bytes=mib * 2**20)


def on_device(
    gaussians, consensus, duals, step_sizes, cameras, camera_ids, block_lists, depth_order,
    block_counts, targets, intersection,
):
    own, prior, dual = [value[0].swapaxes(0, 1) for value in (gaussians, consensus, duals)]
    params, blocks = own.shape[0], own.shape[1]
    peers = lax.axis_size("tile")
    me = lax.axis_index("tile")[None]
    listed = block_lists.shape[2]
    pixels = targets.shape[3]
    yrows = pixels // LANES
    outer = peers // INNER
    f32 = jnp.float32
    shape_of = jax.ShapeDtypeStruct
    basis = constants(pixels)

    def swap(value, mask):
        return lax.ppermute(value, "tile", [(i, i ^ mask) for i in range(peers)])

    hop_bits = list(reversed(range(2, peers.bit_length() - 1)))
    mine, pack, held = pl.pallas_call(
        pack_kernel,
        out_shape=(
            shape_of((1, 16 + listed), f32),
            shape_of((1, 3 * listed), jnp.int32),
            shape_of(own.shape, f32),
        ),
        in_specs=smem(2) + vmem(4),
        out_specs=tuple(vmem(3)),
        compiler_params=params_with(8),
        name="pack",
    )(camera_ids, block_counts, block_lists[0], depth_order[0], cameras, own)
    ids = mine
    everything = held[None]
    masks = [0]
    for step, bit in enumerate(hop_bits):
        arrived = swap(own[None] if step == 0 else everything, 1 << bit)
        if step < 2:
            ids = jnp.concatenate([ids, swap(ids, 1 << step)], 0)
        everything = jnp.concatenate([everything, arrived], 0)
        masks += [mask | (1 << bit) for mask in masks]

    group_total = lax.axis_size("scene")
    group = lax.axis_index("scene")[None]
    share = intersection[0, 0]
    if group_total == 2:
        routes = [[(0, 1), (1, 0)]]
        links = [(lambda g: g == 0, lambda g: g >= 0)]
    else:
        routes = [
            [(g + 1, g) for g in range(group_total - 1)],
            [(g, g + 1) for g in range(group_total - 1)],
        ]
        links = [
            (lambda g: g >= 0, lambda g: g < group_total - 1),
            (lambda g: g < 0, lambda g: g > 0),
        ]
    lists = [lax.ppermute(share, "scene", route) for route in routes]

    base, steps, pick, mask = pl.pallas_call(
        functools.partial(prepare_kernel, links),
        out_shape=(
            shape_of(own.shape, f32),
            shape_of(own.shape, f32),
            shape_of((len(links), blocks * LANES, blocks * LANES), jnp.bfloat16),
            shape_of((len(links), blocks, LANES), f32),
        ),
        in_specs=smem() + vmem(3) + smem() + vmem(1 + len(links)),
        out_specs=tuple(vmem(4)),
        compiler_params=params_with(8),
        name="prepare",
    )(group, held, prior, dual, step_sizes, share, *lists)

    messages = pl.pallas_call(
        functools.partial(project_kernel, masks, yrows, listed),
        out_shape=tuple([shape_of((COEFS * outer, LANES), f32)] * INNER),
        in_specs=smem() + vmem(2),
        out_specs=tuple(vmem(INNER)),
        scratch_shapes=[pltpu.VMEM((COEFS * outer * INNER, LANES), f32)],
        compiler_params=params_with(8),
        name="project",
    )(me, everything, ids)
    sources = [messages[0]] + [swap(messages[j], j) for j in range(1, INNER)]

    outbox = pl.pallas_call(
        functools.partial(render_kernel, pixels, blocks, listed, hop_bits),
        out_shape=shape_of((peers, MSG, LANES), f32),
        in_specs=smem(2) + vmem(INNER + 3),
        out_specs=vmem()[0],
        scratch_shapes=[
            pltpu.VMEM((COEFS * peers, LANES), f32),
            pltpu.VMEM(((listed + 2) * KDIM, LANES), f32),
            pltpu.VMEM(((listed + 2) * LANES, 3 * LANES), f32),
            pltpu.VMEM((LANES, pixels), f32),
            pltpu.VMEM((LANES, pixels), f32),
            pltpu.VMEM((LANES, pixels), f32),
            pltpu.VMEM((LANES, pixels), f32),
            pltpu.VMEM(((listed + 1) * LANES, pixels), f32),
            pltpu.VMEM(((listed + 1) * LANES, pixels), f32),
            pltpu.VMEM((yrows, SUB, LANES), f32),
            pltpu.VMEM((listed + 1, yrows, SUB, LANES), f32),
            pltpu.VMEM((listed + 1, yrows, SUB, LANES), f32),
            pltpu.VMEM((listed + 1, 3, yrows, SUB, LANES), f32),
            pltpu.VMEM((3, yrows, SUB, LANES), f32),
            pltpu.VMEM((KDIM, pixels), f32),
            pltpu.VMEM((KDIM, pixels), jnp.bfloat16),
            pltpu.VMEM((yrows, SUB, LANES), f32),
            pltpu.VMEM((MOMENTS * LANES, LANES), f32),
            pltpu.VMEM((MOMENTS * LANES, LANES), f32),
            pltpu.VMEM((listed + 4, SUB, MOMENTS * LANES), f32),
            pltpu.VMEM((listed * MSG, LANES), f32),
            pltpu.SMEM((listed,), jnp.int32),
        ],
        compiler_params=params_with(48),
        name="render",
    )(
        me, pack, mine, *sources, targets[0, 0], basis,
    )
    inbox = lax.all_to_all(outbox, "tile", split_axis=0, concat_axis=0, tiled=True)
    updated, shifted, sent = pl.pallas_call(
        owner_kernel,
        out_shape=(
            shape_of(own.shape, f32),
            shape_of(own.shape, f32),
            shape_of((len(links),) + own.shape, f32),
        ),
        in_specs=vmem(6),
        out_specs=tuple(vmem(3)),
        scratch_shapes=[pltpu.VMEM((params * blocks, LANES), f32)] * 2,
        compiler_params=params_with(16),
        name="owner",
    )(inbox.reshape(peers * MSG, LANES), held, base, dual, steps, pick)
    new_duals = jnp.zeros_like(shifted)
    for n, route in enumerate(routes):
        theirs = lax.ppermute(sent[n], "scene", route)
        change = shifted - 0.5 * (shifted + theirs)
        new_duals = jnp.where(mask[n] > 0.5, change, new_duals)
    return updated.swapaxes(0, 1)[None], new_duals.swapaxes(0, 1)[None]


def solution(mesh):
    placed = (
        P("scene", "tile", None, None),
        P("scene", "tile", None, None),
        P("scene", "tile", None, None),
        P(),
        P(),
        P("scene", "tile"),
        P("scene", "tile", None),
        P("scene", "tile", None),
        P("scene", "tile"),
        P("scene", "tile", None, None),
        P("scene", "tile", None, None),
    )
    return jax.shard_map(
        on_device,
        mesh=mesh,
        in_specs=placed,
        out_specs=(P("scene", "tile", None, None), P("scene", "tile", None, None)),
        check_vma=False,
    )
```

```python
import functools

import jax
import jax.numpy as jnp
import numpy as np
from jax import lax
from jax.experimental import pallas as pl
from jax.experimental.pallas import tpu as pltpu
from jax.sharding import PartitionSpec as P

penalty_weight = 0.5
blur_floor = 0.3
alpha_ceiling = 0.99
log2e = 1.4426950408889634
sh_zero = 0.28209479177387814
sh_one = 0.4886025119029199
sh_two = (
    1.0925484305920792,
    -1.0925484305920792,
    0.31539156525252005,
    -1.0925484305920792,
    0.5462742152960396,
)
sh_three = (
    -0.5900435899266435,
    2.890611442640554,
    -0.4570457994644658,
    0.3731763325901154,
    -0.4570457994644658,
    1.445305721320277,
    -0.5900435899266435,
)

LANES = 128
SUB = 8
PART = 16
KDIM = 3 * PART
COEFS = 9
INNER = 4
MOMENTS = 6
WIDE = 256
MSG = 16
highest = lax.Precision.HIGHEST


def harmonic_basis(x, y, z):
    xx, yy, zz = x * x, y * y, z * z
    return [
        sh_zero + 0.0 * x,
        -sh_one * y,
        sh_one * z,
        -sh_one * x,
        sh_two[0] * x * y,
        sh_two[1] * y * z,
        sh_two[2] * (2.0 * zz - xx - yy),
        sh_two[3] * x * z,
        sh_two[4] * (xx - yy),
        sh_three[0] * y * (3.0 * xx - yy),
        sh_three[1] * x * y * z,
        sh_three[2] * y * (4.0 * zz - xx - yy),
        sh_three[3] * z * (2.0 * zz - 3.0 * xx - 3.0 * yy),
        sh_three[4] * x * (4.0 * zz - xx - yy),
        sh_three[5] * z * (xx - yy),
        sh_three[6] * x * (xx - 3.0 * yy),
    ]


def geometry(row, cam):
    mean = [row(0), row(1), row(2)]
    rot = [[cam[3 * i + j] for j in range(3)] for i in range(3)]
    shift = [cam[9 + i] for i in range(3)]
    focal_x, focal_y = cam[12], cam[13]
    view = [
        rot[i][0] * mean[0] + rot[i][1] * mean[1] + rot[i][2] * mean[2] + shift[i] for i in range(3)
    ]
    inverse = 1.0 / view[2]
    u = view[0] * inverse
    v = view[1] * inverse
    quat = [row(6 + i) for i in range(4)]
    norm = lax.rsqrt(sum(q * q for q in quat))
    w, x, y, z = [q * norm for q in quat]
    turn = [
        [1.0 - 2.0 * (y * y + z * z), 2.0 * (x * y - w * z), 2.0 * (x * z + w * y)],
        [2.0 * (x * y + w * z), 1.0 - 2.0 * (x * x + z * z), 2.0 * (y * z - w * x)],
        [2.0 * (x * z - w * y), 2.0 * (y * z + w * x), 1.0 - 2.0 * (x * x + y * y)],
    ]
    scales = [jnp.exp(row(3 + k)) for k in range(3)]
    spread = [[turn[j][k] * scales[k] for k in range(3)] for j in range(3)]
    axes = [
        [sum(rot[i][j] * spread[j][k] for j in range(3)) for k in range(3)] for i in range(3)
    ]
    scale_x = focal_x * inverse
    scale_y = focal_y * inverse
    lean_x = [axes[0][k] - u * axes[2][k] for k in range(3)]
    lean_y = [axes[1][k] - v * axes[2][k] for k in range(3)]
    row_one = [scale_x * lean_x[k] for k in range(3)]
    row_two = [scale_y * lean_y[k] for k in range(3)]
    cov_xx = sum(a * a for a in row_one) + blur_floor
    cov_xy = sum(a * b for a, b in zip(row_one, row_two))
    cov_yy = sum(b * b for b in row_two) + blur_floor
    scale = 1.0 / (cov_xx * cov_yy - cov_xy * cov_xy)
    conic = (cov_yy * scale, -cov_xy * scale, cov_xx * scale)
    eye = [-(rot[0][i] * shift[0] + rot[1][i] * shift[1] + rot[2][i] * shift[2]) for i in range(3)]
    away = [mean[i] - eye[i] for i in range(3)]
    shrink = lax.rsqrt(sum(a * a for a in away))
    toward = [a * shrink for a in away]
    return dict(
        rot=rot,
        view=view,
        inverse=inverse,
        u=u,
        v=v,
        norm=norm,
        unit=(w, x, y, z),
        scales=scales,
        spread=spread,
        axes=axes,
        scale_x=scale_x,
        scale_y=scale_y,
        lean_x=lean_x,
        lean_y=lean_y,
        row_one=row_one,
        row_two=row_two,
        conic=conic,
        shrink=shrink,
        toward=toward,
    )


def three_parts(value):
    high = value.astype(jnp.bfloat16).astype(jnp.float32)
    rest = value - high
    mid = rest.astype(jnp.bfloat16).astype(jnp.float32)
    return high, mid, rest - mid


def exact_pick(value, pick):
    high, mid, low = [part.astype(jnp.bfloat16) for part in three_parts(value)]
    dot = functools.partial(jnp.dot, preferred_element_type=jnp.float32)
    return (dot(high, pick) + dot(mid, pick)) + dot(low, pick)


def segment_order(back):
    shape = (LANES, LANES)
    gauss = lax.broadcasted_iota(jnp.int32, shape, int(back))
    place = lax.broadcasted_iota(jnp.int32, shape, 1 - int(back))
    return (gauss == (place % SUB) * (LANES // SUB) + place // SUB).astype(jnp.bfloat16)


def sub_roll(value, shift):
    return pltpu.roll(value, shift % SUB, 0)


def prepare_kernel(
    links, group_ref, own_ref, cons_ref, dual_ref, step_ref, share_ref, *refs
):
    others, (base_ref, steps_ref, pick_ref, mask_ref) = refs[: len(links)], refs[len(links) :]
    params, blocks = own_ref.shape[0], own_ref.shape[1]
    group = group_ref[0]
    for p in range(params):
        step = step_ref[p]
        here = own_ref[p]
        steps_ref[p] = jnp.full((blocks, LANES), step)
        base_ref[p] = here - step * (penalty_weight * (here - cons_ref[p] + dual_ref[p]))
    half = share_ref.shape[1]
    local = lax.broadcasted_iota(jnp.int32, (blocks * LANES, half), 0)
    contract = (((1,), (1,)), ((), ()))
    for n, (side_of, exists_of) in enumerate(links):
        other = others[n]
        up = side_of(group)
        mine = jnp.where(up, share_ref[0:1, :], share_ref[1:2, :])
        theirs = jnp.where(up, other[1:2, :], other[0:1, :])
        source = (local == mine).astype(jnp.bfloat16)
        target = (local == theirs).astype(jnp.bfloat16)
        pick_ref[n] = lax.dot_general(
            source, target, contract, preferred_element_type=jnp.float32
        ).astype(jnp.bfloat16)
        there = jnp.full((SUB, half), jnp.where(exists_of(group), 1.0, 0.0)).astype(jnp.bfloat16)
        mask = lax.dot_general(there, source, contract, preferred_element_type=jnp.float32)
        for b in range(blocks):
            mask_ref[n, b : b + 1, :] = mask[0:1, b * LANES : (b + 1) * LANES]


def pack_kernel(
    camera_ref, count_ref, list_ref, depth_ref, cameras_ref, own_ref, mine_ref, pack_ref, held_ref
):
    held_ref[...] = own_ref[...]
    listed = list_ref.shape[1]
    blocks = list_ref[...]
    mine_ref[:, :16] = cameras_ref[pl.ds(camera_ref[0, 0], 1), :]
    mine_ref[:, 16:] = blocks.astype(jnp.float32)
    pack_ref[:, :listed] = blocks
    pack_ref[:, listed : 2 * listed] = depth_ref[...]
    pack_ref[:, 2 * listed :] = jnp.full((1, listed), count_ref[0, 0], jnp.int32)


def project_kernel(masks, yrows, listed, me_ref, raw_ref, ids_ref, *refs):
    outs, feat = refs[:INNER], refs[INNER]
    outer = len(masks)
    blocks = raw_ref.shape[2]
    me = me_ref[0]
    ids = jnp.concatenate([ids_ref[...]] * (SUB // INNER), axis=0)
    lane = lax.broadcasted_iota(jnp.int32, (SUB, LANES), 1)
    sub = lax.broadcasted_iota(jnp.int32, (SUB, LANES), 0)
    cam = [jnp.broadcast_to(ids[:, k : k + 1], (SUB, LANES)) for k in range(16)]
    top = (((me & 3) ^ (sub & 3)) * yrows).astype(jnp.float32)
    lists = ids[:, 16 : 16 + listed]
    rows = outer * INNER
    for v in range(rows // SUB):
        owners = [2 * v, 2 * v + 1]
        first = jnp.where(sub < INNER, (me ^ masks[owners[0]]) * blocks, (me ^ masks[owners[1]]) * blocks)
        found = []
        for b in range(1, blocks):
            same = (lists == (first[:, :listed] + b).astype(jnp.float32)).astype(jnp.float32)
            found.append(jnp.broadcast_to(jnp.max(same, axis=1, keepdims=True), (SUB, LANES)) > 0.5)

        def row(p):
            def of(b):
                return jnp.where(
                    sub < INNER,
                    jnp.broadcast_to(raw_ref[owners[0], p, b : b + 1, :], (SUB, LANES)),
                    jnp.broadcast_to(raw_ref[owners[1], p, b : b + 1, :], (SUB, LANES)),
                )

            value = of(0)
            for b in range(1, blocks):
                value = jnp.where(found[b - 1], of(b), value)
            return value

        geo = geometry(row, cam)
        sx = cam[12] * geo["u"] + (cam[14] - 64.0)
        sy = cam[13] * geo["v"] + (cam[15] - top - 4.0)
        basis = harmonic_basis(*geo["toward"])
        tint = [sum(basis[k] * row(11 + 3 * k + c) for k in range(16)) + 0.5 for c in range(3)]
        lo = -jnp.log(1.0 + jnp.exp(-row(10))) * log2e
        ca, cb, cc = geo["conic"]
        kxx = (-0.5 * log2e) * ca
        kxy = -log2e * cb
        kyy = (-0.5 * log2e) * cc
        kx = -2.0 * kxx * sx - kxy * sy
        ky = -2.0 * kyy * sy - kxy * sx
        k1 = kxx * sx * sx + kxy * sx * sy + kyy * sy * sy + lo
        for m, value in enumerate([kxx, kxy, kyy, kx, ky, k1, *tint]):
            feat[m * rows + v * SUB : m * rows + (v + 1) * SUB, :] = value
    feat[...] = exact_pick(feat[...], segment_order(False))
    for j in range(INNER):
        outs[j][...] = feat[pl.ds(j, COEFS * outer, stride=INNER), :]


def render_kernel(
    pixels, blocks, listed, hop_bits, me_ref, pack_ref, ids_ref, src0, src1, src2, src3, target_ref,
    basis_ref, out_ref,
    raw, coef, lefts, shade, gaps_a, gaps_b, alphas, weights, carry, before, passed,
    colours, resid, mirror, pulls, behind, sums_a, sums_b, found, rows, slots,
):
    peers = out_ref.shape[0]
    outer = peers // INNER
    per_owner = blocks
    yrows = pixels // LANES
    groups = LANES // SUB
    me = me_ref[0]
    count = pack_ref[0, 2 * listed]
    top = ((me % 4) * yrows).astype(jnp.float32)

    def place_slot(j, ends):
        live_end, dead_end = ends
        slot = pack_ref[0, listed + j]
        live = slot < count
        slots[jnp.where(live, live_end, dead_end)] = slot
        return jnp.where(live, live_end + 1, live_end), jnp.where(live, dead_end, dead_end + 1)

    lax.fori_loop(0, listed, place_slot, (jnp.int32(0), count))

    for j, src in enumerate((src0, src1, src2, src3)):
        raw[j * COEFS * outer : (j + 1) * COEFS * outer, :] = src[...]
    coef[...] = jnp.zeros(coef.shape, jnp.float32)
    for k in range(coef.shape[0] // KDIM):
        coef[k * KDIM + 5 : k * KDIM + 6, :] = jnp.full((1, LANES), -4096.0)

    def fetch(k, _):
        apart = me ^ (pack_ref[0, slots[k]] // per_owner)
        near = sum((((apart >> bit) & 1) << t) for t, bit in enumerate(hop_bits))
        start = (apart & (INNER - 1)) * (COEFS * outer) + near
        value = raw[pl.ds(start, COEFS, stride=outer), :]
        for part, piece in enumerate(three_parts(value)):
            base = pl.multiple_of(k * KDIM + part * PART, PART)
            coef[pl.ds(base, COEFS), :] = piece
            coef[pl.ds(base + COEFS, 1), :] = piece[0:1, :]
            coef[pl.ds(base + COEFS + 1, 3), :] = piece[COEFS - 3 : COEFS, :]
        return 0

    lax.fori_loop(0, count, fetch, 0)

    sub = lax.broadcasted_iota(jnp.int32, (SUB, LANES), 0)
    one = jnp.ones((SUB, LANES), jnp.float32)
    none = jnp.zeros((SUB, LANES), jnp.float32)
    row_sets = [range(yrows // 2), range(yrows // 2, yrows)]
    for y in range(yrows):
        carry[y] = one
        behind[y] = none
        for c in range(3):
            resid[c, y] = none

    def spread_row(value, index):
        return jnp.broadcast_to(value[index : index + 1, :], (SUB, LANES))

    def rows_at(start, size, step):
        return pl.ds(pl.multiple_of(start, step), size)

    for k in range(coef.shape[0] // KDIM):
        mine = coef[k * KDIM : (k + 1) * KDIM, :].T
        lefts[k * LANES : (k + 1) * LANES, :] = mine.astype(jnp.bfloat16)

    def left(k):
        return lefts[rows_at(k * LANES, LANES, LANES), :]

    def times(mine, right, start, width):
        here = slice(start, start + width)
        return jnp.dot(mine, right[:, here], preferred_element_type=jnp.float32)

    def chain(k):
        base = pl.multiple_of(k * LANES, LANES)
        mine = left(k)
        for start in range(0, pixels, WIDE):
            value = jnp.minimum(alpha_ceiling, jnp.exp2(times(mine, basis_ref, start, WIDE)))
            kept = [one] * (WIDE // LANES)
            for i in range(groups):
                here = rows_at(base + i * SUB, SUB, SUB)
                for j in range(WIDE // LANES):
                    alpha = value[i * SUB : (i + 1) * SUB, j * LANES : (j + 1) * LANES]
                    weight = alpha * kept[j]
                    lanes = slice(start + j * LANES, start + (j + 1) * LANES)
                    alphas[here, lanes] = alpha
                    weights[here, lanes] = weight
                    kept[j] = kept[j] - weight
            for j in range(WIDE // LANES):
                passed[k, start // LANES + j] = kept[j]
        shade[rows_at(k * LANES, LANES, LANES), :] = times(mine, basis_ref, pixels, 3 * LANES)

    def tally(k, ended):
        base = pl.multiple_of(k * LANES, LANES)
        for some in row_sets:
            total = [[last - last for last in ends] for ends in ended]
            for i in range(groups):
                here = rows_at(base + i * SUB, SUB, SUB)
                tints = [shade[here, c * LANES : (c + 1) * LANES] for c in range(3)]
                for j, y in enumerate(some):
                    weight = weights[here, y * LANES : (y + 1) * LANES]
                    for c in range(3):
                        total[c][j] = total[c][j] + weight * tints[c]
            for j, y in enumerate(some):
                through = passed[k, y]
                for step in (1, 2, 4):
                    through = through * jnp.where(sub >= step, sub_roll(through, step), 1.0)
                entering = carry[y]
                ahead = entering * jnp.where(sub >= 1, sub_roll(through, 1), 1.0)
                before[k, y] = ahead
                carry[y] = entering * spread_row(through, SUB - 1)
                for c in range(3):
                    colours[k, c, y] = total[c][j]
                    resid[c, y] = resid[c, y] + ahead * total[c][j]
            ended = total
        return ended

    pairs = (count + 1) // 2
    fresh = [[none] * (yrows // 2)] * 3
    chain(0)
    chain(1)

    def forward(pair, _):
        tally(2 * pair - 1, tally(2 * pair - 2, fresh))
        chain(2 * pair)
        chain(2 * pair + 1)
        return 0

    lax.fori_loop(1, pairs, forward, 0)
    tally(2 * pairs - 1, tally(2 * pairs - 2, fresh))

    mirror[...] = jnp.zeros(mirror.shape, jnp.float32)
    for y in range(yrows):
        for c in range(3):
            value = jnp.sum(resid[c, y], axis=0, keepdims=True)
            value = value - target_ref[c : c + 1, y * LANES : (y + 1) * LANES]
            resid[c, y] = jnp.broadcast_to(value, (SUB, LANES))
            high, low, _ = three_parts(value)
            for piece in range(3):
                lanes = slice(y * LANES, (y + 1) * LANES)
                at = piece * PART + COEFS - 3 + c
                mirror[at : at + 1, lanes] = high
                if piece < 2:
                    mirror[at + 4 : at + 5, lanes] = low
    pulls[...] = mirror[...].astype(jnp.bfloat16)

    def follow(k, gaps):
        base = pl.multiple_of(k * LANES, LANES)
        rear = [None] * yrows
        for y in range(yrows):
            gain = passed[k, y]
            value = sum(colours[k, c, y] * resid[c, y] for c in range(3))
            for step in (1, 2, 4):
                inside = sub < SUB - step
                value = value + gain * jnp.where(inside, sub_roll(value, -step), 0.0)
                gain = gain * jnp.where(inside, sub_roll(gain, -step), 1.0)
            last = behind[y]
            rear[y] = jnp.where(
                sub < SUB - 1, sub_roll(value, -1) + sub_roll(gain, -1) * last, last
            )
            behind[y] = spread_row(value + gain * last, 0)
        mine = left(k)
        for start in range(0, pixels, WIDE):
            value = times(mine, pulls, start, WIDE)
            for i in reversed(range(groups)):
                here = slice(i * SUB, (i + 1) * SUB)
                for j in range(WIDE // LANES):
                    y = start // LANES + j
                    lanes = slice(y * LANES, (y + 1) * LANES)
                    gap = value[here, j * LANES : (j + 1) * LANES] - rear[y]
                    gaps[here, lanes] = gap
                    rear[y] = rear[y] + alphas[rows_at(base + i * SUB, SUB, SUB), lanes] * gap

    def weigh(k, gaps, sums):
        base = pl.multiple_of(k * LANES, LANES)
        front = [before[k, y] for y in range(yrows)]
        for i in range(groups):
            at = slice(i * SUB, (i + 1) * SUB)
            here = rows_at(base + i * SUB, SUB, SUB)
            run = [none] * MOMENTS
            for y in range(yrows):
                lanes = slice(y * LANES, (y + 1) * LANES)
                weight = weights[here, lanes] * front[y]
                slope = jnp.where(alphas[here, lanes] < alpha_ceiling, weight * gaps[at, lanes], 0.0)
                run[0] = run[0] + slope
                run[1] = run[1] + run[0]
                run[2] = run[2] + run[1]
                for c in range(3):
                    run[3 + c] = run[3 + c] + weight * resid[c, y]
            for m, value in enumerate(run):
                sums[m * LANES + i * SUB : m * LANES + (i + 1) * SUB, :] = value

    across = (lax.broadcasted_iota(jnp.int32, (SUB, LANES), 1) - 64).astype(jnp.float32)
    square = across * across
    coarse = square.astype(jnp.bfloat16).astype(jnp.float32)
    xmom = jnp.where(sub == 0, one, jnp.where(sub == 1, across, none))
    xmom = jnp.where(sub == 2, coarse, jnp.where(sub == 3, square - coarse, xmom))
    xmom = xmom.astype(jnp.bfloat16)

    def moments(k, sums):
        value = sums[...]
        high = value.astype(jnp.bfloat16)
        low = (value - high.astype(jnp.float32)).astype(jnp.bfloat16)
        contract = (((1,), (1,)), ((), ()))
        found[k] = lax.dot_general(
            xmom, high, contract, preferred_element_type=jnp.float32
        ) + lax.dot_general(xmom, low, contract, preferred_element_type=jnp.float32)

    rearmost = 2 * pairs - 1

    def retreat(k):
        follow(k, gaps_a)
        follow(k - 1, gaps_b)

    def collect(k):
        moments(k + 2, sums_a)
        weigh(k, gaps_a, sums_a)
        moments(k + 1, sums_b)
        weigh(k - 1, gaps_b, sums_b)

    def backward(pair, _):
        k = rearmost - 2 * pair
        collect(k + 2)
        retreat(k)
        return 0

    retreat(rearmost)
    lax.fori_loop(1, pairs, backward, 0)
    collect(jnp.int32(1))
    moments(1, sums_a)
    moments(0, sums_b)

    lane = lax.broadcasted_iota(jnp.int32, (1, LANES), 1)
    camera = jnp.concatenate([ids_ref[...], jnp.zeros((1, LANES - ids_ref.shape[1]), jnp.float32)], 1)
    meta = jnp.where(lane < 16, camera, jnp.where(lane == 17, top, 0.0))

    rows[...] = jnp.zeros(rows.shape, jnp.float32)

    def gather_moments(k, _):
        part = lambda order, m: found[k, order : order + 1, m * LANES : (m + 1) * LANES]
        rise = yrows - 4.0
        s0, x1, x2 = part(0, 0), part(1, 0), part(2, 0) + part(3, 0)
        t1, tx, t2 = part(0, 1), part(1, 1), 2.0 * part(0, 2) - part(0, 1)
        answer = [s0, x1, rise * s0 - t1, x2, rise * x1 - tx, rise * (rise * s0 - 2.0 * t1) + t2]
        answer += [part(0, 3 + c) for c in range(3)]
        for m, value in enumerate(answer):
            rows[pl.ds(k * MSG + m, 1), :] = value
        return 0

    lax.fori_loop(0, count, gather_moments, 0)
    rows[...] = exact_pick(rows[...], segment_order(True))

    if peers > listed:
        absent = jnp.where(lane == 16, -1.0, 0.0)
        for peer in range(peers):
            out_ref[peer] = jnp.broadcast_to(absent, (MSG, LANES))

    def send(k, _):
        block = pack_ref[0, slots[k]]
        owner = block // per_owner
        place = (block % per_owner).astype(jnp.float32)
        rows[pl.ds(k * MSG + 9, 1), :] = jnp.where(lane == 16, place, meta)
        out_ref[owner] = rows[pl.ds(pl.multiple_of(k * MSG, MSG), MSG), :]
        return 0

    lax.fori_loop(0, listed, send, 0)


def owner_kernel(
    inbox_ref, own_ref, base_ref, dual_ref, steps_ref, pick_ref, new_ref, shifted_ref, sent_ref,
    grad, moved
):
    params, blocks = own_ref.shape[0], own_ref.shape[1]
    strips = inbox_ref.shape[0] // MSG

    def message(m):
        return inbox_ref[pl.ds(m, strips, stride=MSG), :]

    meta = message(9)
    cam = [jnp.broadcast_to(meta[:, k : k + 1], (strips, LANES)) for k in range(18)]
    place, top = cam[16], cam[17]

    def row(p):
        value = jnp.broadcast_to(own_ref[p, 0:1, :], (strips, LANES))
        for b in range(1, blocks):
            value = jnp.where(place == b, own_ref[p, b : b + 1, :], value)
        return value

    geo = geometry(row, cam)
    u, v, inverse = geo["u"], geo["v"], geo["inverse"]
    focal_x, focal_y = cam[12], cam[13]
    at_x = focal_x * u + (cam[14] - 64.0)
    at_y = focal_y * v + (cam[15] - top - 4.0)
    s0, x1, y1, x2, xy, y2, *drawn = [message(m) for m in range(9)]
    sx = x1 - at_x * s0
    sy = y1 - at_y * s0
    sxx = x2 - at_x * (x1 + sx)
    sxy = xy - at_x * y1 - at_y * sx
    syy = y2 - at_y * (y1 + sy)
    ca, cb, cc = geo["conic"]
    axes, rot = geo["axes"], geo["rot"]
    grads = {}
    opacity = 1.0 / (1.0 + jnp.exp(-row(10)))
    grads[10] = s0 * (1.0 - opacity)
    t00, t01 = sxx * ca + sxy * cb, sxx * cb + sxy * cc
    t10, t11 = sxy * ca + syy * cb, sxy * cb + syy * cc
    g_xx = 0.5 * (ca * t00 + cb * t10)
    g_xy = ca * t01 + cb * t11
    g_yy = 0.5 * (cb * t01 + cc * t11)
    one, two = geo["row_one"], geo["row_two"]
    g_one = [2.0 * g_xx * one[k] + g_xy * two[k] for k in range(3)]
    g_two = [2.0 * g_yy * two[k] + g_xy * one[k] for k in range(3)]
    px, py = geo["scale_x"], geo["scale_y"]
    g_axes = [
        [px * g_one[k] for k in range(3)],
        [py * g_two[k] for k in range(3)],
        [-(px * u * g_one[k] + py * v * g_two[k]) for k in range(3)],
    ]
    g_px = sum(g_one[k] * geo["lean_x"][k] for k in range(3))
    g_py = sum(g_two[k] * geo["lean_y"][k] for k in range(3))
    g_u = focal_x * (ca * sx + cb * sy) - px * sum(g_one[k] * axes[2][k] for k in range(3))
    g_v = focal_y * (cc * sy + cb * sx) - py * sum(g_two[k] * axes[2][k] for k in range(3))
    view = geo["view"]
    g_inverse = focal_x * g_px + focal_y * g_py + view[0] * g_u + view[1] * g_v
    g_view = [inverse * g_u, inverse * g_v, -inverse * inverse * g_inverse]
    g_spread = [
        [sum(rot[i][j] * g_axes[i][k] for i in range(3)) for k in range(3)] for j in range(3)
    ]
    for k in range(3):
        grads[3 + k] = sum(g_spread[j][k] * geo["spread"][j][k] for j in range(3))
    g = [[g_spread[j][k] * geo["scales"][k] for k in range(3)] for j in range(3)]
    w, x, y, z = geo["unit"]
    g_w = 2.0 * (z * (g[1][0] - g[0][1]) + y * (g[0][2] - g[2][0]) + x * (g[2][1] - g[1][2]))
    g_x = 2.0 * (
        y * (g[0][1] + g[1][0])
        + z * (g[0][2] + g[2][0])
        + w * (g[2][1] - g[1][2])
        - 2.0 * x * (g[1][1] + g[2][2])
    )
    g_y = 2.0 * (
        x * (g[0][1] + g[1][0])
        + z * (g[1][2] + g[2][1])
        + w * (g[0][2] - g[2][0])
        - 2.0 * y * (g[0][0] + g[2][2])
    )
    g_z = 2.0 * (
        x * (g[0][2] + g[2][0])
        + y * (g[1][2] + g[2][1])
        + w * (g[1][0] - g[0][1])
        - 2.0 * z * (g[0][0] + g[1][1])
    )
    along = w * g_w + x * g_x + y * g_y + z * g_z
    for p, (g_q, q) in enumerate(((g_w, w), (g_x, x), (g_y, y), (g_z, z))):
        grads[6 + p] = (g_q - q * along) * geo["norm"]
    x, y, z = geo["toward"]
    basis = harmonic_basis(x, y, z)
    h = [None]
    for k in range(16):
        if k:
            h.append(sum(drawn[c] * row(11 + 3 * k + c) for c in range(3)))
        for c in range(3):
            grads[11 + 3 * k + c] = basis[k] * drawn[c]
    a, d = sh_two, sh_three
    xx, yy, zz, xy, yz, xz = x * x, y * y, z * z, x * y, y * z, x * z
    g_dx = (
        -sh_one * h[3] + a[0] * y * h[4] - 2.0 * a[2] * x * h[6] + a[3] * z * h[7]
        + 2.0 * a[4] * x * h[8] + 6.0 * d[0] * xy * h[9] + d[1] * yz * h[10]
        - 2.0 * d[2] * xy * h[11] - 6.0 * d[3] * xz * h[12]
        + d[4] * (4.0 * zz - 3.0 * xx - yy) * h[13] + 2.0 * d[5] * xz * h[14]
        + 3.0 * d[6] * (xx - yy) * h[15]
    )
    g_dy = (
        -sh_one * h[1] + a[0] * x * h[4] + a[1] * z * h[5] - 2.0 * a[2] * y * h[6]
        - 2.0 * a[4] * y * h[8] + 3.0 * d[0] * (xx - yy) * h[9] + d[1] * xz * h[10]
        + d[2] * (4.0 * zz - xx - 3.0 * yy) * h[11] - 6.0 * d[3] * yz * h[12]
        - 2.0 * d[4] * xy * h[13] - 2.0 * d[5] * yz * h[14] - 6.0 * d[6] * xy * h[15]
    )
    g_dz = (
        sh_one * h[2] + a[1] * y * h[5] + 4.0 * a[2] * z * h[6] + a[3] * x * h[7]
        + d[1] * xy * h[10] + 8.0 * d[2] * yz * h[11]
        + 3.0 * d[3] * (2.0 * zz - xx - yy) * h[12] + 8.0 * d[4] * xz * h[13]
        + d[5] * (xx - yy) * h[14]
    )
    along = x * g_dx + y * g_dy + z * g_dz
    turned = [(gd - t * along) * geo["shrink"] for gd, t in ((g_dx, x), (g_dy, y), (g_dz, z))]
    for j in range(3):
        grads[j] = sum(rot[i][j] * g_view[i] for i in range(3)) + turned[j]
    for b in range(blocks):
        mine = place == b
        for p in range(params):
            grad[p * blocks + b : p * blocks + b + 1, :] = jnp.sum(
                jnp.where(mine, grads[p], 0.0), axis=0, keepdims=True
            )

    for p in range(params):
        here = slice(p * blocks, (p + 1) * blocks)
        new = base_ref[p] - steps_ref[p] * grad[here, :]
        shifted = new + dual_ref[p]
        new_ref[p] = new
        shifted_ref[p] = shifted
        moved[here, :] = shifted
    shifted = jnp.concatenate(
        [moved[pl.ds(b, params, stride=blocks), :] for b in range(blocks)], axis=1
    )
    for n in range(pick_ref.shape[0]):
        value = exact_pick(shifted, pick_ref[n])
        for b in range(blocks):
            moved[pl.ds(b, params, stride=blocks), :] = value[:, b * LANES : (b + 1) * LANES]
        for p in range(params):
            sent_ref[n, p] = moved[p * blocks : (p + 1) * blocks, :]


def constants(pixels):
    place = np.arange(pixels)
    x = (place % LANES - 64).astype(np.float32)
    y = (place // LANES - 4).astype(np.float32)
    square = (x * x).astype(jnp.bfloat16).astype(np.float32)
    part = np.zeros((PART, pixels + 3 * LANES), np.float32)
    for c, value in enumerate([square, x * y, y * y, x, y, np.ones_like(x)]):
        part[c, :pixels] = value
    part[COEFS, :pixels] = x * x - square
    for c in range(3):
        part[COEFS - 3 + c, pixels + c * LANES : pixels + (c + 1) * LANES] = 1.0
    basis = np.concatenate([part] * 3)
    return jnp.asarray(basis, jnp.bfloat16)


def vmem(number=1):
    return [pl.BlockSpec(memory_space=pltpu.VMEM)] * number


def smem(number=1):
    return [pl.BlockSpec(memory_space=pltpu.SMEM)] * number


def params_with(mib):
    return pltpu.CompilerParams(vmem_limit_bytes=mib * 2**20)


def on_device(
    gaussians, consensus, duals, step_sizes, cameras, camera_ids, block_lists, depth_order,
    block_counts, targets, intersection,
):
    own, prior, dual = [value[0].swapaxes(0, 1) for value in (gaussians, consensus, duals)]
    params, blocks = own.shape[0], own.shape[1]
    peers = lax.axis_size("tile")
    me = lax.axis_index("tile")[None]
    listed = block_lists.shape[2]
    pixels = targets.shape[3]
    yrows = pixels // LANES
    outer = peers // INNER
    f32 = jnp.float32
    shape_of = jax.ShapeDtypeStruct
    basis = constants(pixels)

    def swap(value, mask):
        return lax.ppermute(value, "tile", [(i, i ^ mask) for i in range(peers)])

    hop_bits = list(reversed(range(2, peers.bit_length() - 1)))
    mine, pack, held = pl.pallas_call(
        pack_kernel,
        out_shape=(
            shape_of((1, 16 + listed), f32),
            shape_of((1, 3 * listed), jnp.int32),
            shape_of(own.shape, f32),
        ),
        in_specs=smem(2) + vmem(4),
        out_specs=tuple(vmem(3)),
        compiler_params=params_with(8),
        name="pack",
    )(camera_ids, block_counts, block_lists[0], depth_order[0], cameras, own)
    ids = mine
    everything = held[None]
    masks = [0]
    for step, bit in enumerate(hop_bits):
        arrived = swap(own[None] if step == 0 else everything, 1 << bit)
        if step < 2:
            ids = jnp.concatenate([ids, swap(ids, 1 << step)], 0)
        everything = jnp.concatenate([everything, arrived], 0)
        masks += [mask | (1 << bit) for mask in masks]

    group_total = lax.axis_size("scene")
    group = lax.axis_index("scene")[None]
    share = intersection[0, 0]
    if group_total == 2:
        routes = [[(0, 1), (1, 0)]]
        links = [(lambda g: g == 0, lambda g: g >= 0)]
    else:
        routes = [
            [(g + 1, g) for g in range(group_total - 1)],
            [(g, g + 1) for g in range(group_total - 1)],
        ]
        links = [
            (lambda g: g >= 0, lambda g: g < group_total - 1),
            (lambda g: g < 0, lambda g: g > 0),
        ]
    lists = [lax.ppermute(share, "scene", route) for route in routes]

    base, steps, pick, mask = pl.pallas_call(
        functools.partial(prepare_kernel, links),
        out_shape=(
            shape_of(own.shape, f32),
            shape_of(own.shape, f32),
            shape_of((len(links), blocks * LANES, blocks * LANES), jnp.bfloat16),
            shape_of((len(links), blocks, LANES), f32),
        ),
        in_specs=smem() + vmem(3) + smem() + vmem(1 + len(links)),
        out_specs=tuple(vmem(4)),
        compiler_params=params_with(8),
        name="prepare",
    )(group, held, prior, dual, step_sizes, share, *lists)

    messages = pl.pallas_call(
        functools.partial(project_kernel, masks, yrows, listed),
        out_shape=tuple([shape_of((COEFS * outer, LANES), f32)] * INNER),
        in_specs=smem() + vmem(2),
        out_specs=tuple(vmem(INNER)),
        scratch_shapes=[pltpu.VMEM((COEFS * outer * INNER, LANES), f32)],
        compiler_params=params_with(8),
        name="project",
    )(me, everything, ids)
    sources = [messages[0]] + [swap(messages[j], j) for j in range(1, INNER)]

    outbox = pl.pallas_call(
        functools.partial(render_kernel, pixels, blocks, listed, hop_bits),
        out_shape=shape_of((peers, MSG, LANES), f32),
        in_specs=smem(2) + vmem(INNER + 3),
        out_specs=vmem()[0],
        scratch_shapes=[
            pltpu.VMEM((COEFS * peers, LANES), f32),
            pltpu.VMEM(((listed + 1) * KDIM, LANES), f32),
            pltpu.VMEM(((listed + 1) * LANES, KDIM), jnp.bfloat16),
            pltpu.VMEM(((listed + 1) * LANES, 3 * LANES), f32),
            pltpu.VMEM((LANES, pixels), f32),
            pltpu.VMEM((LANES, pixels), f32),
            pltpu.VMEM(((listed + 1) * LANES, pixels), f32),
            pltpu.VMEM(((listed + 1) * LANES, pixels), f32),
            pltpu.VMEM((yrows, SUB, LANES), f32),
            pltpu.VMEM((listed + 1, yrows, SUB, LANES), f32),
            pltpu.VMEM((listed + 1, yrows, SUB, LANES), f32),
            pltpu.VMEM((listed + 1, 3, yrows, SUB, LANES), f32),
            pltpu.VMEM((3, yrows, SUB, LANES), f32),
            pltpu.VMEM((KDIM, pixels), f32),
            pltpu.VMEM((KDIM, pixels), jnp.bfloat16),
            pltpu.VMEM((yrows, SUB, LANES), f32),
            pltpu.VMEM((MOMENTS * LANES, LANES), f32),
            pltpu.VMEM((MOMENTS * LANES, LANES), f32),
            pltpu.VMEM((listed + 4, SUB, MOMENTS * LANES), f32),
            pltpu.VMEM((listed * MSG, LANES), f32),
            pltpu.SMEM((listed,), jnp.int32),
        ],
        compiler_params=params_with(48),
        name="render",
    )(
        me, pack, mine, *sources, targets[0, 0], basis,
    )
    inbox = lax.all_to_all(outbox, "tile", split_axis=0, concat_axis=0, tiled=True)
    updated, shifted, sent = pl.pallas_call(
        owner_kernel,
        out_shape=(
            shape_of(own.shape, f32),
            shape_of(own.shape, f32),
            shape_of((len(links),) + own.shape, f32),
        ),
        in_specs=vmem(6),
        out_specs=tuple(vmem(3)),
        scratch_shapes=[pltpu.VMEM((params * blocks, LANES), f32)] * 2,
        compiler_params=params_with(16),
        name="owner",
    )(inbox.reshape(peers * MSG, LANES), held, base, dual, steps, pick)
    new_duals = jnp.zeros_like(shifted)
    for n, route in enumerate(routes):
        theirs = lax.ppermute(sent[n], "scene", route)
        change = shifted - 0.5 * (shifted + theirs)
        new_duals = jnp.where(mask[n] > 0.5, change, new_duals)
    return updated.swapaxes(0, 1)[None], new_duals.swapaxes(0, 1)[None]


def solution(mesh):
    placed = (
        P("scene", "tile", None, None),
        P("scene", "tile", None, None),
        P("scene", "tile", None, None),
        P(),
        P(),
        P("scene", "tile"),
        P("scene", "tile", None),
        P("scene", "tile", None),
        P("scene", "tile"),
        P("scene", "tile", None, None),
        P("scene", "tile", None, None),
    )
    return jax.shard_map(
        on_device,
        mesh=mesh,
        in_specs=placed,
        out_specs=(P("scene", "tile", None, None), P("scene", "tile", None, None)),
        check_vma=False,
    )
```

```python
import functools

import jax
import jax.numpy as jnp
import numpy as np
from jax import lax
from jax.experimental import pallas as pl
from jax.experimental.pallas import tpu as pltpu
from jax.sharding import PartitionSpec as P

penalty_weight = 0.5
blur_floor = 0.3
alpha_ceiling = 0.99
log2e = 1.4426950408889634
sh_zero = 0.28209479177387814
sh_one = 0.4886025119029199
sh_two = (
    1.0925484305920792,
    -1.0925484305920792,
    0.31539156525252005,
    -1.0925484305920792,
    0.5462742152960396,
)
sh_three = (
    -0.5900435899266435,
    2.890611442640554,
    -0.4570457994644658,
    0.3731763325901154,
    -0.4570457994644658,
    1.445305721320277,
    -0.5900435899266435,
)

LANES = 128
SUB = 8
PART = 16
KDIM = 3 * PART
COEFS = 9
INNER = 4
MOMENTS = 6
WIDE = 256
MSG = 16
highest = lax.Precision.HIGHEST


def harmonic_basis(x, y, z):
    xx, yy, zz = x * x, y * y, z * z
    return [
        sh_zero + 0.0 * x,
        -sh_one * y,
        sh_one * z,
        -sh_one * x,
        sh_two[0] * x * y,
        sh_two[1] * y * z,
        sh_two[2] * (2.0 * zz - xx - yy),
        sh_two[3] * x * z,
        sh_two[4] * (xx - yy),
        sh_three[0] * y * (3.0 * xx - yy),
        sh_three[1] * x * y * z,
        sh_three[2] * y * (4.0 * zz - xx - yy),
        sh_three[3] * z * (2.0 * zz - 3.0 * xx - 3.0 * yy),
        sh_three[4] * x * (4.0 * zz - xx - yy),
        sh_three[5] * z * (xx - yy),
        sh_three[6] * x * (xx - 3.0 * yy),
    ]


def geometry(row, cam):
    mean = [row(0), row(1), row(2)]
    rot = [[cam[3 * i + j] for j in range(3)] for i in range(3)]
    shift = [cam[9 + i] for i in range(3)]
    focal_x, focal_y = cam[12], cam[13]
    view = [
        rot[i][0] * mean[0] + rot[i][1] * mean[1] + rot[i][2] * mean[2] + shift[i] for i in range(3)
    ]
    inverse = 1.0 / view[2]
    u = view[0] * inverse
    v = view[1] * inverse
    quat = [row(6 + i) for i in range(4)]
    norm = lax.rsqrt(sum(q * q for q in quat))
    w, x, y, z = [q * norm for q in quat]
    turn = [
        [1.0 - 2.0 * (y * y + z * z), 2.0 * (x * y - w * z), 2.0 * (x * z + w * y)],
        [2.0 * (x * y + w * z), 1.0 - 2.0 * (x * x + z * z), 2.0 * (y * z - w * x)],
        [2.0 * (x * z - w * y), 2.0 * (y * z + w * x), 1.0 - 2.0 * (x * x + y * y)],
    ]
    scales = [jnp.exp(row(3 + k)) for k in range(3)]
    spread = [[turn[j][k] * scales[k] for k in range(3)] for j in range(3)]
    axes = [
        [sum(rot[i][j] * spread[j][k] for j in range(3)) for k in range(3)] for i in range(3)
    ]
    scale_x = focal_x * inverse
    scale_y = focal_y * inverse
    lean_x = [axes[0][k] - u * axes[2][k] for k in range(3)]
    lean_y = [axes[1][k] - v * axes[2][k] for k in range(3)]
    row_one = [scale_x * lean_x[k] for k in range(3)]
    row_two = [scale_y * lean_y[k] for k in range(3)]
    cov_xx = sum(a * a for a in row_one) + blur_floor
    cov_xy = sum(a * b for a, b in zip(row_one, row_two))
    cov_yy = sum(b * b for b in row_two) + blur_floor
    scale = 1.0 / (cov_xx * cov_yy - cov_xy * cov_xy)
    conic = (cov_yy * scale, -cov_xy * scale, cov_xx * scale)
    eye = [-(rot[0][i] * shift[0] + rot[1][i] * shift[1] + rot[2][i] * shift[2]) for i in range(3)]
    away = [mean[i] - eye[i] for i in range(3)]
    shrink = lax.rsqrt(sum(a * a for a in away))
    toward = [a * shrink for a in away]
    return dict(
        rot=rot,
        view=view,
        inverse=inverse,
        u=u,
        v=v,
        norm=norm,
        unit=(w, x, y, z),
        scales=scales,
        spread=spread,
        axes=axes,
        scale_x=scale_x,
        scale_y=scale_y,
        lean_x=lean_x,
        lean_y=lean_y,
        row_one=row_one,
        row_two=row_two,
        conic=conic,
        shrink=shrink,
        toward=toward,
    )


def three_parts(value):
    high = value.astype(jnp.bfloat16).astype(jnp.float32)
    rest = value - high
    mid = rest.astype(jnp.bfloat16).astype(jnp.float32)
    return high, mid, rest - mid


def exact_pick(value, pick):
    high, mid, low = [part.astype(jnp.bfloat16) for part in three_parts(value)]
    dot = functools.partial(jnp.dot, preferred_element_type=jnp.float32)
    return (dot(high, pick) + dot(mid, pick)) + dot(low, pick)


def segment_order(back):
    shape = (LANES, LANES)
    gauss = lax.broadcasted_iota(jnp.int32, shape, int(back))
    place = lax.broadcasted_iota(jnp.int32, shape, 1 - int(back))
    return (gauss == (place % SUB) * (LANES // SUB) + place // SUB).astype(jnp.bfloat16)


def sub_roll(value, shift):
    return pltpu.roll(value, shift % SUB, 0)


def prepare_kernel(
    links, group_ref, own_ref, cons_ref, dual_ref, step_ref, share_ref, *refs
):
    others, (base_ref, steps_ref, pick_ref, mask_ref) = refs[: len(links)], refs[len(links) :]
    params, blocks = own_ref.shape[0], own_ref.shape[1]
    group = group_ref[0]
    for p in range(params):
        step = step_ref[p]
        here = own_ref[p]
        steps_ref[p] = jnp.full((blocks, LANES), step)
        base_ref[p] = here - step * (penalty_weight * (here - cons_ref[p] + dual_ref[p]))
    half = share_ref.shape[1]
    local = lax.broadcasted_iota(jnp.int32, (blocks * LANES, half), 0)
    contract = (((1,), (1,)), ((), ()))
    for n, (side_of, exists_of) in enumerate(links):
        other = others[n]
        up = side_of(group)
        mine = jnp.where(up, share_ref[0:1, :], share_ref[1:2, :])
        theirs = jnp.where(up, other[1:2, :], other[0:1, :])
        source = (local == mine).astype(jnp.bfloat16)
        target = (local == theirs).astype(jnp.bfloat16)
        pick_ref[n] = lax.dot_general(
            source, target, contract, preferred_element_type=jnp.float32
        ).astype(jnp.bfloat16)
        there = jnp.full((SUB, half), jnp.where(exists_of(group), 1.0, 0.0)).astype(jnp.bfloat16)
        mask = lax.dot_general(there, source, contract, preferred_element_type=jnp.float32)
        for b in range(blocks):
            mask_ref[n, b : b + 1, :] = mask[0:1, b * LANES : (b + 1) * LANES]


def hold_kernel(own_ref, held_ref):
    held_ref[...] = own_ref[...]


def pack_kernel(camera_ref, count_ref, list_ref, depth_ref, cameras_ref, mine_ref, pack_ref):
    listed = list_ref.shape[1]
    blocks = list_ref[...]
    shape = cameras_ref.shape
    chosen = lax.broadcasted_iota(jnp.int32, shape, 0) == jnp.broadcast_to(camera_ref[...], shape)
    mine_ref[:, :16] = jnp.sum(jnp.where(chosen, cameras_ref[...], 0.0), axis=0, keepdims=True)
    mine_ref[:, 16:] = blocks.astype(jnp.float32)
    pack_ref[:, :listed] = blocks
    pack_ref[:, listed : 2 * listed] = depth_ref[...]
    pack_ref[:, 2 * listed :] = jnp.broadcast_to(count_ref[...], (1, listed))


def project_kernel(masks, yrows, listed, me_ref, raw_ref, ids_ref, *refs):
    outs, feat = refs[:INNER], refs[INNER]
    outer = len(masks)
    blocks = raw_ref.shape[2]
    me = me_ref[0]
    ids = jnp.concatenate([ids_ref[...]] * (SUB // INNER), axis=0)
    lane = lax.broadcasted_iota(jnp.int32, (SUB, LANES), 1)
    sub = lax.broadcasted_iota(jnp.int32, (SUB, LANES), 0)
    cam = [jnp.broadcast_to(ids[:, k : k + 1], (SUB, LANES)) for k in range(16)]
    top = (((me & 3) ^ (sub & 3)) * yrows).astype(jnp.float32)
    lists = ids[:, 16 : 16 + listed]
    rows = outer * INNER
    for v in range(rows // SUB):
        owners = [2 * v, 2 * v + 1]
        first = jnp.where(sub < INNER, (me ^ masks[owners[0]]) * blocks, (me ^ masks[owners[1]]) * blocks)
        found = []
        for b in range(1, blocks):
            same = (lists == (first[:, :listed] + b).astype(jnp.float32)).astype(jnp.float32)
            found.append(jnp.broadcast_to(jnp.max(same, axis=1, keepdims=True), (SUB, LANES)) > 0.5)

        def row(p):
            def of(b):
                return jnp.where(
                    sub < INNER,
                    jnp.broadcast_to(raw_ref[owners[0], p, b : b + 1, :], (SUB, LANES)),
                    jnp.broadcast_to(raw_ref[owners[1], p, b : b + 1, :], (SUB, LANES)),
                )

            value = of(0)
            for b in range(1, blocks):
                value = jnp.where(found[b - 1], of(b), value)
            return value

        geo = geometry(row, cam)
        sx = cam[12] * geo["u"] + (cam[14] - 64.0)
        sy = cam[13] * geo["v"] + (cam[15] - top - 4.0)
        basis = harmonic_basis(*geo["toward"])
        tint = [sum(basis[k] * row(11 + 3 * k + c) for k in range(16)) + 0.5 for c in range(3)]
        lo = -jnp.log(1.0 + jnp.exp(-row(10))) * log2e
        ca, cb, cc = geo["conic"]
        kxx = (-0.5 * log2e) * ca
        kxy = -log2e * cb
        kyy = (-0.5 * log2e) * cc
        kx = -2.0 * kxx * sx - kxy * sy
        ky = -2.0 * kyy * sy - kxy * sx
        k1 = kxx * sx * sx + kxy * sx * sy + kyy * sy * sy + lo
        for m, value in enumerate([kxx, kxy, kyy, kx, ky, k1, *tint]):
            feat[m * rows + v * SUB : m * rows + (v + 1) * SUB, :] = value
    feat[...] = exact_pick(feat[...], segment_order(False))
    for j in range(INNER):
        outs[j][...] = feat[pl.ds(j, COEFS * outer, stride=INNER), :]


def render_kernel(
    pixels, blocks, listed, hop_bits, me_ref, pack_ref, ids_ref, src0, src1, src2, src3, target_ref,
    basis_ref, out_ref,
    raw, coef, lefts, shade, gaps_a, gaps_b, alphas, weights, carry, before, passed,
    colours, resid, mirror, pulls, behind, sums_a, sums_b, found, rows, slots,
):
    peers = out_ref.shape[0]
    outer = peers // INNER
    per_owner = blocks
    yrows = pixels // LANES
    groups = LANES // SUB
    me = me_ref[0]
    count = pack_ref[0, 2 * listed]
    top = ((me % 4) * yrows).astype(jnp.float32)

    def place_slot(j, ends):
        live_end, dead_end = ends
        slot = pack_ref[0, listed + j]
        live = slot < count
        slots[jnp.where(live, live_end, dead_end)] = slot
        return jnp.where(live, live_end + 1, live_end), jnp.where(live, dead_end, dead_end + 1)

    lax.fori_loop(0, listed, place_slot, (jnp.int32(0), count))

    for j, src in enumerate((src0, src1, src2, src3)):
        raw[j * COEFS * outer : (j + 1) * COEFS * outer, :] = src[...]
    coef[...] = jnp.zeros(coef.shape, jnp.float32)
    for k in range(coef.shape[0] // KDIM):
        coef[k * KDIM + 5 : k * KDIM + 6, :] = jnp.full((1, LANES), -4096.0)

    def fetch(k, _):
        apart = me ^ (pack_ref[0, slots[k]] // per_owner)
        near = sum((((apart >> bit) & 1) << t) for t, bit in enumerate(hop_bits))
        start = (apart & (INNER - 1)) * (COEFS * outer) + near
        value = raw[pl.ds(start, COEFS, stride=outer), :]
        for part, piece in enumerate(three_parts(value)):
            base = pl.multiple_of(k * KDIM + part * PART, PART)
            coef[pl.ds(base, COEFS), :] = piece
            coef[pl.ds(base + COEFS, 1), :] = piece[0:1, :]
            coef[pl.ds(base + COEFS + 1, 3), :] = piece[COEFS - 3 : COEFS, :]
        return 0

    lax.fori_loop(0, count, fetch, 0)

    sub = lax.broadcasted_iota(jnp.int32, (SUB, LANES), 0)
    one = jnp.ones((SUB, LANES), jnp.float32)
    none = jnp.zeros((SUB, LANES), jnp.float32)
    row_sets = [range(yrows // 2), range(yrows // 2, yrows)]
    for y in range(yrows):
        carry[y] = one
        behind[y] = none
        for c in range(3):
            resid[c, y] = none

    def spread_row(value, index):
        return jnp.broadcast_to(value[index : index + 1, :], (SUB, LANES))

    def rows_at(start, size, step):
        return pl.ds(pl.multiple_of(start, step), size)

    for k in range(coef.shape[0] // KDIM):
        mine = coef[k * KDIM : (k + 1) * KDIM, :].T
        lefts[k * LANES : (k + 1) * LANES, :] = mine.astype(jnp.bfloat16)

    def left(k):
        return lefts[rows_at(k * LANES, LANES, LANES), :]

    def times(mine, right, start, width):
        here = slice(start, start + width)
        return jnp.dot(mine, right[:, here], preferred_element_type=jnp.float32)

    def chain(k):
        base = pl.multiple_of(k * LANES, LANES)
        mine = left(k)
        for start in range(0, pixels, WIDE):
            value = jnp.minimum(alpha_ceiling, jnp.exp2(times(mine, basis_ref, start, WIDE)))
            kept = [one] * (WIDE // LANES)
            for i in range(groups):
                here = rows_at(base + i * SUB, SUB, SUB)
                for j in range(WIDE // LANES):
                    alpha = value[i * SUB : (i + 1) * SUB, j * LANES : (j + 1) * LANES]
                    weight = alpha * kept[j]
                    lanes = slice(start + j * LANES, start + (j + 1) * LANES)
                    alphas[here, lanes] = alpha
                    weights[here, lanes] = weight
                    kept[j] = kept[j] - weight
            for j in range(WIDE // LANES):
                passed[k, start // LANES + j] = kept[j]
        shade[rows_at(k * LANES, LANES, LANES), :] = times(mine, basis_ref, pixels, 3 * LANES)

    def tally(k, ended):
        base = pl.multiple_of(k * LANES, LANES)
        for some in row_sets:
            total = [[last - last for last in ends] for ends in ended]
            for i in range(groups):
                here = rows_at(base + i * SUB, SUB, SUB)
                tints = [shade[here, c * LANES : (c + 1) * LANES] for c in range(3)]
                for j, y in enumerate(some):
                    weight = weights[here, y * LANES : (y + 1) * LANES]
                    for c in range(3):
                        total[c][j] = total[c][j] + weight * tints[c]
            for j, y in enumerate(some):
                through = passed[k, y]
                for step in (1, 2, 4):
                    through = through * jnp.where(sub >= step, sub_roll(through, step), 1.0)
                entering = carry[y]
                ahead = entering * jnp.where(sub >= 1, sub_roll(through, 1), 1.0)
                before[k, y] = ahead
                carry[y] = entering * spread_row(through, SUB - 1)
                for c in range(3):
                    colours[k, c, y] = total[c][j]
                    resid[c, y] = resid[c, y] + ahead * total[c][j]
            ended = total
        return ended

    pairs = (count + 1) // 2
    fresh = [[none] * (yrows // 2)] * 3
    chain(0)
    chain(1)

    def forward(pair, _):
        tally(2 * pair - 1, tally(2 * pair - 2, fresh))
        chain(2 * pair)
        chain(2 * pair + 1)
        return 0

    lax.fori_loop(1, pairs, forward, 0)
    tally(2 * pairs - 1, tally(2 * pairs - 2, fresh))

    mirror[...] = jnp.zeros(mirror.shape, jnp.float32)
    for y in range(yrows):
        for c in range(3):
            value = jnp.sum(resid[c, y], axis=0, keepdims=True)
            value = value - target_ref[c : c + 1, y * LANES : (y + 1) * LANES]
            resid[c, y] = jnp.broadcast_to(value, (SUB, LANES))
            high, low, _ = three_parts(value)
            for piece in range(3):
                lanes = slice(y * LANES, (y + 1) * LANES)
                at = piece * PART + COEFS - 3 + c
                mirror[at : at + 1, lanes] = high
                if piece < 2:
                    mirror[at + 4 : at + 5, lanes] = low
    pulls[...] = mirror[...].astype(jnp.bfloat16)

    def follow(k, gaps):
        base = pl.multiple_of(k * LANES, LANES)
        rear = [None] * yrows
        for y in range(yrows):
            gain = passed[k, y]
            value = sum(colours[k, c, y] * resid[c, y] for c in range(3))
            for step in (1, 2, 4):
                inside = sub < SUB - step
                value = value + gain * jnp.where(inside, sub_roll(value, -step), 0.0)
                gain = gain * jnp.where(inside, sub_roll(gain, -step), 1.0)
            last = behind[y]
            rear[y] = jnp.where(
                sub < SUB - 1, sub_roll(value, -1) + sub_roll(gain, -1) * last, last
            )
            behind[y] = spread_row(value + gain * last, 0)
        mine = left(k)
        for start in range(0, pixels, WIDE):
            value = times(mine, pulls, start, WIDE)
            for i in reversed(range(groups)):
                here = slice(i * SUB, (i + 1) * SUB)
                for j in range(WIDE // LANES):
                    y = start // LANES + j
                    lanes = slice(y * LANES, (y + 1) * LANES)
                    gap = value[here, j * LANES : (j + 1) * LANES] - rear[y]
                    gaps[here, lanes] = gap
                    rear[y] = rear[y] + alphas[rows_at(base + i * SUB, SUB, SUB), lanes] * gap

    def weigh(k, gaps, sums):
        base = pl.multiple_of(k * LANES, LANES)
        front = [before[k, y] for y in range(yrows)]
        for i in range(groups):
            at = slice(i * SUB, (i + 1) * SUB)
            here = rows_at(base + i * SUB, SUB, SUB)
            run = [none] * MOMENTS
            for y in range(yrows):
                lanes = slice(y * LANES, (y + 1) * LANES)
                weight = weights[here, lanes] * front[y]
                slope = jnp.where(alphas[here, lanes] < alpha_ceiling, weight * gaps[at, lanes], 0.0)
                run[0] = run[0] + slope
                run[1] = run[1] + run[0]
                run[2] = run[2] + run[1]
                for c in range(3):
                    run[3 + c] = run[3 + c] + weight * resid[c, y]
            for m, value in enumerate(run):
                sums[m * LANES + i * SUB : m * LANES + (i + 1) * SUB, :] = value

    across = (lax.broadcasted_iota(jnp.int32, (SUB, LANES), 1) - 64).astype(jnp.float32)
    square = across * across
    coarse = square.astype(jnp.bfloat16).astype(jnp.float32)
    xmom = jnp.where(sub == 0, one, jnp.where(sub == 1, across, none))
    xmom = jnp.where(sub == 2, coarse, jnp.where(sub == 3, square - coarse, xmom))
    xmom = xmom.astype(jnp.bfloat16)

    def moments(k, sums):
        value = sums[...]
        high = value.astype(jnp.bfloat16)
        low = (value - high.astype(jnp.float32)).astype(jnp.bfloat16)
        contract = (((1,), (1,)), ((), ()))
        found[k] = lax.dot_general(
            xmom, high, contract, preferred_element_type=jnp.float32
        ) + lax.dot_general(xmom, low, contract, preferred_element_type=jnp.float32)

    rearmost = 2 * pairs - 1

    def backward(pair, _):
        k = rearmost - 2 * pair
        moments(k + 4, sums_a)
        weigh(k + 2, gaps_a, sums_a)
        follow(k, gaps_a)
        moments(k + 3, sums_b)
        weigh(k + 1, gaps_b, sums_b)
        follow(k - 1, gaps_b)
        return 0

    follow(rearmost, gaps_a)
    follow(rearmost - 1, gaps_b)
    lax.fori_loop(1, pairs, backward, 0)
    moments(3, sums_a)
    weigh(1, gaps_a, sums_a)
    moments(2, sums_b)
    weigh(0, gaps_b, sums_b)
    moments(1, sums_a)
    moments(0, sums_b)

    lane = lax.broadcasted_iota(jnp.int32, (1, LANES), 1)
    camera = jnp.concatenate([ids_ref[...], jnp.zeros((1, LANES - ids_ref.shape[1]), jnp.float32)], 1)
    meta = jnp.where(lane < 16, camera, jnp.where(lane == 17, top, 0.0))

    rows[...] = jnp.zeros(rows.shape, jnp.float32)

    def gather_moments(k, _):
        part = lambda order, m: found[k, order : order + 1, m * LANES : (m + 1) * LANES]
        rise = yrows - 4.0
        s0, x1, x2 = part(0, 0), part(1, 0), part(2, 0) + part(3, 0)
        t1, tx, t2 = part(0, 1), part(1, 1), 2.0 * part(0, 2) - part(0, 1)
        answer = [s0, x1, rise * s0 - t1, x2, rise * x1 - tx, rise * (rise * s0 - 2.0 * t1) + t2]
        answer += [part(0, 3 + c) for c in range(3)]
        for m, value in enumerate(answer):
            rows[pl.ds(k * MSG + m, 1), :] = value
        return 0

    lax.fori_loop(0, count, gather_moments, 0)
    rows[...] = exact_pick(rows[...], segment_order(True))

    if peers > listed:
        absent = jnp.where(lane == 16, -1.0, 0.0)
        for peer in range(peers):
            out_ref[peer] = jnp.broadcast_to(absent, (MSG, LANES))

    def send(k, _):
        block = pack_ref[0, slots[k]]
        owner = block // per_owner
        place = (block % per_owner).astype(jnp.float32)
        rows[pl.ds(k * MSG + 9, 1), :] = jnp.where(lane == 16, place, meta)
        out_ref[owner] = rows[pl.ds(pl.multiple_of(k * MSG, MSG), MSG), :]
        return 0

    lax.fori_loop(0, listed, send, 0)


def owner_kernel(
    inbox_ref, own_ref, base_ref, dual_ref, steps_ref, pick_ref, new_ref, shifted_ref, sent_ref,
    grad, moved
):
    params, blocks = own_ref.shape[0], own_ref.shape[1]
    strips = inbox_ref.shape[0] // MSG

    def message(m):
        return inbox_ref[pl.ds(m, strips, stride=MSG), :]

    meta = message(9)
    cam = [jnp.broadcast_to(meta[:, k : k + 1], (strips, LANES)) for k in range(18)]
    place, top = cam[16], cam[17]

    def row(p):
        value = jnp.broadcast_to(own_ref[p, 0:1, :], (strips, LANES))
        for b in range(1, blocks):
            value = jnp.where(place == b, own_ref[p, b : b + 1, :], value)
        return value

    geo = geometry(row, cam)
    u, v, inverse = geo["u"], geo["v"], geo["inverse"]
    focal_x, focal_y = cam[12], cam[13]
    at_x = focal_x * u + (cam[14] - 64.0)
    at_y = focal_y * v + (cam[15] - top - 4.0)
    s0, x1, y1, x2, xy, y2, *drawn = [message(m) for m in range(9)]
    sx = x1 - at_x * s0
    sy = y1 - at_y * s0
    sxx = x2 - at_x * (x1 + sx)
    sxy = xy - at_x * y1 - at_y * sx
    syy = y2 - at_y * (y1 + sy)
    ca, cb, cc = geo["conic"]
    axes, rot = geo["axes"], geo["rot"]
    grads = {}
    opacity = 1.0 / (1.0 + jnp.exp(-row(10)))
    grads[10] = s0 * (1.0 - opacity)
    t00, t01 = sxx * ca + sxy * cb, sxx * cb + sxy * cc
    t10, t11 = sxy * ca + syy * cb, sxy * cb + syy * cc
    g_xx = 0.5 * (ca * t00 + cb * t10)
    g_xy = ca * t01 + cb * t11
    g_yy = 0.5 * (cb * t01 + cc * t11)
    one, two = geo["row_one"], geo["row_two"]
    g_one = [2.0 * g_xx * one[k] + g_xy * two[k] for k in range(3)]
    g_two = [2.0 * g_yy * two[k] + g_xy * one[k] for k in range(3)]
    px, py = geo["scale_x"], geo["scale_y"]
    g_axes = [
        [px * g_one[k] for k in range(3)],
        [py * g_two[k] for k in range(3)],
        [-(px * u * g_one[k] + py * v * g_two[k]) for k in range(3)],
    ]
    g_px = sum(g_one[k] * geo["lean_x"][k] for k in range(3))
    g_py = sum(g_two[k] * geo["lean_y"][k] for k in range(3))
    g_u = focal_x * (ca * sx + cb * sy) - px * sum(g_one[k] * axes[2][k] for k in range(3))
    g_v = focal_y * (cc * sy + cb * sx) - py * sum(g_two[k] * axes[2][k] for k in range(3))
    view = geo["view"]
    g_inverse = focal_x * g_px + focal_y * g_py + view[0] * g_u + view[1] * g_v
    g_view = [inverse * g_u, inverse * g_v, -inverse * inverse * g_inverse]
    g_spread = [
        [sum(rot[i][j] * g_axes[i][k] for i in range(3)) for k in range(3)] for j in range(3)
    ]
    for k in range(3):
        grads[3 + k] = sum(g_spread[j][k] * geo["spread"][j][k] for j in range(3))
    g = [[g_spread[j][k] * geo["scales"][k] for k in range(3)] for j in range(3)]
    w, x, y, z = geo["unit"]
    g_w = 2.0 * (z * (g[1][0] - g[0][1]) + y * (g[0][2] - g[2][0]) + x * (g[2][1] - g[1][2]))
    g_x = 2.0 * (
        y * (g[0][1] + g[1][0])
        + z * (g[0][2] + g[2][0])
        + w * (g[2][1] - g[1][2])
        - 2.0 * x * (g[1][1] + g[2][2])
    )
    g_y = 2.0 * (
        x * (g[0][1] + g[1][0])
        + z * (g[1][2] + g[2][1])
        + w * (g[0][2] - g[2][0])
        - 2.0 * y * (g[0][0] + g[2][2])
    )
    g_z = 2.0 * (
        x * (g[0][2] + g[2][0])
        + y * (g[1][2] + g[2][1])
        + w * (g[1][0] - g[0][1])
        - 2.0 * z * (g[0][0] + g[1][1])
    )
    along = w * g_w + x * g_x + y * g_y + z * g_z
    for p, (g_q, q) in enumerate(((g_w, w), (g_x, x), (g_y, y), (g_z, z))):
        grads[6 + p] = (g_q - q * along) * geo["norm"]
    x, y, z = geo["toward"]
    basis = harmonic_basis(x, y, z)
    h = [None]
    for k in range(16):
        if k:
            h.append(sum(drawn[c] * row(11 + 3 * k + c) for c in range(3)))
        for c in range(3):
            grads[11 + 3 * k + c] = basis[k] * drawn[c]
    a, d = sh_two, sh_three
    xx, yy, zz, xy, yz, xz = x * x, y * y, z * z, x * y, y * z, x * z
    g_dx = (
        -sh_one * h[3] + a[0] * y * h[4] - 2.0 * a[2] * x * h[6] + a[3] * z * h[7]
        + 2.0 * a[4] * x * h[8] + 6.0 * d[0] * xy * h[9] + d[1] * yz * h[10]
        - 2.0 * d[2] * xy * h[11] - 6.0 * d[3] * xz * h[12]
        + d[4] * (4.0 * zz - 3.0 * xx - yy) * h[13] + 2.0 * d[5] * xz * h[14]
        + 3.0 * d[6] * (xx - yy) * h[15]
    )
    g_dy = (
        -sh_one * h[1] + a[0] * x * h[4] + a[1] * z * h[5] - 2.0 * a[2] * y * h[6]
        - 2.0 * a[4] * y * h[8] + 3.0 * d[0] * (xx - yy) * h[9] + d[1] * xz * h[10]
        + d[2] * (4.0 * zz - xx - 3.0 * yy) * h[11] - 6.0 * d[3] * yz * h[12]
        - 2.0 * d[4] * xy * h[13] - 2.0 * d[5] * yz * h[14] - 6.0 * d[6] * xy * h[15]
    )
    g_dz = (
        sh_one * h[2] + a[1] * y * h[5] + 4.0 * a[2] * z * h[6] + a[3] * x * h[7]
        + d[1] * xy * h[10] + 8.0 * d[2] * yz * h[11]
        + 3.0 * d[3] * (2.0 * zz - xx - yy) * h[12] + 8.0 * d[4] * xz * h[13]
        + d[5] * (xx - yy) * h[14]
    )
    along = x * g_dx + y * g_dy + z * g_dz
    turned = [(gd - t * along) * geo["shrink"] for gd, t in ((g_dx, x), (g_dy, y), (g_dz, z))]
    for j in range(3):
        grads[j] = sum(rot[i][j] * g_view[i] for i in range(3)) + turned[j]
    for b in range(blocks):
        mine = place == b
        for p in range(params):
            grad[p * blocks + b : p * blocks + b + 1, :] = jnp.sum(
                jnp.where(mine, grads[p], 0.0), axis=0, keepdims=True
            )

    for p in range(params):
        here = slice(p * blocks, (p + 1) * blocks)
        new = base_ref[p] - steps_ref[p] * grad[here, :]
        shifted = new + dual_ref[p]
        new_ref[p] = new
        shifted_ref[p] = shifted
        moved[here, :] = shifted
    shifted = jnp.concatenate(
        [moved[pl.ds(b, params, stride=blocks), :] for b in range(blocks)], axis=1
    )
    for n in range(pick_ref.shape[0]):
        value = exact_pick(shifted, pick_ref[n])
        for b in range(blocks):
            moved[pl.ds(b, params, stride=blocks), :] = value[:, b * LANES : (b + 1) * LANES]
        for p in range(params):
            sent_ref[n, p] = moved[p * blocks : (p + 1) * blocks, :]


def constants(pixels):
    place = np.arange(pixels)
    x = (place % LANES - 64).astype(np.float32)
    y = (place // LANES - 4).astype(np.float32)
    square = (x * x).astype(jnp.bfloat16).astype(np.float32)
    part = np.zeros((PART, pixels + 3 * LANES), np.float32)
    for c, value in enumerate([square, x * y, y * y, x, y, np.ones_like(x)]):
        part[c, :pixels] = value
    part[COEFS, :pixels] = x * x - square
    for c in range(3):
        part[COEFS - 3 + c, pixels + c * LANES : pixels + (c + 1) * LANES] = 1.0
    basis = np.concatenate([part] * 3)
    return jnp.asarray(basis, jnp.bfloat16)


def vmem(number=1):
    return [pl.BlockSpec(memory_space=pltpu.VMEM)] * number


def smem(number=1):
    return [pl.BlockSpec(memory_space=pltpu.SMEM)] * number


def params_with(mib):
    return pltpu.CompilerParams(vmem_limit_bytes=mib * 2**20)


def on_device(
    gaussians, consensus, duals, step_sizes, cameras, camera_ids, block_lists, depth_order,
    block_counts, targets, intersection,
):
    own, prior, dual = [value[0].swapaxes(0, 1) for value in (gaussians, consensus, duals)]
    params, blocks = own.shape[0], own.shape[1]
    peers = lax.axis_size("tile")
    me = lax.axis_index("tile")[None]
    listed = block_lists.shape[2]
    pixels = targets.shape[3]
    yrows = pixels // LANES
    outer = peers // INNER
    f32 = jnp.float32
    shape_of = jax.ShapeDtypeStruct
    basis = constants(pixels)

    def swap(value, mask):
        return lax.ppermute(value, "tile", [(i, i ^ mask) for i in range(peers)])

    hop_bits = list(reversed(range(2, peers.bit_length() - 1)))
    mine, pack = pl.pallas_call(
        pack_kernel,
        out_shape=(
            shape_of((1, 16 + listed), f32),
            shape_of((1, 3 * listed), jnp.int32),
        ),
        in_specs=vmem(5),
        out_specs=tuple(vmem(2)),
        compiler_params=params_with(8),
        name="pack",
    )(camera_ids, block_counts, block_lists[0], depth_order[0], cameras)
    held = pl.pallas_call(
        hold_kernel,
        out_shape=shape_of(own.shape, f32),
        in_specs=vmem(),
        out_specs=vmem()[0],
        compiler_params=params_with(8),
        name="hold",
    )(own)
    ids = mine
    everything = held[None]
    masks = [0]
    for step, bit in enumerate(hop_bits):
        arrived = swap(own[None] if step == 0 else everything, 1 << bit)
        if step < 2:
            ids = jnp.concatenate([ids, swap(ids, 1 << step)], 0)
        everything = jnp.concatenate([everything, arrived], 0)
        masks += [mask | (1 << bit) for mask in masks]

    group_total = lax.axis_size("scene")
    group = lax.axis_index("scene")[None]
    share = intersection[0, 0]
    if group_total == 2:
        routes = [[(0, 1), (1, 0)]]
        links = [(lambda g: g == 0, lambda g: g >= 0)]
    else:
        routes = [
            [(g + 1, g) for g in range(group_total - 1)],
            [(g, g + 1) for g in range(group_total - 1)],
        ]
        links = [
            (lambda g: g >= 0, lambda g: g < group_total - 1),
            (lambda g: g < 0, lambda g: g > 0),
        ]
    lists = [lax.ppermute(share, "scene", route) for route in routes]

    base, steps, pick, mask = pl.pallas_call(
        functools.partial(prepare_kernel, links),
        out_shape=(
            shape_of(own.shape, f32),
            shape_of(own.shape, f32),
            shape_of((len(links), blocks * LANES, blocks * LANES), jnp.bfloat16),
            shape_of((len(links), blocks, LANES), f32),
        ),
        in_specs=smem() + vmem(3) + smem() + vmem(1 + len(links)),
        out_specs=tuple(vmem(4)),
        compiler_params=params_with(8),
        name="prepare",
    )(group, held, prior, dual, step_sizes, share, *lists)

    messages = pl.pallas_call(
        functools.partial(project_kernel, masks, yrows, listed),
        out_shape=tuple([shape_of((COEFS * outer, LANES), f32)] * INNER),
        in_specs=smem() + vmem(2),
        out_specs=tuple(vmem(INNER)),
        scratch_shapes=[pltpu.VMEM((COEFS * outer * INNER, LANES), f32)],
        compiler_params=params_with(8),
        name="project",
    )(me, everything, ids)
    sources = [messages[0]] + [swap(messages[j], j) for j in range(1, INNER)]

    outbox = pl.pallas_call(
        functools.partial(render_kernel, pixels, blocks, listed, hop_bits),
        out_shape=shape_of((peers, MSG, LANES), f32),
        in_specs=smem(2) + vmem(INNER + 3),
        out_specs=vmem()[0],
        scratch_shapes=[
            pltpu.VMEM((COEFS * peers, LANES), f32),
            pltpu.VMEM(((listed + 1) * KDIM, LANES), f32),
            pltpu.VMEM(((listed + 1) * LANES, KDIM), jnp.bfloat16),
            pltpu.VMEM(((listed + 1) * LANES, 3 * LANES), f32),
            pltpu.VMEM((LANES, pixels), f32),
            pltpu.VMEM((LANES, pixels), f32),
            pltpu.VMEM(((listed + 1) * LANES, pixels), f32),
            pltpu.VMEM(((listed + 1) * LANES, pixels), f32),
            pltpu.VMEM((yrows, SUB, LANES), f32),
            pltpu.VMEM((listed + 1, yrows, SUB, LANES), f32),
            pltpu.VMEM((listed + 1, yrows, SUB, LANES), f32),
            pltpu.VMEM((listed + 1, 3, yrows, SUB, LANES), f32),
            pltpu.VMEM((3, yrows, SUB, LANES), f32),
            pltpu.VMEM((KDIM, pixels), f32),
            pltpu.VMEM((KDIM, pixels), jnp.bfloat16),
            pltpu.VMEM((yrows, SUB, LANES), f32),
            pltpu.VMEM((MOMENTS * LANES, LANES), f32),
            pltpu.VMEM((MOMENTS * LANES, LANES), f32),
            pltpu.VMEM((listed + 4, SUB, MOMENTS * LANES), f32),
            pltpu.VMEM((listed * MSG, LANES), f32),
            pltpu.SMEM((listed,), jnp.int32),
        ],
        compiler_params=params_with(48),
        name="render",
    )(
        me, pack, mine, *sources, targets[0, 0], basis,
    )
    inbox = lax.all_to_all(outbox, "tile", split_axis=0, concat_axis=0, tiled=True)
    updated, shifted, sent = pl.pallas_call(
        owner_kernel,
        out_shape=(
            shape_of(own.shape, f32),
            shape_of(own.shape, f32),
            shape_of((len(links),) + own.shape, f32),
        ),
        in_specs=vmem(6),
        out_specs=tuple(vmem(3)),
        scratch_shapes=[pltpu.VMEM((params * blocks, LANES), f32)] * 2,
        compiler_params=params_with(16),
        name="owner",
    )(inbox.reshape(peers * MSG, LANES), held, base, dual, steps, pick)
    new_duals = jnp.zeros_like(shifted)
    for n, route in enumerate(routes):
        theirs = lax.ppermute(sent[n], "scene", route)
        change = shifted - 0.5 * (shifted + theirs)
        new_duals = jnp.where(mask[n] > 0.5, change, new_duals)
    return updated.swapaxes(0, 1)[None], new_duals.swapaxes(0, 1)[None]


def solution(mesh):
    placed = (
        P("scene", "tile", None, None),
        P("scene", "tile", None, None),
        P("scene", "tile", None, None),
        P(),
        P(),
        P("scene", "tile"),
        P("scene", "tile", None),
        P("scene", "tile", None),
        P("scene", "tile"),
        P("scene", "tile", None, None),
        P("scene", "tile", None, None),
    )
    return jax.shard_map(
        on_device,
        mesh=mesh,
        in_specs=placed,
        out_specs=(P("scene", "tile", None, None), P("scene", "tile", None, None)),
        check_vma=False,
    )
```

```python
import functools

import jax
import jax.numpy as jnp
import numpy as np
from jax import lax
from jax.experimental import pallas as pl
from jax.experimental.pallas import tpu as pltpu
from jax.sharding import PartitionSpec as P

penalty_weight = 0.5
blur_floor = 0.3
alpha_ceiling = 0.99
log2e = 1.4426950408889634
sh_zero = 0.28209479177387814
sh_one = 0.4886025119029199
sh_two = (
    1.0925484305920792,
    -1.0925484305920792,
    0.31539156525252005,
    -1.0925484305920792,
    0.5462742152960396,
)
sh_three = (
    -0.5900435899266435,
    2.890611442640554,
    -0.4570457994644658,
    0.3731763325901154,
    -0.4570457994644658,
    1.445305721320277,
    -0.5900435899266435,
)

LANES = 128
SUB = 8
PART = 16
KDIM = 3 * PART
COEFS = 9
INNER = 4
MOMENTS = 6
WIDE = 256
MSG = 16
highest = lax.Precision.HIGHEST


def harmonic_basis(x, y, z):
    xx, yy, zz = x * x, y * y, z * z
    return [
        sh_zero + 0.0 * x,
        -sh_one * y,
        sh_one * z,
        -sh_one * x,
        sh_two[0] * x * y,
        sh_two[1] * y * z,
        sh_two[2] * (2.0 * zz - xx - yy),
        sh_two[3] * x * z,
        sh_two[4] * (xx - yy),
        sh_three[0] * y * (3.0 * xx - yy),
        sh_three[1] * x * y * z,
        sh_three[2] * y * (4.0 * zz - xx - yy),
        sh_three[3] * z * (2.0 * zz - 3.0 * xx - 3.0 * yy),
        sh_three[4] * x * (4.0 * zz - xx - yy),
        sh_three[5] * z * (xx - yy),
        sh_three[6] * x * (xx - 3.0 * yy),
    ]


def geometry(row, cam):
    mean = [row(0), row(1), row(2)]
    rot = [[cam[3 * i + j] for j in range(3)] for i in range(3)]
    shift = [cam[9 + i] for i in range(3)]
    focal_x, focal_y = cam[12], cam[13]
    view = [
        rot[i][0] * mean[0] + rot[i][1] * mean[1] + rot[i][2] * mean[2] + shift[i] for i in range(3)
    ]
    inverse = 1.0 / view[2]
    u = view[0] * inverse
    v = view[1] * inverse
    quat = [row(6 + i) for i in range(4)]
    norm = lax.rsqrt(sum(q * q for q in quat))
    w, x, y, z = [q * norm for q in quat]
    turn = [
        [1.0 - 2.0 * (y * y + z * z), 2.0 * (x * y - w * z), 2.0 * (x * z + w * y)],
        [2.0 * (x * y + w * z), 1.0 - 2.0 * (x * x + z * z), 2.0 * (y * z - w * x)],
        [2.0 * (x * z - w * y), 2.0 * (y * z + w * x), 1.0 - 2.0 * (x * x + y * y)],
    ]
    scales = [jnp.exp(row(3 + k)) for k in range(3)]
    spread = [[turn[j][k] * scales[k] for k in range(3)] for j in range(3)]
    axes = [
        [sum(rot[i][j] * spread[j][k] for j in range(3)) for k in range(3)] for i in range(3)
    ]
    scale_x = focal_x * inverse
    scale_y = focal_y * inverse
    lean_x = [axes[0][k] - u * axes[2][k] for k in range(3)]
    lean_y = [axes[1][k] - v * axes[2][k] for k in range(3)]
    row_one = [scale_x * lean_x[k] for k in range(3)]
    row_two = [scale_y * lean_y[k] for k in range(3)]
    cov_xx = sum(a * a for a in row_one) + blur_floor
    cov_xy = sum(a * b for a, b in zip(row_one, row_two))
    cov_yy = sum(b * b for b in row_two) + blur_floor
    scale = 1.0 / (cov_xx * cov_yy - cov_xy * cov_xy)
    conic = (cov_yy * scale, -cov_xy * scale, cov_xx * scale)
    eye = [-(rot[0][i] * shift[0] + rot[1][i] * shift[1] + rot[2][i] * shift[2]) for i in range(3)]
    away = [mean[i] - eye[i] for i in range(3)]
    shrink = lax.rsqrt(sum(a * a for a in away))
    toward = [a * shrink for a in away]
    return dict(
        rot=rot,
        view=view,
        inverse=inverse,
        u=u,
        v=v,
        norm=norm,
        unit=(w, x, y, z),
        scales=scales,
        spread=spread,
        axes=axes,
        scale_x=scale_x,
        scale_y=scale_y,
        lean_x=lean_x,
        lean_y=lean_y,
        row_one=row_one,
        row_two=row_two,
        conic=conic,
        shrink=shrink,
        toward=toward,
    )


def three_parts(value):
    high = value.astype(jnp.bfloat16).astype(jnp.float32)
    rest = value - high
    mid = rest.astype(jnp.bfloat16).astype(jnp.float32)
    return high, mid, rest - mid


def exact_pick(value, pick):
    high, mid, low = [part.astype(jnp.bfloat16) for part in three_parts(value)]
    dot = functools.partial(jnp.dot, preferred_element_type=jnp.float32)
    return (dot(high, pick) + dot(mid, pick)) + dot(low, pick)


def segment_order(back):
    shape = (LANES, LANES)
    gauss = lax.broadcasted_iota(jnp.int32, shape, int(back))
    place = lax.broadcasted_iota(jnp.int32, shape, 1 - int(back))
    return (gauss == (place % SUB) * (LANES // SUB) + place // SUB).astype(jnp.bfloat16)


def sub_roll(value, shift):
    return pltpu.roll(value, shift % SUB, 0)


def prepare_kernel(
    links, group_ref, own_ref, cons_ref, dual_ref, step_ref, share_ref, *refs
):
    others, (base_ref, steps_ref, pick_ref, mask_ref) = refs[: len(links)], refs[len(links) :]
    params, blocks = own_ref.shape[0], own_ref.shape[1]
    group = group_ref[0]
    for p in range(params):
        step = step_ref[p]
        here = own_ref[p]
        steps_ref[p] = jnp.full((blocks, LANES), step)
        base_ref[p] = here - step * (penalty_weight * (here - cons_ref[p] + dual_ref[p]))
    half = share_ref.shape[1]
    local = lax.broadcasted_iota(jnp.int32, (blocks * LANES, half), 0)
    contract = (((1,), (1,)), ((), ()))
    for n, (side_of, exists_of) in enumerate(links):
        other = others[n]
        up = side_of(group)
        mine = jnp.where(up, share_ref[0:1, :], share_ref[1:2, :])
        theirs = jnp.where(up, other[1:2, :], other[0:1, :])
        source = (local == mine).astype(jnp.bfloat16)
        target = (local == theirs).astype(jnp.bfloat16)
        pick_ref[n] = lax.dot_general(
            source, target, contract, preferred_element_type=jnp.float32
        ).astype(jnp.bfloat16)
        there = jnp.full((SUB, half), jnp.where(exists_of(group), 1.0, 0.0)).astype(jnp.bfloat16)
        mask = lax.dot_general(there, source, contract, preferred_element_type=jnp.float32)
        for b in range(blocks):
            mask_ref[n, b : b + 1, :] = mask[0:1, b * LANES : (b + 1) * LANES]


def hold_kernel(own_ref, held_ref):
    held_ref[...] = own_ref[...]


def pack_kernel(camera_ref, count_ref, list_ref, depth_ref, cameras_ref, mine_ref, pack_ref):
    listed = list_ref.shape[1]
    blocks = list_ref[...]
    shape = cameras_ref.shape
    chosen = lax.broadcasted_iota(jnp.int32, shape, 0) == jnp.broadcast_to(camera_ref[...], shape)
    mine_ref[:, :16] = jnp.sum(jnp.where(chosen, cameras_ref[...], 0.0), axis=0, keepdims=True)
    mine_ref[:, 16:] = blocks.astype(jnp.float32)
    pack_ref[:, :listed] = blocks
    pack_ref[:, listed : 2 * listed] = depth_ref[...]
    pack_ref[:, 2 * listed :] = jnp.broadcast_to(count_ref[...], (1, listed))


def project_kernel(masks, yrows, listed, me_ref, raw_ref, ids_ref, *refs):
    outs, feat = refs[:INNER], refs[INNER]
    outer = len(masks)
    blocks = raw_ref.shape[2]
    me = me_ref[0]
    ids = jnp.concatenate([ids_ref[...]] * (SUB // INNER), axis=0)
    lane = lax.broadcasted_iota(jnp.int32, (SUB, LANES), 1)
    sub = lax.broadcasted_iota(jnp.int32, (SUB, LANES), 0)
    cam = [jnp.broadcast_to(ids[:, k : k + 1], (SUB, LANES)) for k in range(16)]
    top = (((me & 3) ^ (sub & 3)) * yrows).astype(jnp.float32)
    lists = ids[:, 16 : 16 + listed]
    rows = outer * INNER
    for v in range(rows // SUB):
        owners = [2 * v, 2 * v + 1]
        first = jnp.where(sub < INNER, (me ^ masks[owners[0]]) * blocks, (me ^ masks[owners[1]]) * blocks)
        found = []
        for b in range(1, blocks):
            same = (lists == (first[:, :listed] + b).astype(jnp.float32)).astype(jnp.float32)
            found.append(jnp.broadcast_to(jnp.max(same, axis=1, keepdims=True), (SUB, LANES)) > 0.5)

        def row(p):
            def of(b):
                return jnp.where(
                    sub < INNER,
                    jnp.broadcast_to(raw_ref[owners[0], p, b : b + 1, :], (SUB, LANES)),
                    jnp.broadcast_to(raw_ref[owners[1], p, b : b + 1, :], (SUB, LANES)),
                )

            value = of(0)
            for b in range(1, blocks):
                value = jnp.where(found[b - 1], of(b), value)
            return value

        geo = geometry(row, cam)
        sx = cam[12] * geo["u"] + (cam[14] - 64.0)
        sy = cam[13] * geo["v"] + (cam[15] - top - 4.0)
        basis = harmonic_basis(*geo["toward"])
        tint = [sum(basis[k] * row(11 + 3 * k + c) for k in range(16)) + 0.5 for c in range(3)]
        lo = -jnp.log(1.0 + jnp.exp(-row(10))) * log2e
        ca, cb, cc = geo["conic"]
        kxx = (-0.5 * log2e) * ca
        kxy = -log2e * cb
        kyy = (-0.5 * log2e) * cc
        kx = -2.0 * kxx * sx - kxy * sy
        ky = -2.0 * kyy * sy - kxy * sx
        k1 = kxx * sx * sx + kxy * sx * sy + kyy * sy * sy + lo
        for m, value in enumerate([kxx, kxy, kyy, kx, ky, k1, *tint]):
            feat[m * rows + v * SUB : m * rows + (v + 1) * SUB, :] = value
    feat[...] = exact_pick(feat[...], segment_order(False))
    for j in range(INNER):
        outs[j][...] = feat[pl.ds(j, COEFS * outer, stride=INNER), :]


def render_kernel(
    pixels, blocks, listed, hop_bits, me_ref, pack_ref, ids_ref, src0, src1, src2, src3, target_ref,
    basis_ref, out_ref,
    raw, coef, lefts, shade, gaps_a, gaps_b, alphas, weights, carry, before, passed,
    colours, resid, mirror, pulls, behind, sums_a, sums_b, found, rows, slots,
):
    peers = out_ref.shape[0]
    outer = peers // INNER
    per_owner = blocks
    yrows = pixels // LANES
    groups = LANES // SUB
    me = me_ref[0]
    count = pack_ref[0, 2 * listed]
    top = ((me % 4) * yrows).astype(jnp.float32)

    def place_slot(j, ends):
        live_end, dead_end = ends
        slot = pack_ref[0, listed + j]
        live = slot < count
        slots[jnp.where(live, live_end, dead_end)] = slot
        return jnp.where(live, live_end + 1, live_end), jnp.where(live, dead_end, dead_end + 1)

    lax.fori_loop(0, listed, place_slot, (jnp.int32(0), count))

    for j, src in enumerate((src0, src1, src2, src3)):
        raw[j * COEFS * outer : (j + 1) * COEFS * outer, :] = src[...]
    coef[...] = jnp.zeros(coef.shape, jnp.float32)
    for k in range(coef.shape[0] // KDIM):
        coef[k * KDIM + 5 : k * KDIM + 6, :] = jnp.full((1, LANES), -4096.0)

    def fetch(k, _):
        apart = me ^ (pack_ref[0, slots[k]] // per_owner)
        near = sum((((apart >> bit) & 1) << t) for t, bit in enumerate(hop_bits))
        start = (apart & (INNER - 1)) * (COEFS * outer) + near
        value = raw[pl.ds(start, COEFS, stride=outer), :]
        for part, piece in enumerate(three_parts(value)):
            base = pl.multiple_of(k * KDIM + part * PART, PART)
            coef[pl.ds(base, COEFS), :] = piece
            coef[pl.ds(base + COEFS, 1), :] = piece[0:1, :]
            coef[pl.ds(base + COEFS + 1, 3), :] = piece[COEFS - 3 : COEFS, :]
        return 0

    lax.fori_loop(0, count, fetch, 0)

    sub = lax.broadcasted_iota(jnp.int32, (SUB, LANES), 0)
    one = jnp.ones((SUB, LANES), jnp.float32)
    none = jnp.zeros((SUB, LANES), jnp.float32)
    row_sets = [range(yrows // 2), range(yrows // 2, yrows)]
    for y in range(yrows):
        carry[y] = one
        behind[y] = none
        for c in range(3):
            resid[c, y] = none

    def spread_row(value, index):
        return jnp.broadcast_to(value[index : index + 1, :], (SUB, LANES))

    def rows_at(start, size, step):
        return pl.ds(pl.multiple_of(start, step), size)

    for k in range(coef.shape[0] // KDIM):
        mine = coef[k * KDIM : (k + 1) * KDIM, :].T
        lefts[k * LANES : (k + 1) * LANES, :] = mine.astype(jnp.bfloat16)

    def left(k):
        return lefts[rows_at(k * LANES, LANES, LANES), :]

    def times(mine, right, start, width):
        here = slice(start, start + width)
        return jnp.dot(mine, right[:, here], preferred_element_type=jnp.float32)

    def chain(k):
        base = pl.multiple_of(k * LANES, LANES)
        mine = left(k)
        for start in range(0, pixels, WIDE):
            value = jnp.minimum(alpha_ceiling, jnp.exp2(times(mine, basis_ref, start, WIDE)))
            kept = [one] * (WIDE // LANES)
            for i in range(groups):
                here = rows_at(base + i * SUB, SUB, SUB)
                for j in range(WIDE // LANES):
                    alpha = value[i * SUB : (i + 1) * SUB, j * LANES : (j + 1) * LANES]
                    weight = alpha * kept[j]
                    lanes = slice(start + j * LANES, start + (j + 1) * LANES)
                    alphas[here, lanes] = alpha
                    weights[here, lanes] = weight
                    kept[j] = kept[j] - weight
            for j in range(WIDE // LANES):
                passed[k, start // LANES + j] = kept[j]
        shade[rows_at(k * LANES, LANES, LANES), :] = times(mine, basis_ref, pixels, 3 * LANES)

    def tally(k, ended):
        base = pl.multiple_of(k * LANES, LANES)
        for some in row_sets:
            total = [[last - last for last in ends] for ends in ended]
            for i in range(groups):
                here = rows_at(base + i * SUB, SUB, SUB)
                tints = [shade[here, c * LANES : (c + 1) * LANES] for c in range(3)]
                for j, y in enumerate(some):
                    weight = weights[here, y * LANES : (y + 1) * LANES]
                    for c in range(3):
                        total[c][j] = total[c][j] + weight * tints[c]
            for j, y in enumerate(some):
                through = passed[k, y]
                for step in (1, 2, 4):
                    through = through * jnp.where(sub >= step, sub_roll(through, step), 1.0)
                entering = carry[y]
                ahead = entering * jnp.where(sub >= 1, sub_roll(through, 1), 1.0)
                before[k, y] = ahead
                carry[y] = entering * spread_row(through, SUB - 1)
                for c in range(3):
                    colours[k, c, y] = total[c][j]
                    resid[c, y] = resid[c, y] + ahead * total[c][j]
            ended = total
        return ended

    pairs = (count + 1) // 2
    fresh = [[none] * (yrows // 2)] * 3
    chain(0)
    chain(1)

    def forward(pair, _):
        tally(2 * pair - 1, tally(2 * pair - 2, fresh))
        chain(2 * pair)
        chain(2 * pair + 1)
        return 0

    lax.fori_loop(1, pairs, forward, 0)
    tally(2 * pairs - 1, tally(2 * pairs - 2, fresh))

    mirror[...] = jnp.zeros(mirror.shape, jnp.float32)
    for y in range(yrows):
        for c in range(3):
            value = jnp.sum(resid[c, y], axis=0, keepdims=True)
            value = value - target_ref[c : c + 1, y * LANES : (y + 1) * LANES]
            resid[c, y] = jnp.broadcast_to(value, (SUB, LANES))
            high, low, _ = three_parts(value)
            for piece in range(3):
                lanes = slice(y * LANES, (y + 1) * LANES)
                at = piece * PART + COEFS - 3 + c
                mirror[at : at + 1, lanes] = high
                if piece < 2:
                    mirror[at + 4 : at + 5, lanes] = low
    pulls[...] = mirror[...].astype(jnp.bfloat16)

    def follow(k, gaps):
        base = pl.multiple_of(k * LANES, LANES)
        rear = [None] * yrows
        for y in range(yrows):
            gain = passed[k, y]
            value = sum(colours[k, c, y] * resid[c, y] for c in range(3))
            for step in (1, 2, 4):
                inside = sub < SUB - step
                value = value + gain * jnp.where(inside, sub_roll(value, -step), 0.0)
                gain = gain * jnp.where(inside, sub_roll(gain, -step), 1.0)
            last = behind[y]
            rear[y] = jnp.where(
                sub < SUB - 1, sub_roll(value, -1) + sub_roll(gain, -1) * last, last
            )
            behind[y] = spread_row(value + gain * last, 0)
        mine = left(k)
        for start in range(0, pixels, WIDE):
            value = times(mine, pulls, start, WIDE)
            for i in reversed(range(groups)):
                here = slice(i * SUB, (i + 1) * SUB)
                for j in range(WIDE // LANES):
                    y = start // LANES + j
                    lanes = slice(y * LANES, (y + 1) * LANES)
                    gap = value[here, j * LANES : (j + 1) * LANES] - rear[y]
                    gaps[here, lanes] = gap
                    rear[y] = rear[y] + alphas[rows_at(base + i * SUB, SUB, SUB), lanes] * gap

    def weigh(k, gaps, sums):
        base = pl.multiple_of(k * LANES, LANES)
        front = [before[k, y] for y in range(yrows)]
        for i in range(groups):
            at = slice(i * SUB, (i + 1) * SUB)
            here = rows_at(base + i * SUB, SUB, SUB)
            run = [none] * MOMENTS
            for y in range(yrows):
                lanes = slice(y * LANES, (y + 1) * LANES)
                weight = weights[here, lanes] * front[y]
                slope = jnp.where(alphas[here, lanes] < alpha_ceiling, weight * gaps[at, lanes], 0.0)
                run[0] = run[0] + slope
                run[1] = run[1] + run[0]
                run[2] = run[2] + run[1]
                for c in range(3):
                    run[3 + c] = run[3 + c] + weight * resid[c, y]
            for m, value in enumerate(run):
                sums[m * LANES + i * SUB : m * LANES + (i + 1) * SUB, :] = value

    across = (lax.broadcasted_iota(jnp.int32, (SUB, LANES), 1) - 64).astype(jnp.float32)
    square = across * across
    coarse = square.astype(jnp.bfloat16).astype(jnp.float32)
    xmom = jnp.where(sub == 0, one, jnp.where(sub == 1, across, none))
    xmom = jnp.where(sub == 2, coarse, jnp.where(sub == 3, square - coarse, xmom))
    xmom = xmom.astype(jnp.bfloat16)

    def moments(k, sums):
        value = sums[...]
        high = value.astype(jnp.bfloat16)
        low = (value - high.astype(jnp.float32)).astype(jnp.bfloat16)
        contract = (((1,), (1,)), ((), ()))
        found[k] = lax.dot_general(
            xmom, high, contract, preferred_element_type=jnp.float32
        ) + lax.dot_general(xmom, low, contract, preferred_element_type=jnp.float32)

    rearmost = 2 * pairs - 1

    def backward(pair, _):
        k = rearmost - 2 * pair
        moments(k + 4, sums_a)
        weigh(k + 2, gaps_a, sums_a)
        follow(k, gaps_a)
        moments(k + 3, sums_b)
        weigh(k + 1, gaps_b, sums_b)
        follow(k - 1, gaps_b)
        return 0

    follow(rearmost, gaps_a)
    follow(rearmost - 1, gaps_b)
    lax.fori_loop(1, pairs, backward, 0)
    moments(3, sums_a)
    weigh(1, gaps_a, sums_a)
    moments(2, sums_b)
    weigh(0, gaps_b, sums_b)
    moments(1, sums_a)
    moments(0, sums_b)

    lane = lax.broadcasted_iota(jnp.int32, (1, LANES), 1)
    camera = jnp.concatenate([ids_ref[...], jnp.zeros((1, LANES - ids_ref.shape[1]), jnp.float32)], 1)
    meta = jnp.where(lane < 16, camera, jnp.where(lane == 17, top, 0.0))

    rows[...] = jnp.zeros(rows.shape, jnp.float32)

    def gather_moments(k, _):
        part = lambda order, m: found[k, order : order + 1, m * LANES : (m + 1) * LANES]
        rise = yrows - 4.0
        s0, x1, x2 = part(0, 0), part(1, 0), part(2, 0) + part(3, 0)
        t1, tx, t2 = part(0, 1), part(1, 1), 2.0 * part(0, 2) - part(0, 1)
        answer = [s0, x1, rise * s0 - t1, x2, rise * x1 - tx, rise * (rise * s0 - 2.0 * t1) + t2]
        answer += [part(0, 3 + c) for c in range(3)]
        for m, value in enumerate(answer):
            rows[pl.ds(k * MSG + m, 1), :] = value
        return 0

    lax.fori_loop(0, count, gather_moments, 0)
    rows[...] = exact_pick(rows[...], segment_order(True))

    if peers > listed:
        absent = jnp.where(lane == 16, -1.0, 0.0)
        for peer in range(peers):
            out_ref[peer] = jnp.broadcast_to(absent, (MSG, LANES))

    def send(k, _):
        block = pack_ref[0, slots[k]]
        owner = block // per_owner
        place = (block % per_owner).astype(jnp.float32)
        rows[pl.ds(k * MSG + 9, 1), :] = jnp.where(lane == 16, place, meta)
        out_ref[owner] = rows[pl.ds(pl.multiple_of(k * MSG, MSG), MSG), :]
        return 0

    lax.fori_loop(0, listed, send, 0)


def owner_kernel(
    inbox_ref, own_ref, base_ref, dual_ref, steps_ref, pick_ref, new_ref, shifted_ref, sent_ref,
    grad, moved
):
    params, blocks = own_ref.shape[0], own_ref.shape[1]
    strips = inbox_ref.shape[0] // MSG

    def message(m):
        return inbox_ref[pl.ds(m, strips, stride=MSG), :]

    meta = message(9)
    cam = [jnp.broadcast_to(meta[:, k : k + 1], (strips, LANES)) for k in range(18)]
    place, top = cam[16], cam[17]

    def row(p):
        value = jnp.broadcast_to(own_ref[p, 0:1, :], (strips, LANES))
        for b in range(1, blocks):
            value = jnp.where(place == b, own_ref[p, b : b + 1, :], value)
        return value

    geo = geometry(row, cam)
    u, v, inverse = geo["u"], geo["v"], geo["inverse"]
    focal_x, focal_y = cam[12], cam[13]
    at_x = focal_x * u + (cam[14] - 64.0)
    at_y = focal_y * v + (cam[15] - top - 4.0)
    s0, x1, y1, x2, xy, y2, *drawn = [message(m) for m in range(9)]
    sx = x1 - at_x * s0
    sy = y1 - at_y * s0
    sxx = x2 - at_x * (x1 + sx)
    sxy = xy - at_x * y1 - at_y * sx
    syy = y2 - at_y * (y1 + sy)
    ca, cb, cc = geo["conic"]
    axes, rot = geo["axes"], geo["rot"]
    grads = {}
    opacity = 1.0 / (1.0 + jnp.exp(-row(10)))
    grads[10] = s0 * (1.0 - opacity)
    t00, t01 = sxx * ca + sxy * cb, sxx * cb + sxy * cc
    t10, t11 = sxy * ca + syy * cb, sxy * cb + syy * cc
    g_xx = 0.5 * (ca * t00 + cb * t10)
    g_xy = ca * t01 + cb * t11
    g_yy = 0.5 * (cb * t01 + cc * t11)
    one, two = geo["row_one"], geo["row_two"]
    g_one = [2.0 * g_xx * one[k] + g_xy * two[k] for k in range(3)]
    g_two = [2.0 * g_yy * two[k] + g_xy * one[k] for k in range(3)]
    px, py = geo["scale_x"], geo["scale_y"]
    g_axes = [
        [px * g_one[k] for k in range(3)],
        [py * g_two[k] for k in range(3)],
        [-(px * u * g_one[k] + py * v * g_two[k]) for k in range(3)],
    ]
    g_px = sum(g_one[k] * geo["lean_x"][k] for k in range(3))
    g_py = sum(g_two[k] * geo["lean_y"][k] for k in range(3))
    g_u = focal_x * (ca * sx + cb * sy) - px * sum(g_one[k] * axes[2][k] for k in range(3))
    g_v = focal_y * (cc * sy + cb * sx) - py * sum(g_two[k] * axes[2][k] for k in range(3))
    view = geo["view"]
    g_inverse = focal_x * g_px + focal_y * g_py + view[0] * g_u + view[1] * g_v
    g_view = [inverse * g_u, inverse * g_v, -inverse * inverse * g_inverse]
    g_spread = [
        [sum(rot[i][j] * g_axes[i][k] for i in range(3)) for k in range(3)] for j in range(3)
    ]
    for k in range(3):
        grads[3 + k] = sum(g_spread[j][k] * geo["spread"][j][k] for j in range(3))
    g = [[g_spread[j][k] * geo["scales"][k] for k in range(3)] for j in range(3)]
    w, x, y, z = geo["unit"]
    g_w = 2.0 * (z * (g[1][0] - g[0][1]) + y * (g[0][2] - g[2][0]) + x * (g[2][1] - g[1][2]))
    g_x = 2.0 * (
        y * (g[0][1] + g[1][0])
        + z * (g[0][2] + g[2][0])
        + w * (g[2][1] - g[1][2])
        - 2.0 * x * (g[1][1] + g[2][2])
    )
    g_y = 2.0 * (
        x * (g[0][1] + g[1][0])
        + z * (g[1][2] + g[2][1])
        + w * (g[0][2] - g[2][0])
        - 2.0 * y * (g[0][0] + g[2][2])
    )
    g_z = 2.0 * (
        x * (g[0][2] + g[2][0])
        + y * (g[1][2] + g[2][1])
        + w * (g[1][0] - g[0][1])
        - 2.0 * z * (g[0][0] + g[1][1])
    )
    along = w * g_w + x * g_x + y * g_y + z * g_z
    for p, (g_q, q) in enumerate(((g_w, w), (g_x, x), (g_y, y), (g_z, z))):
        grads[6 + p] = (g_q - q * along) * geo["norm"]
    x, y, z = geo["toward"]
    basis = harmonic_basis(x, y, z)
    h = [None]
    for k in range(16):
        if k:
            h.append(sum(drawn[c] * row(11 + 3 * k + c) for c in range(3)))
        for c in range(3):
            grads[11 + 3 * k + c] = basis[k] * drawn[c]
    a, d = sh_two, sh_three
    xx, yy, zz, xy, yz, xz = x * x, y * y, z * z, x * y, y * z, x * z
    g_dx = (
        -sh_one * h[3] + a[0] * y * h[4] - 2.0 * a[2] * x * h[6] + a[3] * z * h[7]
        + 2.0 * a[4] * x * h[8] + 6.0 * d[0] * xy * h[9] + d[1] * yz * h[10]
        - 2.0 * d[2] * xy * h[11] - 6.0 * d[3] * xz * h[12]
        + d[4] * (4.0 * zz - 3.0 * xx - yy) * h[13] + 2.0 * d[5] * xz * h[14]
        + 3.0 * d[6] * (xx - yy) * h[15]
    )
    g_dy = (
        -sh_one * h[1] + a[0] * x * h[4] + a[1] * z * h[5] - 2.0 * a[2] * y * h[6]
        - 2.0 * a[4] * y * h[8] + 3.0 * d[0] * (xx - yy) * h[9] + d[1] * xz * h[10]
        + d[2] * (4.0 * zz - xx - 3.0 * yy) * h[11] - 6.0 * d[3] * yz * h[12]
        - 2.0 * d[4] * xy * h[13] - 2.0 * d[5] * yz * h[14] - 6.0 * d[6] * xy * h[15]
    )
    g_dz = (
        sh_one * h[2] + a[1] * y * h[5] + 4.0 * a[2] * z * h[6] + a[3] * x * h[7]
        + d[1] * xy * h[10] + 8.0 * d[2] * yz * h[11]
        + 3.0 * d[3] * (2.0 * zz - xx - yy) * h[12] + 8.0 * d[4] * xz * h[13]
        + d[5] * (xx - yy) * h[14]
    )
    along = x * g_dx + y * g_dy + z * g_dz
    turned = [(gd - t * along) * geo["shrink"] for gd, t in ((g_dx, x), (g_dy, y), (g_dz, z))]
    for j in range(3):
        grads[j] = sum(rot[i][j] * g_view[i] for i in range(3)) + turned[j]
    for b in range(blocks):
        mine = place == b
        for p in range(params):
            grad[p * blocks + b : p * blocks + b + 1, :] = jnp.sum(
                jnp.where(mine, grads[p], 0.0), axis=0, keepdims=True
            )

    for p in range(params):
        here = slice(p * blocks, (p + 1) * blocks)
        new = base_ref[p] - steps_ref[p] * grad[here, :]
        shifted = new + dual_ref[p]
        new_ref[p] = new
        shifted_ref[p] = shifted
        moved[here, :] = shifted
    shifted = jnp.concatenate(
        [moved[pl.ds(b, params, stride=blocks), :] for b in range(blocks)], axis=1
    )
    for n in range(pick_ref.shape[0]):
        value = exact_pick(shifted, pick_ref[n])
        for b in range(blocks):
            moved[pl.ds(b, params, stride=blocks), :] = value[:, b * LANES : (b + 1) * LANES]
        for p in range(params):
            sent_ref[n, p] = moved[p * blocks : (p + 1) * blocks, :]


def constants(pixels):
    place = np.arange(pixels)
    x = (place % LANES - 64).astype(np.float32)
    y = (place // LANES - 4).astype(np.float32)
    square = (x * x).astype(jnp.bfloat16).astype(np.float32)
    part = np.zeros((PART, pixels + 3 * LANES), np.float32)
    for c, value in enumerate([square, x * y, y * y, x, y, np.ones_like(x)]):
        part[c, :pixels] = value
    part[COEFS, :pixels] = x * x - square
    for c in range(3):
        part[COEFS - 3 + c, pixels + c * LANES : pixels + (c + 1) * LANES] = 1.0
    basis = np.concatenate([part] * 3)
    return jnp.asarray(basis, jnp.bfloat16)


def vmem(number=1):
    return [pl.BlockSpec(memory_space=pltpu.VMEM)] * number


def smem(number=1):
    return [pl.BlockSpec(memory_space=pltpu.SMEM)] * number


def params_with(mib):
    return pltpu.CompilerParams(vmem_limit_bytes=mib * 2**20)


def on_device(
    gaussians, consensus, duals, step_sizes, cameras, camera_ids, block_lists, depth_order,
    block_counts, targets, intersection,
):
    own, prior, dual = [value[0].swapaxes(0, 1) for value in (gaussians, consensus, duals)]
    params, blocks = own.shape[0], own.shape[1]
    peers = lax.axis_size("tile")
    me = lax.axis_index("tile")[None]
    listed = block_lists.shape[2]
    pixels = targets.shape[3]
    yrows = pixels // LANES
    outer = peers // INNER
    f32 = jnp.float32
    shape_of = jax.ShapeDtypeStruct
    basis = constants(pixels)

    def swap(value, mask):
        return lax.ppermute(value, "tile", [(i, i ^ mask) for i in range(peers)])

    hop_bits = list(reversed(range(2, peers.bit_length() - 1)))
    mine, pack = pl.pallas_call(
        pack_kernel,
        out_shape=(
            shape_of((1, 16 + listed), f32),
            shape_of((1, 3 * listed), jnp.int32),
        ),
        in_specs=vmem(5),
        out_specs=tuple(vmem(2)),
        compiler_params=params_with(8),
        name="pack",
    )(camera_ids, block_counts, block_lists[0], depth_order[0], cameras)
    held = pl.pallas_call(
        hold_kernel,
        out_shape=shape_of(own.shape, f32),
        in_specs=vmem(),
        out_specs=vmem()[0],
        compiler_params=params_with(8),
        name="hold",
    )(own)
    ids = mine
    everything = held[None]
    masks = [0]
    for step, bit in enumerate(hop_bits):
        arrived = swap(own[None] if step == 0 else everything, 1 << bit)
        if step < 2:
            ids = jnp.concatenate([ids, swap(ids, 1 << step)], 0)
        everything = jnp.concatenate([everything, arrived], 0)
        masks += [mask | (1 << bit) for mask in masks]

    group_total = lax.axis_size("scene")
    group = lax.axis_index("scene")[None]
    share = intersection[0, 0]
    if group_total == 2:
        routes = [[(0, 1), (1, 0)]]
        links = [(lambda g: g == 0, lambda g: g >= 0)]
    else:
        routes = [
            [(g + 1, g) for g in range(group_total - 1)],
            [(g, g + 1) for g in range(group_total - 1)],
        ]
        links = [
            (lambda g: g >= 0, lambda g: g < group_total - 1),
            (lambda g: g < 0, lambda g: g > 0),
        ]
    lists = [lax.ppermute(share, "scene", route) for route in routes]

    base, steps, pick, mask = pl.pallas_call(
        functools.partial(prepare_kernel, links),
        out_shape=(
            shape_of(own.shape, f32),
            shape_of(own.shape, f32),
            shape_of((len(links), blocks * LANES, blocks * LANES), jnp.bfloat16),
            shape_of((len(links), blocks, LANES), f32),
        ),
        in_specs=smem() + vmem(3) + smem() + vmem(1 + len(links)),
        out_specs=tuple(vmem(4)),
        compiler_params=params_with(8),
        name="prepare",
    )(group, held, prior, dual, step_sizes, share, *lists)

    messages = pl.pallas_call(
        functools.partial(project_kernel, masks, yrows, listed),
        out_shape=tuple([shape_of((COEFS * outer, LANES), f32)] * INNER),
        in_specs=smem() + vmem(2),
        out_specs=tuple(vmem(INNER)),
        scratch_shapes=[pltpu.VMEM((COEFS * outer * INNER, LANES), f32)],
        compiler_params=params_with(8),
        name="project",
    )(me, everything, ids)
    sources = [messages[0]] + [swap(messages[j], j) for j in range(1, INNER)]

    pack, base, steps, pick, mask = lax.optimization_barrier((pack, base, steps, pick, mask))
    outbox = pl.pallas_call(
        functools.partial(render_kernel, pixels, blocks, listed, hop_bits),
        out_shape=shape_of((peers, MSG, LANES), f32),
        in_specs=smem(2) + vmem(INNER + 3),
        out_specs=vmem()[0],
        scratch_shapes=[
            pltpu.VMEM((COEFS * peers, LANES), f32),
            pltpu.VMEM(((listed + 1) * KDIM, LANES), f32),
            pltpu.VMEM(((listed + 1) * LANES, KDIM), jnp.bfloat16),
            pltpu.VMEM(((listed + 1) * LANES, 3 * LANES), f32),
            pltpu.VMEM((LANES, pixels), f32),
            pltpu.VMEM((LANES, pixels), f32),
            pltpu.VMEM(((listed + 1) * LANES, pixels), f32),
            pltpu.VMEM(((listed + 1) * LANES, pixels), f32),
            pltpu.VMEM((yrows, SUB, LANES), f32),
            pltpu.VMEM((listed + 1, yrows, SUB, LANES), f32),
            pltpu.VMEM((listed + 1, yrows, SUB, LANES), f32),
            pltpu.VMEM((listed + 1, 3, yrows, SUB, LANES), f32),
            pltpu.VMEM((3, yrows, SUB, LANES), f32),
            pltpu.VMEM((KDIM, pixels), f32),
            pltpu.VMEM((KDIM, pixels), jnp.bfloat16),
            pltpu.VMEM((yrows, SUB, LANES), f32),
            pltpu.VMEM((MOMENTS * LANES, LANES), f32),
            pltpu.VMEM((MOMENTS * LANES, LANES), f32),
            pltpu.VMEM((listed + 4, SUB, MOMENTS * LANES), f32),
            pltpu.VMEM((listed * MSG, LANES), f32),
            pltpu.SMEM((listed,), jnp.int32),
        ],
        compiler_params=params_with(48),
        name="render",
    )(
        me, pack, mine, *sources, targets[0, 0], basis,
    )
    inbox = lax.all_to_all(outbox, "tile", split_axis=0, concat_axis=0, tiled=True)
    updated, shifted, sent = pl.pallas_call(
        owner_kernel,
        out_shape=(
            shape_of(own.shape, f32),
            shape_of(own.shape, f32),
            shape_of((len(links),) + own.shape, f32),
        ),
        in_specs=vmem(6),
        out_specs=tuple(vmem(3)),
        scratch_shapes=[pltpu.VMEM((params * blocks, LANES), f32)] * 2,
        compiler_params=params_with(16),
        name="owner",
    )(inbox.reshape(peers * MSG, LANES), held, base, dual, steps, pick)
    new_duals = jnp.zeros_like(shifted)
    for n, route in enumerate(routes):
        theirs = lax.ppermute(sent[n], "scene", route)
        change = shifted - 0.5 * (shifted + theirs)
        new_duals = jnp.where(mask[n] > 0.5, change, new_duals)
    return updated.swapaxes(0, 1)[None], new_duals.swapaxes(0, 1)[None]


def solution(mesh):
    placed = (
        P("scene", "tile", None, None),
        P("scene", "tile", None, None),
        P("scene", "tile", None, None),
        P(),
        P(),
        P("scene", "tile"),
        P("scene", "tile", None),
        P("scene", "tile", None),
        P("scene", "tile"),
        P("scene", "tile", None, None),
        P("scene", "tile", None, None),
    )
    return jax.shard_map(
        on_device,
        mesh=mesh,
        in_specs=placed,
        out_specs=(P("scene", "tile", None, None), P("scene", "tile", None, None)),
        check_vma=False,
    )
```

```python
import functools

import jax
import jax.numpy as jnp
import numpy as np
from jax import lax
from jax.experimental import pallas as pl
from jax.experimental.pallas import tpu as pltpu
from jax.sharding import PartitionSpec as P

penalty_weight = 0.5
blur_floor = 0.3
alpha_ceiling = 0.99
log2e = 1.4426950408889634
sh_zero = 0.28209479177387814
sh_one = 0.4886025119029199
sh_two = (
    1.0925484305920792,
    -1.0925484305920792,
    0.31539156525252005,
    -1.0925484305920792,
    0.5462742152960396,
)
sh_three = (
    -0.5900435899266435,
    2.890611442640554,
    -0.4570457994644658,
    0.3731763325901154,
    -0.4570457994644658,
    1.445305721320277,
    -0.5900435899266435,
)

LANES = 128
SUB = 8
PART = 16
KDIM = 3 * PART
COEFS = 9
INNER = 4
MOMENTS = 6
WIDE = 256
MSG = 16
highest = lax.Precision.HIGHEST


def harmonic_basis(x, y, z):
    xx, yy, zz = x * x, y * y, z * z
    return [
        sh_zero + 0.0 * x,
        -sh_one * y,
        sh_one * z,
        -sh_one * x,
        sh_two[0] * x * y,
        sh_two[1] * y * z,
        sh_two[2] * (2.0 * zz - xx - yy),
        sh_two[3] * x * z,
        sh_two[4] * (xx - yy),
        sh_three[0] * y * (3.0 * xx - yy),
        sh_three[1] * x * y * z,
        sh_three[2] * y * (4.0 * zz - xx - yy),
        sh_three[3] * z * (2.0 * zz - 3.0 * xx - 3.0 * yy),
        sh_three[4] * x * (4.0 * zz - xx - yy),
        sh_three[5] * z * (xx - yy),
        sh_three[6] * x * (xx - 3.0 * yy),
    ]


def geometry(row, cam):
    mean = [row(0), row(1), row(2)]
    rot = [[cam[3 * i + j] for j in range(3)] for i in range(3)]
    shift = [cam[9 + i] for i in range(3)]
    focal_x, focal_y = cam[12], cam[13]
    view = [
        rot[i][0] * mean[0] + rot[i][1] * mean[1] + rot[i][2] * mean[2] + shift[i] for i in range(3)
    ]
    inverse = 1.0 / view[2]
    u = view[0] * inverse
    v = view[1] * inverse
    quat = [row(6 + i) for i in range(4)]
    norm = lax.rsqrt(sum(q * q for q in quat))
    w, x, y, z = [q * norm for q in quat]
    turn = [
        [1.0 - 2.0 * (y * y + z * z), 2.0 * (x * y - w * z), 2.0 * (x * z + w * y)],
        [2.0 * (x * y + w * z), 1.0 - 2.0 * (x * x + z * z), 2.0 * (y * z - w * x)],
        [2.0 * (x * z - w * y), 2.0 * (y * z + w * x), 1.0 - 2.0 * (x * x + y * y)],
    ]
    scales = [jnp.exp(row(3 + k)) for k in range(3)]
    spread = [[turn[j][k] * scales[k] for k in range(3)] for j in range(3)]
    axes = [
        [sum(rot[i][j] * spread[j][k] for j in range(3)) for k in range(3)] for i in range(3)
    ]
    scale_x = focal_x * inverse
    scale_y = focal_y * inverse
    lean_x = [axes[0][k] - u * axes[2][k] for k in range(3)]
    lean_y = [axes[1][k] - v * axes[2][k] for k in range(3)]
    row_one = [scale_x * lean_x[k] for k in range(3)]
    row_two = [scale_y * lean_y[k] for k in range(3)]
    cov_xx = sum(a * a for a in row_one) + blur_floor
    cov_xy = sum(a * b for a, b in zip(row_one, row_two))
    cov_yy = sum(b * b for b in row_two) + blur_floor
    scale = 1.0 / (cov_xx * cov_yy - cov_xy * cov_xy)
    conic = (cov_yy * scale, -cov_xy * scale, cov_xx * scale)
    eye = [-(rot[0][i] * shift[0] + rot[1][i] * shift[1] + rot[2][i] * shift[2]) for i in range(3)]
    away = [mean[i] - eye[i] for i in range(3)]
    shrink = lax.rsqrt(sum(a * a for a in away))
    toward = [a * shrink for a in away]
    return dict(
        rot=rot,
        view=view,
        inverse=inverse,
        u=u,
        v=v,
        norm=norm,
        unit=(w, x, y, z),
        scales=scales,
        spread=spread,
        axes=axes,
        scale_x=scale_x,
        scale_y=scale_y,
        lean_x=lean_x,
        lean_y=lean_y,
        row_one=row_one,
        row_two=row_two,
        conic=conic,
        shrink=shrink,
        toward=toward,
    )


def three_parts(value):
    high = value.astype(jnp.bfloat16).astype(jnp.float32)
    rest = value - high
    mid = rest.astype(jnp.bfloat16).astype(jnp.float32)
    return high, mid, rest - mid


def exact_pick(value, pick):
    high, mid, low = [part.astype(jnp.bfloat16) for part in three_parts(value)]
    dot = functools.partial(jnp.dot, preferred_element_type=jnp.float32)
    return (dot(high, pick) + dot(mid, pick)) + dot(low, pick)


def segment_order(back):
    shape = (LANES, LANES)
    gauss = lax.broadcasted_iota(jnp.int32, shape, int(back))
    place = lax.broadcasted_iota(jnp.int32, shape, 1 - int(back))
    return (gauss == (place % SUB) * (LANES // SUB) + place // SUB).astype(jnp.bfloat16)


def sub_roll(value, shift):
    return pltpu.roll(value, shift % SUB, 0)


def prepare_kernel(
    links, group_ref, own_ref, cons_ref, dual_ref, step_ref, share_ref, *refs
):
    others, (base_ref, steps_ref, pick_ref, mask_ref) = refs[: len(links)], refs[len(links) :]
    params, blocks = own_ref.shape[0], own_ref.shape[1]
    group = group_ref[0]
    for p in range(params):
        step = step_ref[p]
        here = own_ref[p]
        steps_ref[p] = jnp.full((blocks, LANES), step)
        base_ref[p] = here - step * (penalty_weight * (here - cons_ref[p] + dual_ref[p]))
    half = share_ref.shape[1]
    local = lax.broadcasted_iota(jnp.int32, (blocks * LANES, half), 0)
    contract = (((1,), (1,)), ((), ()))
    for n, (side_of, exists_of) in enumerate(links):
        other = others[n]
        up = side_of(group)
        mine = jnp.where(up, share_ref[0:1, :], share_ref[1:2, :])
        theirs = jnp.where(up, other[1:2, :], other[0:1, :])
        source = (local == mine).astype(jnp.bfloat16)
        target = (local == theirs).astype(jnp.bfloat16)
        pick_ref[n] = lax.dot_general(
            source, target, contract, preferred_element_type=jnp.float32
        ).astype(jnp.bfloat16)
        there = jnp.full((SUB, half), jnp.where(exists_of(group), 1.0, 0.0)).astype(jnp.bfloat16)
        mask = lax.dot_general(there, source, contract, preferred_element_type=jnp.float32)
        for b in range(blocks):
            mask_ref[n, b : b + 1, :] = mask[0:1, b * LANES : (b + 1) * LANES]


def hold_kernel(own_ref, held_ref):
    held_ref[...] = own_ref[...]


def pack_kernel(camera_ref, count_ref, list_ref, depth_ref, cameras_ref, mine_ref, pack_ref):
    listed = list_ref.shape[1]
    blocks = list_ref[...]
    shape = cameras_ref.shape
    chosen = lax.broadcasted_iota(jnp.int32, shape, 0) == jnp.broadcast_to(camera_ref[...], shape)
    mine_ref[:, :16] = jnp.sum(jnp.where(chosen, cameras_ref[...], 0.0), axis=0, keepdims=True)
    mine_ref[:, 16:] = blocks.astype(jnp.float32)
    pack_ref[:, :listed] = blocks
    pack_ref[:, listed : 2 * listed] = depth_ref[...]
    pack_ref[:, 2 * listed :] = jnp.broadcast_to(count_ref[...], (1, listed))


def project_kernel(masks, yrows, listed, me_ref, raw_ref, ids_ref, *refs):
    outs, feat = refs[:INNER], refs[INNER]
    outer = len(masks)
    blocks = raw_ref.shape[2]
    me = me_ref[0]
    ids = jnp.concatenate([ids_ref[...]] * (SUB // INNER), axis=0)
    lane = lax.broadcasted_iota(jnp.int32, (SUB, LANES), 1)
    sub = lax.broadcasted_iota(jnp.int32, (SUB, LANES), 0)
    cam = [jnp.broadcast_to(ids[:, k : k + 1], (SUB, LANES)) for k in range(16)]
    top = (((me & 3) ^ (sub & 3)) * yrows).astype(jnp.float32)
    lists = ids[:, 16 : 16 + listed]
    rows = outer * INNER
    for v in range(rows // SUB):
        owners = [2 * v, 2 * v + 1]
        first = jnp.where(sub < INNER, (me ^ masks[owners[0]]) * blocks, (me ^ masks[owners[1]]) * blocks)
        found = []
        for b in range(1, blocks):
            same = (lists == (first[:, :listed] + b).astype(jnp.float32)).astype(jnp.float32)
            found.append(jnp.broadcast_to(jnp.max(same, axis=1, keepdims=True), (SUB, LANES)) > 0.5)

        def row(p):
            def of(b):
                return jnp.where(
                    sub < INNER,
                    jnp.broadcast_to(raw_ref[owners[0], p, b : b + 1, :], (SUB, LANES)),
                    jnp.broadcast_to(raw_ref[owners[1], p, b : b + 1, :], (SUB, LANES)),
                )

            value = of(0)
            for b in range(1, blocks):
                value = jnp.where(found[b - 1], of(b), value)
            return value

        geo = geometry(row, cam)
        sx = cam[12] * geo["u"] + (cam[14] - 64.0)
        sy = cam[13] * geo["v"] + (cam[15] - top - 4.0)
        basis = harmonic_basis(*geo["toward"])
        tint = [sum(basis[k] * row(11 + 3 * k + c) for k in range(16)) + 0.5 for c in range(3)]
        lo = -jnp.log(1.0 + jnp.exp(-row(10))) * log2e
        ca, cb, cc = geo["conic"]
        kxx = (-0.5 * log2e) * ca
        kxy = -log2e * cb
        kyy = (-0.5 * log2e) * cc
        kx = -2.0 * kxx * sx - kxy * sy
        ky = -2.0 * kyy * sy - kxy * sx
        k1 = kxx * sx * sx + kxy * sx * sy + kyy * sy * sy + lo
        for m, value in enumerate([kxx, kxy, kyy, kx, ky, k1, *tint]):
            feat[m * rows + v * SUB : m * rows + (v + 1) * SUB, :] = value
    feat[...] = exact_pick(feat[...], segment_order(False))
    for j in range(INNER):
        outs[j][...] = feat[pl.ds(j, COEFS * outer, stride=INNER), :]


def render_kernel(
    pixels, blocks, listed, hop_bits, me_ref, pack_ref, ids_ref, src0, src1, src2, src3, target_ref,
    basis_ref, out_ref,
    raw, coef, lefts, shade, gaps_a, gaps_b, alphas, weights, carry, before, passed,
    colours, resid, mirror, pulls, behind, sums_a, sums_b, found, rows, slots,
):
    peers = out_ref.shape[0]
    outer = peers // INNER
    per_owner = blocks
    yrows = pixels // LANES
    groups = LANES // SUB
    me = me_ref[0]
    count = pack_ref[0, 2 * listed]
    top = ((me % 4) * yrows).astype(jnp.float32)

    def place_slot(j, ends):
        live_end, dead_end = ends
        slot = pack_ref[0, listed + j]
        live = slot < count
        slots[jnp.where(live, live_end, dead_end)] = slot
        return jnp.where(live, live_end + 1, live_end), jnp.where(live, dead_end, dead_end + 1)

    ends = (jnp.int32(0), count)
    for j in range(listed):
        ends = place_slot(j, ends)

    for j, src in enumerate((src0, src1, src2, src3)):
        raw[j * COEFS * outer : (j + 1) * COEFS * outer, :] = src[...]
    place = lax.broadcasted_iota(jnp.int32, (PART, LANES), 0)
    blank = jnp.where(place == 5, -4096.0, 0.0)
    for k in range(coef.shape[0] // KDIM):
        for part in range(3):
            at = k * KDIM + part * PART
            coef[at : at + PART, :] = jnp.zeros_like(blank) if part else blank
    for k in range(listed):
        apart = me ^ (pack_ref[0, slots[k]] // per_owner)
        near_by = sum((((apart >> bit) & 1) << t) for t, bit in enumerate(hop_bits))
        start = (apart & (INNER - 1)) * (COEFS * outer) + near_by
        value = raw[pl.ds(start, COEFS, stride=outer), :]
        live = k < count
        for part, piece in enumerate(three_parts(value)):
            at = k * KDIM + part * PART
            piece = jnp.where(live, piece, blank[:COEFS, :] if part == 0 else 0.0)
            coef[at : at + COEFS, :] = piece
            coef[at + COEFS : at + COEFS + 1, :] = piece[0:1, :]
            coef[at + COEFS + 1 : at + COEFS + 4, :] = piece[COEFS - 3 : COEFS, :]

    sub = lax.broadcasted_iota(jnp.int32, (SUB, LANES), 0)
    one = jnp.ones((SUB, LANES), jnp.float32)
    none = jnp.zeros((SUB, LANES), jnp.float32)
    row_sets = [range(yrows // 2), range(yrows // 2, yrows)]
    for y in range(yrows):
        carry[y] = one
        behind[y] = none
        for c in range(3):
            resid[c, y] = none

    def spread_row(value, index):
        return jnp.broadcast_to(value[index : index + 1, :], (SUB, LANES))

    def rows_at(start, size, step):
        return pl.ds(pl.multiple_of(start, step), size)

    for k in range(coef.shape[0] // KDIM):
        mine = coef[k * KDIM : (k + 1) * KDIM, :].T
        lefts[k * LANES : (k + 1) * LANES, :] = mine.astype(jnp.bfloat16)

    def left(k):
        return lefts[rows_at(k * LANES, LANES, LANES), :]

    def times(mine, right, start, width):
        here = slice(start, start + width)
        return jnp.dot(mine, right[:, here], preferred_element_type=jnp.float32)

    def chain(k):
        base = pl.multiple_of(k * LANES, LANES)
        mine = left(k)
        for start in range(0, pixels, WIDE):
            value = jnp.minimum(alpha_ceiling, jnp.exp2(times(mine, basis_ref, start, WIDE)))
            kept = [one] * (WIDE // LANES)
            for i in range(groups):
                here = rows_at(base + i * SUB, SUB, SUB)
                for j in range(WIDE // LANES):
                    alpha = value[i * SUB : (i + 1) * SUB, j * LANES : (j + 1) * LANES]
                    weight = alpha * kept[j]
                    lanes = slice(start + j * LANES, start + (j + 1) * LANES)
                    alphas[here, lanes] = alpha
                    weights[here, lanes] = weight
                    kept[j] = kept[j] - weight
            for j in range(WIDE // LANES):
                passed[k, start // LANES + j] = kept[j]
        shade[rows_at(k * LANES, LANES, LANES), :] = times(mine, basis_ref, pixels, 3 * LANES)

    def tally(k, ended):
        base = pl.multiple_of(k * LANES, LANES)
        for some in row_sets:
            total = [[last - last for last in ends] for ends in ended]
            for i in range(groups):
                here = rows_at(base + i * SUB, SUB, SUB)
                tints = [shade[here, c * LANES : (c + 1) * LANES] for c in range(3)]
                for j, y in enumerate(some):
                    weight = weights[here, y * LANES : (y + 1) * LANES]
                    for c in range(3):
                        total[c][j] = total[c][j] + weight * tints[c]
            for j, y in enumerate(some):
                through = passed[k, y]
                for step in (1, 2, 4):
                    through = through * jnp.where(sub >= step, sub_roll(through, step), 1.0)
                entering = carry[y]
                ahead = entering * jnp.where(sub >= 1, sub_roll(through, 1), 1.0)
                before[k, y] = ahead
                carry[y] = entering * spread_row(through, SUB - 1)
                for c in range(3):
                    colours[k, c, y] = total[c][j]
                    resid[c, y] = resid[c, y] + ahead * total[c][j]
            ended = total
        return ended

    pairs = (count + 1) // 2
    fresh = [[none] * (yrows // 2)] * 3
    chain(0)
    chain(1)

    def forward(pair, _):
        tally(2 * pair - 1, tally(2 * pair - 2, fresh))
        chain(2 * pair)
        chain(2 * pair + 1)
        return 0

    lax.fori_loop(1, pairs, forward, 0)
    tally(2 * pairs - 1, tally(2 * pairs - 2, fresh))

    mirror[...] = jnp.zeros(mirror.shape, jnp.float32)
    for y in range(yrows):
        for c in range(3):
            value = jnp.sum(resid[c, y], axis=0, keepdims=True)
            value = value - target_ref[c : c + 1, y * LANES : (y + 1) * LANES]
            resid[c, y] = jnp.broadcast_to(value, (SUB, LANES))
            high, low, _ = three_parts(value)
            for piece in range(3):
                lanes = slice(y * LANES, (y + 1) * LANES)
                at = piece * PART + COEFS - 3 + c
                mirror[at : at + 1, lanes] = high
                if piece < 2:
                    mirror[at + 4 : at + 5, lanes] = low
    pulls[...] = mirror[...].astype(jnp.bfloat16)

    def follow(k, gaps):
        base = pl.multiple_of(k * LANES, LANES)
        rear = [None] * yrows
        for y in range(yrows):
            gain = passed[k, y]
            value = sum(colours[k, c, y] * resid[c, y] for c in range(3))
            for step in (1, 2, 4):
                inside = sub < SUB - step
                value = value + gain * jnp.where(inside, sub_roll(value, -step), 0.0)
                gain = gain * jnp.where(inside, sub_roll(gain, -step), 1.0)
            last = behind[y]
            rear[y] = jnp.where(
                sub < SUB - 1, sub_roll(value, -1) + sub_roll(gain, -1) * last, last
            )
            behind[y] = spread_row(value + gain * last, 0)
        mine = left(k)
        for start in range(0, pixels, WIDE):
            value = times(mine, pulls, start, WIDE)
            for i in reversed(range(groups)):
                here = slice(i * SUB, (i + 1) * SUB)
                for j in range(WIDE // LANES):
                    y = start // LANES + j
                    lanes = slice(y * LANES, (y + 1) * LANES)
                    gap = value[here, j * LANES : (j + 1) * LANES] - rear[y]
                    gaps[here, lanes] = gap
                    rear[y] = rear[y] + alphas[rows_at(base + i * SUB, SUB, SUB), lanes] * gap

    def weigh(k, gaps, sums):
        base = pl.multiple_of(k * LANES, LANES)
        front = [before[k, y] for y in range(yrows)]
        for i in range(groups):
            at = slice(i * SUB, (i + 1) * SUB)
            here = rows_at(base + i * SUB, SUB, SUB)
            run = [none] * MOMENTS
            for y in range(yrows):
                lanes = slice(y * LANES, (y + 1) * LANES)
                weight = weights[here, lanes] * front[y]
                slope = jnp.where(alphas[here, lanes] < alpha_ceiling, weight * gaps[at, lanes], 0.0)
                run[0] = run[0] + slope
                run[1] = run[1] + run[0]
                run[2] = run[2] + run[1]
                for c in range(3):
                    run[3 + c] = run[3 + c] + weight * resid[c, y]
            for m, value in enumerate(run):
                sums[m * LANES + i * SUB : m * LANES + (i + 1) * SUB, :] = value

    across = (lax.broadcasted_iota(jnp.int32, (SUB, LANES), 1) - 64).astype(jnp.float32)
    square = across * across
    coarse = square.astype(jnp.bfloat16).astype(jnp.float32)
    xmom = jnp.where(sub == 0, one, jnp.where(sub == 1, across, none))
    xmom = jnp.where(sub == 2, coarse, jnp.where(sub == 3, square - coarse, xmom))
    xmom = xmom.astype(jnp.bfloat16)

    def moments(k, sums):
        value = sums[...]
        high = value.astype(jnp.bfloat16)
        low = (value - high.astype(jnp.float32)).astype(jnp.bfloat16)
        contract = (((1,), (1,)), ((), ()))
        found[k] = lax.dot_general(
            xmom, high, contract, preferred_element_type=jnp.float32
        ) + lax.dot_general(xmom, low, contract, preferred_element_type=jnp.float32)

    rearmost = 2 * pairs - 1

    def backward(pair, _):
        k = rearmost - 2 * pair
        moments(k + 4, sums_a)
        weigh(k + 2, gaps_a, sums_a)
        follow(k, gaps_a)
        moments(k + 3, sums_b)
        weigh(k + 1, gaps_b, sums_b)
        follow(k - 1, gaps_b)
        return 0

    follow(rearmost, gaps_a)
    follow(rearmost - 1, gaps_b)
    lax.fori_loop(1, pairs, backward, 0)
    moments(3, sums_a)
    weigh(1, gaps_a, sums_a)
    moments(2, sums_b)
    weigh(0, gaps_b, sums_b)
    moments(1, sums_a)
    moments(0, sums_b)

    lane = lax.broadcasted_iota(jnp.int32, (1, LANES), 1)
    camera = jnp.concatenate([ids_ref[...], jnp.zeros((1, LANES - ids_ref.shape[1]), jnp.float32)], 1)
    meta = jnp.where(lane < 16, camera, jnp.where(lane == 17, top, 0.0))

    rows[...] = jnp.zeros(rows.shape, jnp.float32)

    def gather_moments(k):
        part = lambda order, m: found[k, order : order + 1, m * LANES : (m + 1) * LANES]
        rise = yrows - 4.0
        s0, x1, x2 = part(0, 0), part(1, 0), part(2, 0) + part(3, 0)
        t1, tx, t2 = part(0, 1), part(1, 1), 2.0 * part(0, 2) - part(0, 1)
        answer = [s0, x1, rise * s0 - t1, x2, rise * x1 - tx, rise * (rise * s0 - 2.0 * t1) + t2]
        answer += [part(0, 3 + c) for c in range(3)]
        for m, value in enumerate(answer):
            rows[k * MSG + m : k * MSG + m + 1, :] = jnp.where(k < count, value, 0.0)

    for k in range(listed):
        gather_moments(k)
    rows[...] = exact_pick(rows[...], segment_order(True))

    if peers > listed:
        absent = jnp.where(lane == 16, -1.0, 0.0)
        for peer in range(peers):
            out_ref[peer] = jnp.broadcast_to(absent, (MSG, LANES))

    for k in range(listed):
        block = pack_ref[0, slots[k]]
        place = (block % per_owner).astype(jnp.float32)
        rows[k * MSG + 9 : k * MSG + 10, :] = jnp.where(lane == 16, place, meta)
        out_ref[block // per_owner] = rows[k * MSG : (k + 1) * MSG, :]


def owner_kernel(
    inbox_ref, own_ref, base_ref, dual_ref, steps_ref, pick_ref, new_ref, shifted_ref, sent_ref,
    grad, moved
):
    params, blocks = own_ref.shape[0], own_ref.shape[1]
    strips = inbox_ref.shape[0] // MSG

    def message(m):
        return inbox_ref[pl.ds(m, strips, stride=MSG), :]

    meta = message(9)
    cam = [jnp.broadcast_to(meta[:, k : k + 1], (strips, LANES)) for k in range(18)]
    place, top = cam[16], cam[17]

    def row(p):
        value = jnp.broadcast_to(own_ref[p, 0:1, :], (strips, LANES))
        for b in range(1, blocks):
            value = jnp.where(place == b, own_ref[p, b : b + 1, :], value)
        return value

    geo = geometry(row, cam)
    u, v, inverse = geo["u"], geo["v"], geo["inverse"]
    focal_x, focal_y = cam[12], cam[13]
    at_x = focal_x * u + (cam[14] - 64.0)
    at_y = focal_y * v + (cam[15] - top - 4.0)
    s0, x1, y1, x2, xy, y2, *drawn = [message(m) for m in range(9)]
    sx = x1 - at_x * s0
    sy = y1 - at_y * s0
    sxx = x2 - at_x * (x1 + sx)
    sxy = xy - at_x * y1 - at_y * sx
    syy = y2 - at_y * (y1 + sy)
    ca, cb, cc = geo["conic"]
    axes, rot = geo["axes"], geo["rot"]
    grads = {}
    opacity = 1.0 / (1.0 + jnp.exp(-row(10)))
    grads[10] = s0 * (1.0 - opacity)
    t00, t01 = sxx * ca + sxy * cb, sxx * cb + sxy * cc
    t10, t11 = sxy * ca + syy * cb, sxy * cb + syy * cc
    g_xx = 0.5 * (ca * t00 + cb * t10)
    g_xy = ca * t01 + cb * t11
    g_yy = 0.5 * (cb * t01 + cc * t11)
    one, two = geo["row_one"], geo["row_two"]
    g_one = [2.0 * g_xx * one[k] + g_xy * two[k] for k in range(3)]
    g_two = [2.0 * g_yy * two[k] + g_xy * one[k] for k in range(3)]
    px, py = geo["scale_x"], geo["scale_y"]
    g_axes = [
        [px * g_one[k] for k in range(3)],
        [py * g_two[k] for k in range(3)],
        [-(px * u * g_one[k] + py * v * g_two[k]) for k in range(3)],
    ]
    g_px = sum(g_one[k] * geo["lean_x"][k] for k in range(3))
    g_py = sum(g_two[k] * geo["lean_y"][k] for k in range(3))
    g_u = focal_x * (ca * sx + cb * sy) - px * sum(g_one[k] * axes[2][k] for k in range(3))
    g_v = focal_y * (cc * sy + cb * sx) - py * sum(g_two[k] * axes[2][k] for k in range(3))
    view = geo["view"]
    g_inverse = focal_x * g_px + focal_y * g_py + view[0] * g_u + view[1] * g_v
    g_view = [inverse * g_u, inverse * g_v, -inverse * inverse * g_inverse]
    g_spread = [
        [sum(rot[i][j] * g_axes[i][k] for i in range(3)) for k in range(3)] for j in range(3)
    ]
    for k in range(3):
        grads[3 + k] = sum(g_spread[j][k] * geo["spread"][j][k] for j in range(3))
    g = [[g_spread[j][k] * geo["scales"][k] for k in range(3)] for j in range(3)]
    w, x, y, z = geo["unit"]
    g_w = 2.0 * (z * (g[1][0] - g[0][1]) + y * (g[0][2] - g[2][0]) + x * (g[2][1] - g[1][2]))
    g_x = 2.0 * (
        y * (g[0][1] + g[1][0])
        + z * (g[0][2] + g[2][0])
        + w * (g[2][1] - g[1][2])
        - 2.0 * x * (g[1][1] + g[2][2])
    )
    g_y = 2.0 * (
        x * (g[0][1] + g[1][0])
        + z * (g[1][2] + g[2][1])
        + w * (g[0][2] - g[2][0])
        - 2.0 * y * (g[0][0] + g[2][2])
    )
    g_z = 2.0 * (
        x * (g[0][2] + g[2][0])
        + y * (g[1][2] + g[2][1])
        + w * (g[1][0] - g[0][1])
        - 2.0 * z * (g[0][0] + g[1][1])
    )
    along = w * g_w + x * g_x + y * g_y + z * g_z
    for p, (g_q, q) in enumerate(((g_w, w), (g_x, x), (g_y, y), (g_z, z))):
        grads[6 + p] = (g_q - q * along) * geo["norm"]
    x, y, z = geo["toward"]
    basis = harmonic_basis(x, y, z)
    h = [None]
    for k in range(16):
        if k:
            h.append(sum(drawn[c] * row(11 + 3 * k + c) for c in range(3)))
        for c in range(3):
            grads[11 + 3 * k + c] = basis[k] * drawn[c]
    a, d = sh_two, sh_three
    xx, yy, zz, xy, yz, xz = x * x, y * y, z * z, x * y, y * z, x * z
    g_dx = (
        -sh_one * h[3] + a[0] * y * h[4] - 2.0 * a[2] * x * h[6] + a[3] * z * h[7]
        + 2.0 * a[4] * x * h[8] + 6.0 * d[0] * xy * h[9] + d[1] * yz * h[10]
        - 2.0 * d[2] * xy * h[11] - 6.0 * d[3] * xz * h[12]
        + d[4] * (4.0 * zz - 3.0 * xx - yy) * h[13] + 2.0 * d[5] * xz * h[14]
        + 3.0 * d[6] * (xx - yy) * h[15]
    )
    g_dy = (
        -sh_one * h[1] + a[0] * x * h[4] + a[1] * z * h[5] - 2.0 * a[2] * y * h[6]
        - 2.0 * a[4] * y * h[8] + 3.0 * d[0] * (xx - yy) * h[9] + d[1] * xz * h[10]
        + d[2] * (4.0 * zz - xx - 3.0 * yy) * h[11] - 6.0 * d[3] * yz * h[12]
        - 2.0 * d[4] * xy * h[13] - 2.0 * d[5] * yz * h[14] - 6.0 * d[6] * xy * h[15]
    )
    g_dz = (
        sh_one * h[2] + a[1] * y * h[5] + 4.0 * a[2] * z * h[6] + a[3] * x * h[7]
        + d[1] * xy * h[10] + 8.0 * d[2] * yz * h[11]
        + 3.0 * d[3] * (2.0 * zz - xx - yy) * h[12] + 8.0 * d[4] * xz * h[13]
        + d[5] * (xx - yy) * h[14]
    )
    along = x * g_dx + y * g_dy + z * g_dz
    turned = [(gd - t * along) * geo["shrink"] for gd, t in ((g_dx, x), (g_dy, y), (g_dz, z))]
    for j in range(3):
        grads[j] = sum(rot[i][j] * g_view[i] for i in range(3)) + turned[j]
    for b in range(blocks):
        mine = place == b
        for p in range(params):
            grad[p * blocks + b : p * blocks + b + 1, :] = jnp.sum(
                jnp.where(mine, grads[p], 0.0), axis=0, keepdims=True
            )

    for p in range(params):
        here = slice(p * blocks, (p + 1) * blocks)
        new = base_ref[p] - steps_ref[p] * grad[here, :]
        shifted = new + dual_ref[p]
        new_ref[p] = new
        shifted_ref[p] = shifted
        moved[here, :] = shifted
    shifted = jnp.concatenate(
        [moved[pl.ds(b, params, stride=blocks), :] for b in range(blocks)], axis=1
    )
    for n in range(pick_ref.shape[0]):
        value = exact_pick(shifted, pick_ref[n])
        for b in range(blocks):
            moved[pl.ds(b, params, stride=blocks), :] = value[:, b * LANES : (b + 1) * LANES]
        for p in range(params):
            sent_ref[n, p] = moved[p * blocks : (p + 1) * blocks, :]


def constants(pixels):
    place = np.arange(pixels)
    x = (place % LANES - 64).astype(np.float32)
    y = (place // LANES - 4).astype(np.float32)
    square = (x * x).astype(jnp.bfloat16).astype(np.float32)
    part = np.zeros((PART, pixels + 3 * LANES), np.float32)
    for c, value in enumerate([square, x * y, y * y, x, y, np.ones_like(x)]):
        part[c, :pixels] = value
    part[COEFS, :pixels] = x * x - square
    for c in range(3):
        part[COEFS - 3 + c, pixels + c * LANES : pixels + (c + 1) * LANES] = 1.0
    basis = np.concatenate([part] * 3)
    return jnp.asarray(basis, jnp.bfloat16)


def vmem(number=1):
    return [pl.BlockSpec(memory_space=pltpu.VMEM)] * number


def smem(number=1):
    return [pl.BlockSpec(memory_space=pltpu.SMEM)] * number


def params_with(mib):
    return pltpu.CompilerParams(vmem_limit_bytes=mib * 2**20)


def on_device(
    gaussians, consensus, duals, step_sizes, cameras, camera_ids, block_lists, depth_order,
    block_counts, targets, intersection,
):
    own, prior, dual = [value[0].swapaxes(0, 1) for value in (gaussians, consensus, duals)]
    params, blocks = own.shape[0], own.shape[1]
    peers = lax.axis_size("tile")
    me = lax.axis_index("tile")[None]
    listed = block_lists.shape[2]
    pixels = targets.shape[3]
    yrows = pixels // LANES
    outer = peers // INNER
    f32 = jnp.float32
    shape_of = jax.ShapeDtypeStruct
    basis = constants(pixels)

    def swap(value, mask):
        return lax.ppermute(value, "tile", [(i, i ^ mask) for i in range(peers)])

    hop_bits = list(reversed(range(2, peers.bit_length() - 1)))
    mine, pack = pl.pallas_call(
        pack_kernel,
        out_shape=(
            shape_of((1, 16 + listed), f32),
            shape_of((1, 3 * listed), jnp.int32),
        ),
        in_specs=vmem(5),
        out_specs=tuple(vmem(2)),
        compiler_params=params_with(8),
        name="pack",
    )(camera_ids, block_counts, block_lists[0], depth_order[0], cameras)
    held = pl.pallas_call(
        hold_kernel,
        out_shape=shape_of(own.shape, f32),
        in_specs=vmem(),
        out_specs=vmem()[0],
        compiler_params=params_with(8),
        name="hold",
    )(own)
    ids = mine
    everything = held[None]
    masks = [0]
    for step, bit in enumerate(hop_bits):
        arrived = swap(own[None] if step == 0 else everything, 1 << bit)
        if step < 2:
            ids = jnp.concatenate([ids, swap(ids, 1 << step)], 0)
        everything = jnp.concatenate([everything, arrived], 0)
        masks += [mask | (1 << bit) for mask in masks]

    group_total = lax.axis_size("scene")
    group = lax.axis_index("scene")[None]
    share = intersection[0, 0]
    if group_total == 2:
        routes = [[(0, 1), (1, 0)]]
        links = [(lambda g: g == 0, lambda g: g >= 0)]
    else:
        routes = [
            [(g + 1, g) for g in range(group_total - 1)],
            [(g, g + 1) for g in range(group_total - 1)],
        ]
        links = [
            (lambda g: g >= 0, lambda g: g < group_total - 1),
            (lambda g: g < 0, lambda g: g > 0),
        ]
    lists = [lax.ppermute(share, "scene", route) for route in routes]

    base, steps, pick, mask = pl.pallas_call(
        functools.partial(prepare_kernel, links),
        out_shape=(
            shape_of(own.shape, f32),
            shape_of(own.shape, f32),
            shape_of((len(links), blocks * LANES, blocks * LANES), jnp.bfloat16),
            shape_of((len(links), blocks, LANES), f32),
        ),
        in_specs=smem() + vmem(3) + smem() + vmem(1 + len(links)),
        out_specs=tuple(vmem(4)),
        compiler_params=params_with(8),
        name="prepare",
    )(group, held, prior, dual, step_sizes, share, *lists)

    messages = pl.pallas_call(
        functools.partial(project_kernel, masks, yrows, listed),
        out_shape=tuple([shape_of((COEFS * outer, LANES), f32)] * INNER),
        in_specs=smem() + vmem(2),
        out_specs=tuple(vmem(INNER)),
        scratch_shapes=[pltpu.VMEM((COEFS * outer * INNER, LANES), f32)],
        compiler_params=params_with(8),
        name="project",
    )(me, everything, ids)
    sources = [messages[0]] + [swap(messages[j], j) for j in range(1, INNER)]

    pack, base, steps, pick, mask = lax.optimization_barrier((pack, base, steps, pick, mask))
    outbox = pl.pallas_call(
        functools.partial(render_kernel, pixels, blocks, listed, hop_bits),
        out_shape=shape_of((peers, MSG, LANES), f32),
        in_specs=smem(2) + vmem(INNER + 3),
        out_specs=vmem()[0],
        scratch_shapes=[
            pltpu.VMEM((COEFS * peers, LANES), f32),
            pltpu.VMEM(((listed + 1) * KDIM, LANES), f32),
            pltpu.VMEM(((listed + 1) * LANES, KDIM), jnp.bfloat16),
            pltpu.VMEM(((listed + 1) * LANES, 3 * LANES), f32),
            pltpu.VMEM((LANES, pixels), f32),
            pltpu.VMEM((LANES, pixels), f32),
            pltpu.VMEM(((listed + 1) * LANES, pixels), f32),
            pltpu.VMEM(((listed + 1) * LANES, pixels), f32),
            pltpu.VMEM((yrows, SUB, LANES), f32),
            pltpu.VMEM((listed + 1, yrows, SUB, LANES), f32),
            pltpu.VMEM((listed + 1, yrows, SUB, LANES), f32),
            pltpu.VMEM((listed + 1, 3, yrows, SUB, LANES), f32),
            pltpu.VMEM((3, yrows, SUB, LANES), f32),
            pltpu.VMEM((KDIM, pixels), f32),
            pltpu.VMEM((KDIM, pixels), jnp.bfloat16),
            pltpu.VMEM((yrows, SUB, LANES), f32),
            pltpu.VMEM((MOMENTS * LANES, LANES), f32),
            pltpu.VMEM((MOMENTS * LANES, LANES), f32),
            pltpu.VMEM((listed + 4, SUB, MOMENTS * LANES), f32),
            pltpu.VMEM((listed * MSG, LANES), f32),
            pltpu.SMEM((listed,), jnp.int32),
        ],
        compiler_params=params_with(48),
        name="render",
    )(
        me, pack, mine, *sources, targets[0, 0], basis,
    )
    inbox = lax.all_to_all(outbox, "tile", split_axis=0, concat_axis=0, tiled=True)
    updated, shifted, sent = pl.pallas_call(
        owner_kernel,
        out_shape=(
            shape_of(own.shape, f32),
            shape_of(own.shape, f32),
            shape_of((len(links),) + own.shape, f32),
        ),
        in_specs=vmem(6),
        out_specs=tuple(vmem(3)),
        scratch_shapes=[pltpu.VMEM((params * blocks, LANES), f32)] * 2,
        compiler_params=params_with(16),
        name="owner",
    )(inbox.reshape(peers * MSG, LANES), held, base, dual, steps, pick)
    new_duals = jnp.zeros_like(shifted)
    for n, route in enumerate(routes):
        theirs = lax.ppermute(sent[n], "scene", route)
        change = shifted - 0.5 * (shifted + theirs)
        new_duals = jnp.where(mask[n] > 0.5, change, new_duals)
    return updated.swapaxes(0, 1)[None], new_duals.swapaxes(0, 1)[None]


def solution(mesh):
    placed = (
        P("scene", "tile", None, None),
        P("scene", "tile", None, None),
        P("scene", "tile", None, None),
        P(),
        P(),
        P("scene", "tile"),
        P("scene", "tile", None),
        P("scene", "tile", None),
        P("scene", "tile"),
        P("scene", "tile", None, None),
        P("scene", "tile", None, None),
    )
    return jax.shard_map(
        on_device,
        mesh=mesh,
        in_specs=placed,
        out_specs=(P("scene", "tile", None, None), P("scene", "tile", None, None)),
        check_vma=False,
    )
```
